32 devices in a mesh: lon: 16 (over z, x, core), lat: 2 (over y).
Axes of the slice: x: 2, y: 2, z: 4, core: 2. Of those that a mesh axis runs over, the one named last changes fastest.
Arguments:
- adjoint_final: float32 [34, 256, 256], P(None, 'lon', 'lat'), may hold values from -6 to 6
- lon_courant: float32 [2, 34, 256, 256], P(None, None, 'lon', 'lat'), may hold values from -0.9 to 0.9
- lon_branch: int32 [2, 34, 256, 256], P(None, None, 'lon', 'lat'), may hold values from 0 to 2
- lat_courant: float32 [2, 34, 256, 256], P(None, None, 'lon', 'lat'), may hold values from -0.9 to 0.9
- lat_branch: int32 [2, 34, 256, 256], P(None, None, 'lon', 'lat'), may hold values from 0 to 2
- mixing: float32 [2, 33, 256, 256], P(None, None, 'lon', 'lat'), may hold values from 0.05 to 5
- region_map: int32 [256, 256], P('lon', 'lat'), may hold values from 0 to 8191
- region_order: int32 [8192], replicated, may hold values from 0 to 8191, each once
- prior_cov: float32 [32, 256, 256], P('lon'), may hold values from -0.4 to 0.4
Outputs:
- adjoint_start: float32 [34, 256, 256], P(None, 'lon', 'lat')
- flux_gradient: float32 [2, 8192], P(None, ('lon', 'lat'))
The draws below stay inside these ranges and needn't reach their ends.
Inputs may be any that keep to these rules, and one draw needn't show every extreme that they name: `region_order`: each position appears once.
All inputs are finite; a program needn't handle non-finite values.
Results may differ from the reference program's by a relative error of at most 0.0003.
Values sent between devices are 32-bit elements; how exact they have to be, the bound alone decides.
A program may use at most 128 MiB of HBM per device.

```python
import math
import jax
import jax.numpy as jnp
from jax import lax

LEV = 34
STEPS = 2
REGIONS = 8192
BLK = 256
NLON = 256
NLAT = 256
NBLK = 32


def draw_prior_cov(key, part):
    key_noise, key_scale = jax.random.split(jax.random.fold_in(key, 17))
    block_count = REGIONS // BLK
    noise = jnp.clip(jax.random.normal(key_noise, (block_count, BLK, BLK), jnp.float32), -6.0, 6.0)
    scales = jnp.exp(jax.random.uniform(key_scale, (block_count, BLK), jnp.float32, math.log(0.1), math.log(0.6)))
    mirrored = (noise + jnp.swapaxes(noise, 1, 2)) * (1.0 / math.sqrt(2.0))
    rows = lax.broadcasted_iota(jnp.int32, (BLK, BLK), 0)
    cols = lax.broadcasted_iota(jnp.int32, (BLK, BLK), 1)
    shaped = jnp.where(rows == cols, 1.0, mirrored * (0.3 / math.sqrt(BLK)))
    return shaped * scales[:, :, None] * scales[:, None, :]


def set_ends(values, own_key, least, top_value):
    index_at = [jax.random.randint(jax.random.fold_in(own_key, axis), (), 0, length) for axis, length in enumerate(values.shape)]
    main_axis = values.shape.index(max(values.shape))
    next_to = index_at[:main_axis] + [(index_at[main_axis] + 1) % values.shape[main_axis]] + index_at[main_axis + 1:]
    return values.at[tuple(index_at)].set(least).at[tuple(next_to)].set(top_value)


def level_of(key, extent, cuts, low, largest):
    factor_of, own = 1.0, jax.random.fold_in(key, 6)
    for axis_at, parts in cuts:
        heights = jnp.exp(jax.random.uniform(jax.random.fold_in(own, axis_at), (parts,), jnp.float32, low / len(cuts), largest / len(cuts)))
        factor_of = factor_of * jnp.repeat(heights, extent[axis_at] // parts).reshape([-1 if axis == axis_at else 1 for axis in range(len(extent))])
    return factor_of


def centred(rng, shape, deviation, bound, pieces=(), dtype=jnp.bfloat16):
    values = jax.random.normal(rng, shape, jnp.float32) * deviation
    if len(pieces) > 0:
        values = level_of(rng, shape, pieces, -0.22, 0.18) * values
    return jnp.clip(values, min=-bound, max=bound).astype(dtype)


def setup_inputs(seed: int = 0) -> dict:
    splits = jax.random.split(jax.random.key(seed), 10)
    adjoint_final = centred(splits[0], (LEV, NLON, NLAT), 1.0, 6.0, ((1, 16), (2, 2)), jnp.float32)
    lon_courant = jnp.clip(jax.random.uniform(splits[1], (STEPS, LEV, NLON, NLAT), jnp.float32, -0.9, 0.9) * level_of(splits[1], (STEPS, LEV, NLON, NLAT), ((2, 16), (3, 2)), -0.4, 0.0), -0.9, 0.9)
    lon_branch = set_ends(jax.random.randint(splits[2], (STEPS, LEV, NLON, NLAT), 0, 3), jax.random.fold_in(splits[2], 1), 0, 2).astype(jnp.int32)
    lat_courant = jnp.clip(jax.random.uniform(splits[3], (STEPS, LEV, NLON, NLAT), jnp.float32, -0.9, 0.9) * level_of(splits[3], (STEPS, LEV, NLON, NLAT), ((2, 16), (3, 2)), -0.4, 0.0), -0.9, 0.9)
    lat_branch = set_ends(jax.random.randint(splits[4], (STEPS, LEV, NLON, NLAT), 0, 3), jax.random.fold_in(splits[4], 1), 0, 2).astype(jnp.int32)
    mixing = jnp.clip(jnp.exp(math.log(5.0) - 4.6051702 * jax.random.uniform(splits[5], (STEPS, LEV - 1, NLON, NLAT), jnp.float32) ** level_of(splits[5], (STEPS, LEV - 1, NLON, NLAT), ((2, 16), (3, 2)), -0.2, 0.2)), 0.05, 5.0)
    region_map = set_ends(jax.random.randint(splits[6], (NLON, NLAT), 0, REGIONS), jax.random.fold_in(splits[6], 1), 0, REGIONS - 1).astype(jnp.int32)
    region_order = jax.random.permutation(splits[7], REGIONS).astype(jnp.int32)
    prior_cov = draw_prior_cov(jax.random.fold_in(splits[9], 71), 0)
    return dict(adjoint_final=adjoint_final, lon_courant=lon_courant, lon_branch=lon_branch, lat_courant=lat_courant, lat_branch=lat_branch, mixing=mixing, region_map=region_map, region_order=region_order, prior_cov=prior_cov)


def face_weights(courant, branch):
    half_step = 0.5 * (1.0 - jnp.abs(courant))
    lean_part = courant * half_step
    branch_one = jnp.where(branch == 1, 1.0, 0.0)
    branch_two = jnp.where(branch == 2, 1.0, 0.0)
    upwind_left = jnp.where(courant > 0.0, 1.0, 0.0)
    upwind_right = 1.0 - upwind_left
    donor = courant - branch_one * lean_part + branch_two * lean_part
    weight_far = -(upwind_left * branch_two * lean_part)
    weight_left = upwind_left * donor + upwind_right * branch_one * lean_part
    weight_right = upwind_left * branch_one * lean_part + upwind_right * donor
    weight_next = -(upwind_right * branch_two * lean_part)
    return [weight_far, weight_left, weight_right, weight_next]


def window(array, start, count, axis):
    return lax.slice_in_dim(array, start, start + count, axis=axis)


def transpose_flux(adjoint, padded, weights, axis):
    count = adjoint.shape[axis]
    jumps = window(padded, 1, count + 3, axis) - window(padded, 0, count + 3, axis)
    terms = [window(weight, 1, count + 3, axis) * jumps for weight in weights]
    result = adjoint + window(terms[0], 3, count, axis)
    result = result + window(terms[1], 2, count, axis)
    result = result + window(terms[2], 1, count, axis)
    return result + window(terms[3], 0, count, axis)


def vertical_solve(rhs, mixing):
    level_count = rhs.shape[0]
    ratios = []
    carried = []
    for level in range(level_count):
        if level == 0:
            denom = 1.0 + mixing[0]
            value = rhs[0] / denom
        else:
            lower = mixing[level - 1]
            diagonal = 1.0 + lower + mixing[level] if level < level_count - 1 else 1.0 + lower
            denom = diagonal + lower * ratios[-1]
            value = (rhs[level] + lower * carried[-1]) / denom
        ratios.append(-mixing[level] / denom if level < level_count - 1 else None)
        carried.append(value)
    result = [carried[-1]]
    for level in range(level_count - 2, -1, -1):
        result.insert(0, carried[level] - ratios[level] * result[0])
    return jnp.stack(result)


def horizontal(fields):
    adjoint, lon_c, lon_b, lat_c, lat_b = fields
    lat_weights = [jnp.pad(weight, ((0, 0), (2, 2))) for weight in face_weights(lat_c, lat_b)]
    adjoint = transpose_flux(adjoint, jnp.pad(adjoint, ((0, 0), (2, 2))), lat_weights, 1)
    lon_weights = [jnp.pad(weight, ((2, 2), (0, 0)), mode="wrap") for weight in face_weights(lon_c, lon_b)]
    return transpose_flux(adjoint, jnp.pad(adjoint, ((2, 2), (0, 0)), mode="wrap"), lon_weights, 0)


def reference(adjoint_final, lon_courant, lon_branch, lat_courant, lat_branch, mixing, region_map, region_order, prior_cov):
    lat_index = jnp.arange(NLAT)
    coslat = jnp.cos((lat_index.astype(jnp.float32) + 0.5) * (math.pi / NLAT) - 0.5 * math.pi)
    lat_inner = jnp.where(lat_index == 0, 0.0, lat_courant)
    adjoint = adjoint_final
    surface = [None] * STEPS
    for step in range(STEPS - 1, -1, -1):
        adjoint = vertical_solve(adjoint, mixing[step])
        adjoint = lax.map(horizontal, (adjoint, lon_courant[step], lon_branch[step], lat_inner[step], lat_branch[step]))
        surface[step] = adjoint[0] * coslat[None, :]
    field = jnp.stack(surface).reshape(STEPS, NLON * NLAT)
    slots = jnp.take(region_order, region_map.reshape(NLON * NLAT), axis=0)
    totals = jax.ops.segment_sum(field.T, slots, num_segments=REGIONS).T
    blocks = totals.reshape(STEPS, NBLK, BLK)
    mapped = jnp.einsum("sbj,bji->sbi", blocks, prior_cov, precision=lax.Precision.HIGHEST)
    return adjoint, mapped.reshape(STEPS, REGIONS)
```

```python
import functools
import math

import jax
import jax.numpy as jnp
import numpy as np
from jax import lax
from jax.experimental import pallas as pl
from jax.experimental.pallas import tpu as pltpu
from jax.sharding import PartitionSpec as P

MESH = pl.DeviceIdType.MESH
OWN = 8


def face_weights(courant, branch):
    lean_part = courant * (0.5 * (1.0 - jnp.abs(courant)))
    one_part = jnp.where(branch == 1, lean_part, 0.0)
    two_part = jnp.where(branch == 2, lean_part, 0.0)
    donor = courant - one_part + two_part
    left = courant > 0.0
    return (
        jnp.where(left, -two_part, 0.0),
        jnp.where(left, donor, one_part),
        jnp.where(left, one_part, donor),
        jnp.where(left, 0.0, -two_part),
    )


def kernel(
    nlon,
    nlat,
    width,
    adj_h,
    lonc_h,
    lonb_h,
    latc_h,
    latb_h,
    mix_h,
    cov_h,
    rmap_h,
    order_h,
    cos_h,
    out_ref,
    flux_ref,
    rmap_ref,
    order_ref,
    cos_ref,
    x_ref,
    mixv,
    latc,
    latb,
    lonc,
    lonb,
    covv,
    covh,
    covl,
    inv_ref,
    kin_ref,
    nr_ref,
    y_ref,
    ext,
    lw,
    pack_w,
    land_w,
    pack_a,
    land_a,
    raw_rows,
    rows_a,
    far_a,
    rows_w,
    hi_ref,
    lo_ref,
    cht,
    amat,
    pscr,
    send_ref,
    land,
    local_sem,
    send_sem,
    recv_sem,
    all_sem,
):
    steps, levels, rows, lanes = latc.shape
    count = nlon * nlat
    my_lon, my_lat = lax.axis_index("lon"), lax.axis_index("lat")
    me = my_lon * nlat + my_lat
    blk = covv.shape[0]

    def place(device):
        return (device // nlat, lax.rem(device, nlat))

    barrier = pltpu.get_barrier_semaphore()

    def fetch(src, dst, slot):
        copy = pltpu.make_async_copy(src, dst, local_sem.at[slot])
        copy.start()
        return copy

    get_mix, get_lat, get_lon = {}, {}, {}
    get_mix[1] = fetch(mix_h.at[1], mixv.at[1], 0)
    get_adj = fetch(adj_h, x_ref, 1)
    for s in (1, 0):
        at = 2 + 5 * (1 - s)
        get_lat[s] = (
            fetch(latc_h.at[s], latc.at[s], at),
            fetch(latb_h.at[s], latb.at[s], at + 1),
        )
        get_lon[s] = (
            fetch(lonc_h.at[s], lonc.at[s], at + 2),
            fetch(lonb_h.at[s], lonb.at[s], at + 3),
        )
        if s == 1:
            get_mix[0] = fetch(mix_h.at[0], mixv.at[0], at + 4)
    get_small = (
        fetch(rmap_h, rmap_ref, 11),
        fetch(order_h, order_ref, 12),
        fetch(cos_h.at[my_lat], cos_ref, 13),
    )
    get_cov = fetch(cov_h.at[(my_lat * width) // blk], covv, 14)

    far_first = jnp.where(my_lon >= nlon // 2, 1, 0)

    def greet(k, carry):
        device = far_first * k + (1 - far_first) * (count - 1 - k)

        @pl.when(device != me)
        def _():
            pl.semaphore_signal(barrier, inc=1, device_id=place(device), device_id_type=MESH)

        return carry

    lax.fori_loop(0, count, greet, 0)

    lane = lax.broadcasted_iota(jnp.int32, (rows, lanes), 1)
    pair = lane // 2
    even = lax.rem(lane, 2) == 0
    zero = jnp.zeros((rows, lanes), jnp.float32)

    def roll(value, shift):
        return pltpu.roll(value, shift, 1)

    def remote(src, dst, slot, device):
        copy = pltpu.make_async_remote_copy(
            src_ref=src,
            dst_ref=dst,
            send_sem=send_sem.at[slot],
            recv_sem=recv_sem.at[slot],
            device_id=device,
            device_id_type=MESH,
        )
        copy.start()
        return copy

    north = (my_lon, lax.rem(my_lat + 1, nlat))
    south = (my_lon, lax.rem(my_lat + nlat - 1, nlat))
    east = (lax.rem(my_lon + 1, nlon), my_lat)
    west = (lax.rem(my_lon + nlon - 1, nlon), my_lat)

    def coefficients(s):
        k = mixv[s, 0]
        inv = 1.0 / (1.0 + k)
        inv_ref[s, 0] = inv
        kin_ref[s, 0] = zero
        nr_ref[s, 0] = k * inv

        def body(level, ahead):
            lower, k = mixv[s, level - 1], mixv[s, level]
            inv = 1.0 / ((1.0 + k) + lower * (1.0 - ahead))
            inv_ref[s, level] = inv
            kin_ref[s, level] = lower * inv
            ahead = k * inv
            nr_ref[s, level] = ahead
            return ahead

        ahead = lax.fori_loop(1, levels - 1, body, k * inv, unroll=True)
        lower = mixv[s, levels - 2]
        inv = 1.0 / (1.0 + lower * (1.0 - ahead))
        inv_ref[s, levels - 1] = inv
        kin_ref[s, levels - 1] = lower * inv
        nr_ref[s, levels - 1] = zero

    def tail_head(value, level, tail, head):
        turned = roll(value, 2 * level + 2)
        return jnp.where(pair == level, turned, tail), jnp.where(pair == level + 1, turned, head)

    def solve(s):
        def up(level, carried):
            carried = x_ref[level] * inv_ref[s, level] + kin_ref[s, level] * carried
            y_ref[level] = carried
            return carried

        lax.fori_loop(0, levels, up, zero, unroll=True)

        def down(i, carry):
            value, tail, head = carry
            level = levels - 1 - i
            value = y_ref[level] + nr_ref[s, level] * value
            y_ref[level] = value
            raw_rows[0, pl.ds(2 * level, 2), :] = value[rows - 2 :]
            raw_rows[1, pl.ds(2 * level, 2), :] = value[:2]
            return (value,) + tail_head(value, level, tail, head)

        _, tail, head = lax.fori_loop(0, levels, down, (zero, zero, zero), unroll=True)
        head = roll(head, lanes - 2)
        for member, value in enumerate((tail, head)):
            pack_a[s, member, OWN : OWN + rows] = value
            at = 2 * levels + 2 * member
            rows_a[0, s, at : at + 2] = value[rows - 2 :]
            rows_a[1, s, at : at + 2] = value[:2]

    def pack_weights(s):
        def body(level, carry):
            ct, ch, bt, bh = carry
            ct, ch = tail_head(latc[s, level], level, ct, ch)
            both = (latc[s, level], latb[s, level].astype(jnp.float32))
            bt, bh = tail_head(both[1], level, bt, bh)
            for member in range(2):
                rows_w[0, s, member, pl.ds(2 * level, 2), :] = both[member][rows - 2 :]
                rows_w[1, s, member, pl.ds(2 * level, 2), :] = both[member][:2]
            return ct, ch, bt, bh

        ct, ch, bt, bh = lax.fori_loop(0, levels, body, (zero,) * 4, unroll=True)
        found = ((ct, bt), (roll(ch, lanes - 2), roll(bh, lanes - 2)))
        for end in range(2):
            for member in range(2):
                pack_w[end, s, member, OWN : OWN + rows] = found[end][member]
        for member in range(2):
            at = 2 * levels + 4 + 2 * member
            rows_a[0, s, at : at + 2] = found[1][member][rows - 2 :]
            rows_a[1, s, at : at + 2] = found[1][member][:2]

    def lat_rows(s):
        for side in range(2):
            rows_a[side, s, : 2 * levels] = lat_pass(
                raw_rows[side], rows_w[side, s, 0], rows_w[side, s, 1]
            )

    def lat_pass(a, courant, branch):
        at = lax.broadcasted_iota(jnp.int32, a.shape, 1)
        m2, m1, m0, p1 = face_weights(courant, branch)
        jump = jnp.where(at >= 1, a - roll(a, 1), 0.0)
        out = a + m0 * jump + roll(m1 * jump, lanes - 1)
        out = out + roll(jnp.where(at >= 2, m2 * jump, 0.0), lanes - 2)
        return out + roll(jnp.where(at <= lanes - 2, p1 * jump, 0.0), 1)

    def lat_inner(s):
        def body(level, carry):
            out = lat_pass(y_ref[level], latc[s, level], latb[s, level])
            ext[s, level, OWN : OWN + rows] = out
            return carry

        lax.fori_loop(0, levels, body, 0, unroll=True)

    def lat_edges(s):
        at = 2 * levels
        lane = lax.broadcasted_iota(jnp.int32, (rows + 2 * OWN, lanes), 1)
        even = lax.rem(lane, 2) == 0
        for side, where in enumerate((slice(OWN - 2, OWN), slice(OWN + rows, OWN + rows + 2))):
            for member in range(2):
                pack_a[s, member, where] = far_a[side, s, at + 2 * member : at + 2 * member + 2]
                far = at + 4 + 2 * member
                pack_w[1, s, member, where] = far_a[side, s, far : far + 2]
        tail, head = pack_a[s, 0], pack_a[s, 1]
        before, after = land_a[s, 0], land_a[s, 1]
        m2_after, m1_after, _, _ = face_weights(land_w[1, s, 0], land_w[1, s, 1])
        _, _, m0_head, p1_head = face_weights(pack_w[1, s, 0], pack_w[1, s, 1])
        _, _, _, p1_before = face_weights(land_w[0, s, 0], land_w[0, s, 1])
        jump = after - jnp.where(even, roll(tail, lanes - 1), roll(after, 1))
        top = m2_after * jump + roll(jnp.where(even, m1_after * jump, 0.0), 1)
        top = jnp.where(my_lat < nlat - 1, top, 0.0)
        jump = jnp.where(even, head - roll(before, lanes - 1), before - roll(before, 1))
        flux = jnp.where(even, p1_head, p1_before) * jump
        low = jnp.where(even, m0_head * jump + roll(flux, lanes - 1), roll(flux, 1))
        low = roll(jnp.where(my_lat > 0, low, 0.0), 2)
        first = lax.rem(lane, 4) < 2
        both = (jnp.where(first, top, low), jnp.where(first, low, top))
        edge = jnp.logical_or(lane < 2, lane >= lanes - 2)

        def body(m, carry):
            for odd in range(2):
                level = 2 * m + odd
                turned = jnp.where(edge, roll(both[odd], lanes - 2 - 2 * level), 0.0)
                ext[s, level, OWN : OWN + rows] += turned[OWN : OWN + rows]
                two = pl.ds(2 * level, 2)
                end = OWN + rows
                ext[s, level, OWN - 2 : OWN] = far_a[0, s, two, :] + turned[OWN - 2 : OWN]
                ext[s, level, end : end + 2] = far_a[1, s, two, :] + turned[end : end + 2]
            return carry

        lax.fori_loop(0, levels // 2, body, 0, unroll=True)

    def lon_own_weights(s):
        def body(level, carry):
            found = face_weights(
                lonc[s, level], lonb[s, level]
            )
            for member in range(4):
                lw[s, member, level, OWN : OWN + rows] = found[member]
            return carry

        lax.fori_loop(0, levels, body, 0, unroll=True)

    def lon_level(s, level):
        a = [ext[s, level, OWN + k : OWN + k + rows] for k in range(-2, 3)]
        w = [
            lw[s, member, level, OWN + 2 - member : OWN + 2 - member + rows]
            for member in range(4)
        ]
        out = a[2] + w[0] * (a[4] - a[3]) + w[1] * (a[3] - a[2])
        return out + w[2] * (a[2] - a[1]) + w[3] * (a[1] - a[0])

    def send_lon(s, base):
        end = OWN + rows
        return tuple(
            remote(
                lw.at[s, member, :, pl.ds(src, size), :],
                lw.at[s, member, :, pl.ds(dst, size), :],
                base + k,
                device,
            )
            for k, (member, src, dst, size, device) in enumerate(
                (
                    (0, OWN, end, 2, west),
                    (1, OWN, end, 1, west),
                    (3, end - 1, OWN - 1, 1, east),
                )
            )
        )

    def find_slots():
        order = order_ref[...]
        table = jnp.concatenate([order // 128, lax.rem(order, 128)], axis=0)
        table = table.astype(jnp.float32).astype(jnp.bfloat16)
        high = order.shape[0]
        down = lax.broadcasted_iota(jnp.int32, (lanes, lanes), 0)
        row_of = lax.broadcasted_iota(jnp.int32, (high, lanes), 0)
        for i in range(rows):
            region = rmap_ref[i : i + 1, :]
            hit = jnp.where(down == lax.rem(region, 128), 1.0, 0.0).astype(jnp.bfloat16)
            found = jnp.dot(table, hit, preferred_element_type=jnp.float32)
            here = row_of == region // 128
            hi = jnp.sum(jnp.where(here, found[:high], 0.0), axis=0, keepdims=True)
            lo = jnp.sum(jnp.where(here, found[high:], 0.0), axis=0, keepdims=True)
            hi_ref[i : i + 1, :] = hi
            cht[:, i * lanes : (i + 1) * lanes] = jnp.where(
                down.astype(jnp.float32) == lo, 1.0, 0.0
            ).astype(jnp.bfloat16)

    def regions(s, field):
        high = order_ref.shape[0]
        row_of = lax.broadcasted_iota(jnp.int32, (high, lanes), 0).astype(jnp.float32)
        lo_ref[...] = field
        for i in range(rows):
            here = row_of == hi_ref[i : i + 1, :]
            spread = jnp.where(here, lo_ref[i : i + 1, :], 0.0)
            coarse = spread.astype(jnp.bfloat16)
            fine = (spread - coarse.astype(jnp.float32)).astype(jnp.bfloat16)
            amat[:high, i * lanes : (i + 1) * lanes] = coarse
            amat[high:, i * lanes : (i + 1) * lanes] = fine
        sums = lax.dot_general(
            amat[...], cht[...], (((1,), (1,)), ((), ())), preferred_element_type=jnp.float32
        )
        pscr[...] = sums[:high] + sums[high:]
        for group in range(high // 2):
            send_ref[s, group] = pscr[2 * group : 2 * group + 2, :]

    get_mix[1].wait()
    coefficients(1)
    get_adj.wait()
    solve(1)
    for copy in get_lat[1]:
        copy.wait()
    pack_weights(1)
    lat_rows(1)
    for copy in get_lon[1]:
        copy.wait()
    lon_own_weights(1)
    pl.semaphore_wait(barrier, count - 1)

    turn = {1: lax.rem(my_lon + 1, nlon), -1: lax.rem(my_lon + nlon - 1, nlon)}
    own_rows, first, last_two = pl.ds(OWN, rows), pl.ds(OWN, 2), pl.ds(OWN + rows - 2, 2)
    low, high = pl.ds(OWN - 2, 2), pl.ds(OWN + rows, 2)

    def send_columns(source, target, base):
        copies = []
        for end in range(2):
            beside = (north, south)[end][1]
            for k, (lon, src, dst) in enumerate(
                (
                    (my_lon, own_rows, own_rows),
                    (turn[1], last_two, low),
                    (turn[-1], first, high),
                )
            ):
                copies.append(
                    remote(source(end, src), target(end, dst), base + 3 * end + k, (lon, beside))
                )
        return tuple(copies)

    def exchange(s, base):
        return (
            remote(rows_a.at[0, s], far_a.at[0, s], base, east),
            remote(rows_a.at[1, s], far_a.at[1, s], base + 1, west),
        ) + send_columns(
            lambda end, at: pack_a.at[s, end, at, :],
            lambda end, at: land_a.at[s, end, at, :],
            base + 2,
        )

    def send_lat_weights(s, base):
        return send_columns(
            lambda end, at: pack_w.at[end, s, :, at, :],
            lambda end, at: land_w.at[end, s, :, at, :],
            base,
        )

    def group_of(device):
        return (device * width) // blk

    def scatter(s):
        def body(k, carry):
            device = lax.rem(me + k, count)
            pltpu.make_async_remote_copy(
                src_ref=send_ref.at[s, group_of(device)],
                dst_ref=land.at[s, me],
                send_sem=all_sem.at[2 * s],
                recv_sem=all_sem.at[2 * s + 1],
                device_id=place(device),
                device_id_type=MESH,
            ).start()
            return carry

        lax.fori_loop(1, count, body, 0)
        land[s, me] = send_ref[s, group_of(me)]

    sent_a = {1: exchange(1, 0)}
    sent_w = {1: send_lat_weights(1, 16)}
    sent_lon = {1: send_lon(1, 28)}
    lat_inner(1)
    get_mix[0].wait()
    coefficients(0)
    for copy in get_lat[0]:
        copy.wait()
    pack_weights(0)
    sent_w[0] = send_lat_weights(0, 22)
    for copy in get_lon[0]:
        copy.wait()
    lon_own_weights(0)
    sent_lon[0] = send_lon(0, 31)
    for copy in get_small:
        copy.wait()
    cosine = cos_ref[...]
    find_slots()
    for copy in sent_a[1] + sent_w[1]:
        copy.wait_recv()
    lat_edges(1)
    for copy in sent_lon[1]:
        copy.wait_recv()

    def middle(level, carry):
        x_ref[level] = lon_level(1, level)
        return carry

    lax.fori_loop(0, levels, middle, 0, unroll=True)
    solve(0)
    lat_rows(0)
    sent_a[0] = exchange(0, 8)
    regions(1, x_ref[0] * cosine)
    scatter(1)
    lat_inner(0)
    get_cov.wait()
    covh[...] = covv[...].astype(jnp.bfloat16)
    covl[...] = (covv[...] - covh[...].astype(jnp.float32)).astype(jnp.bfloat16)
    for copy in sent_a[0] + sent_w[0]:
        copy.wait_recv()
    lat_edges(0)
    for copy in sent_lon[0]:
        copy.wait_recv()
    start = lon_level(0, 0)
    out_ref[0] = start
    regions(0, start * cosine)
    scatter(0)

    def last(level, carry):
        out_ref[level] = lon_level(0, level)
        return carry

    lax.fori_loop(1, levels, last, 0, unroll=True)
    for s in range(steps):
        for copy in sent_a[s] + sent_w[s] + sent_lon[s]:
            copy.wait_send()
    for s in range(steps):
        every = land.at[s, pl.ds(0, count - 1)]
        pltpu.make_async_copy(every, every, all_sem.at[2 * s]).wait()
        pltpu.make_async_copy(every, every, all_sem.at[2 * s + 1]).wait()
    totals = jnp.concatenate([jnp.sum(land[s], axis=0) for s in range(steps)], axis=0)
    coarse = totals.astype(jnp.bfloat16).astype(jnp.float32)
    both = jnp.concatenate([coarse, totals - coarse, jnp.zeros((8, lanes), jnp.float32)], axis=0)
    both = both.astype(jnp.bfloat16)
    half = blk // 2

    def product(at):
        found = jnp.dot(both, covh[at], preferred_element_type=jnp.float32)
        found = found + jnp.dot(both, covl[at], preferred_element_type=jnp.float32)
        return found[:4] + found[4:8]

    one, two = product(slice(0, half)), product(slice(half, blk))
    for s in range(steps):
        flux_ref[s : s + 1, :] = one[2 * s : 2 * s + 1] + two[2 * s + 1 : 2 * s + 2]


def per_device(
    nlon,
    nlat,
    adjoint_final,
    lon_courant,
    lon_branch,
    lat_courant,
    lat_branch,
    mixing,
    region_map,
    region_order,
    prior_cov,
):
    steps, levels, rows, lanes = lon_courant.shape
    regions = region_order.shape[0]
    blk = prior_cov.shape[1]
    width = regions // (nlon * nlat)
    lat_total = lanes * nlat
    lat_index = np.arange(lat_total, dtype=np.float32)
    angle = (lat_index + np.float32(0.5)) * np.float32(math.pi / lat_total)
    cosines = np.cos((angle - np.float32(0.5 * math.pi)).astype(np.float32))
    cosines = jnp.asarray(cosines.astype(np.float32).reshape(nlat, 1, lanes))
    f32, i32, b16 = jnp.float32, jnp.int32, jnp.bfloat16
    field = (levels, rows, lanes)
    tall = (levels, rows + 2 * OWN, lanes)
    vm = pltpu.VMEM
    scratch = [
        vm((rows, lanes), i32),
        vm((regions // 128, 128), i32),
        vm((1, lanes), f32),
        vm(field, f32),
        vm((steps, levels - 1, rows, lanes), f32),
        vm((steps,) + field, f32),
        vm((steps,) + field, i32),
        vm((steps,) + field, f32),
        vm((steps,) + field, i32),
        vm((blk, blk), f32),
        vm((blk, blk), b16),
        vm((blk, blk), b16),
        vm((steps,) + field, f32),
        vm((steps,) + field, f32),
        vm((steps,) + field, f32),
        vm(field, f32),
        vm((steps,) + tall, f32),
        vm((steps, 4) + tall, f32),
        vm((2, steps, 2, rows + 2 * OWN, lanes), f32),
        vm((2, steps, 2, rows + 2 * OWN, lanes), f32),
        vm((steps, 2, rows + 2 * OWN, lanes), f32),
        vm((steps, 2, rows + 2 * OWN, lanes), f32),
        vm((2, 2 * levels, lanes), f32),
        vm((2, steps, 2 * levels + 8, lanes), f32),
        vm((2, steps, 2 * levels + 8, lanes), f32),
        vm((2, steps, 2, 2 * levels, lanes), f32),
        vm((rows, lanes), f32),
        vm((rows, lanes), f32),
        vm((128, rows * lanes), b16),
        vm((2 * (regions // 128), rows * lanes), b16),
        vm((regions // 128, 128), f32),
        vm((steps, regions // blk, 2, 128), f32),
        vm((steps, nlon * nlat, 2, 128), f32),
        pltpu.SemaphoreType.DMA((15,)),
        pltpu.SemaphoreType.DMA((34,)),
        pltpu.SemaphoreType.DMA((34,)),
        pltpu.SemaphoreType.DMA((4,)),
    ]
    adjoint, flux = pl.pallas_call(
        functools.partial(kernel, nlon, nlat, width),
        out_shape=(
            pltpu.VMEM(field, f32),
            pltpu.VMEM((steps, blk), f32),
        ),
        in_specs=[pl.BlockSpec(memory_space=pltpu.HBM)] * 10,
        out_specs=(
            pl.BlockSpec(memory_space=pltpu.VMEM),
            pl.BlockSpec(memory_space=pltpu.VMEM),
        ),
        scratch_shapes=scratch,
        compiler_params=pltpu.CompilerParams(
            collective_id=0, has_side_effects=True, vmem_limit_bytes=61 * 1024 * 1024
        ),
    )(
        adjoint_final,
        lon_courant,
        lon_branch,
        lat_courant,
        lat_branch,
        mixing,
        prior_cov,
        region_map,
        region_order.reshape(regions // 128, 128),
        cosines,
    )
    if width < blk:
        start = lax.rem(lax.axis_index("lat") * width, blk)
        flux = lax.dynamic_slice_in_dim(flux, start, width, 1)
    return adjoint, flux


def solution(mesh):
    four = P(None, None, "lon", "lat")
    placed = (
        P(None, "lon", "lat"),
        four,
        four,
        four,
        four,
        four,
        P("lon", "lat"),
        P(),
        P("lon", None, None),
    )
    return jax.shard_map(
        functools.partial(per_device, mesh.shape["lon"], mesh.shape["lat"]),
        mesh=mesh,
        in_specs=placed,
        out_specs=(P(None, "lon", "lat"), P(None, ("lon", "lat"))),
        check_vma=False,
    )
```

```python
import functools
import math

import jax
import jax.numpy as jnp
import numpy as np
from jax import lax
from jax.experimental import pallas as pl
from jax.experimental.pallas import tpu as pltpu
from jax.sharding import PartitionSpec as P

MESH = pl.DeviceIdType.MESH
OWN = 8


def face_weights(courant, branch):
    lean_part = courant * (0.5 * (1.0 - jnp.abs(courant)))
    one_part = jnp.where(branch == 1, lean_part, 0.0)
    two_part = jnp.where(branch == 2, lean_part, 0.0)
    donor = courant - one_part + two_part
    left = courant > 0.0
    return (
        jnp.where(left, -two_part, 0.0),
        jnp.where(left, donor, one_part),
        jnp.where(left, one_part, donor),
        jnp.where(left, 0.0, -two_part),
    )


def kernel(
    nlon,
    nlat,
    width,
    adj_h,
    lonc_h,
    lonb_h,
    latc_h,
    latb_h,
    mix_h,
    cov_h,
    rmap_h,
    order_h,
    cos_h,
    out_h,
    flux_h,
    out_ref,
    flux_ref,
    rmap_ref,
    order_ref,
    cos_ref,
    x_ref,
    mixv,
    latc,
    latb,
    lonc,
    lonb,
    covv,
    covh,
    covl,
    inv_ref,
    kin_ref,
    nr_ref,
    y_ref,
    ext,
    lw,
    pack_w,
    land_w,
    pack_a,
    land_a,
    raw_rows,
    rows_a,
    far_a,
    rows_w,
    ids,
    beside,
    lat_c,
    lon_c,
    bext,
    hot,
    cht,
    amat,
    send_ref,
    land,
    local_sem,
    send_sem,
    recv_sem,
    all_sem,
):
    steps, levels, rows, lanes = latc.shape
    count = nlon * nlat
    my_lon, my_lat = lax.axis_index("lon"), lax.axis_index("lat")
    me = my_lon * nlat + my_lat
    blk = covv.shape[0]

    def place(device):
        return (device // nlat, lax.rem(device, nlat))

    barrier = pltpu.get_barrier_semaphore()

    def fetch(src, dst, slot):
        copy = pltpu.make_async_copy(src, dst, local_sem.at[slot])
        copy.start()
        return copy

    get_mix, get_lat, get_lon = {}, {}, {}
    get_mix[1] = fetch(mix_h.at[1], mixv.at[1], 0)
    get_adj = fetch(adj_h, x_ref, 1)
    for s in (1, 0):
        at = 2 + 5 * (1 - s)
        get_lat[s] = (
            fetch(latc_h.at[s], latc.at[s], at),
            fetch(latb_h.at[s], latb.at[s], at + 1),
        )
        get_lon[s] = (
            fetch(lonc_h.at[s], lonc.at[s], at + 2),
            fetch(lonb_h.at[s], lonb.at[s], at + 3),
        )
        if s == 1:
            get_mix[0] = fetch(mix_h.at[0], mixv.at[0], at + 4)
    get_small = (
        fetch(rmap_h, rmap_ref, 11),
        fetch(order_h, order_ref, 12),
        fetch(cos_h, cos_ref, 13),
    )
    get_cov = fetch(cov_h.at[(my_lat * width) // blk], covv, 14)

    far_first = jnp.where(my_lon >= nlon // 2, 1, 0)

    def greet(k, carry):
        device = far_first * k + (1 - far_first) * (count - 1 - k)

        @pl.when(device != me)
        def _():
            pl.semaphore_signal(barrier, inc=1, device_id=place(device), device_id_type=MESH)

        return carry

    lax.fori_loop(0, count, greet, 0)

    lane = lax.broadcasted_iota(jnp.int32, (rows, lanes), 1)
    pair = lane // 2
    even = lax.rem(lane, 2) == 0
    zero = jnp.zeros((rows, lanes), jnp.float32)

    def roll(value, shift):
        return pltpu.roll(value, shift, 1)

    def remote(src, dst, slot, device, start=True):
        copy = pltpu.make_async_remote_copy(
            src_ref=src,
            dst_ref=dst,
            send_sem=send_sem.at[slot],
            recv_sem=recv_sem.at[slot],
            device_id=device,
            device_id_type=MESH,
        )
        if start:
            copy.start()
        return copy

    north = (my_lon, lax.rem(my_lat + 1, nlat))
    south = (my_lon, lax.rem(my_lat + nlat - 1, nlat))
    east = (lax.rem(my_lon + 1, nlon), my_lat)
    west = (lax.rem(my_lon + nlon - 1, nlon), my_lat)

    def coefficients(s):
        k = mixv[s, 0]
        inv = 1.0 / (1.0 + k)
        inv_ref[s, 0] = inv
        kin_ref[s, 0] = zero
        nr_ref[s, 0] = k * inv

        def body(level, ahead):
            lower, k = mixv[s, level - 1], mixv[s, level]
            inv = 1.0 / ((1.0 + k) + lower * (1.0 - ahead))
            inv_ref[s, level] = inv
            kin_ref[s, level] = lower * inv
            ahead = k * inv
            nr_ref[s, level] = ahead
            return ahead

        ahead = lax.fori_loop(1, levels - 1, body, k * inv, unroll=True)
        lower = mixv[s, levels - 2]
        inv = 1.0 / (1.0 + lower * (1.0 - ahead))
        inv_ref[s, levels - 1] = inv
        kin_ref[s, levels - 1] = lower * inv
        nr_ref[s, levels - 1] = zero

    def tail_head(value, level, tail, head):
        turned = roll(value, 2 * level + 2)
        return jnp.where(pair == level, turned, tail), jnp.where(pair == level + 1, turned, head)

    def solve(s):
        def up(level, carried):
            carried = x_ref[level] * inv_ref[s, level] + kin_ref[s, level] * carried
            y_ref[level] = carried
            return carried

        lax.fori_loop(0, levels, up, zero, unroll=True)

        def down(i, carry):
            value, tail, head = carry
            level = levels - 1 - i
            value = y_ref[level] + nr_ref[s, level] * value
            y_ref[level] = value
            raw_rows[0, pl.ds(2 * level, 2), :] = value[rows - 2 :]
            raw_rows[1, pl.ds(2 * level, 2), :] = value[:2]
            return (value,) + tail_head(value, level, tail, head)

        _, tail, head = lax.fori_loop(0, levels, down, (zero, zero, zero), unroll=True)
        head = roll(head, lanes - 2)
        for member, value in enumerate((tail, head)):
            pack_a[s, member, OWN : OWN + rows] = value
            at = 2 * levels + 2 * member
            rows_a[0, s, at : at + 2] = value[rows - 2 :]
            rows_a[1, s, at : at + 2] = value[:2]

    def pack_weights(s):
        def body(level, carry):
            ct, ch, bt, bh = carry
            ct, ch = tail_head(latc[s, level], level, ct, ch)
            both = (latc[s, level], latb[s, level].astype(jnp.float32))
            bt, bh = tail_head(both[1], level, bt, bh)
            for member in range(2):
                rows_w[0, s, member, pl.ds(2 * level, 2), :] = both[member][rows - 2 :]
                rows_w[1, s, member, pl.ds(2 * level, 2), :] = both[member][:2]
            return ct, ch, bt, bh

        ct, ch, bt, bh = lax.fori_loop(0, levels, body, (zero,) * 4, unroll=True)
        found = ((ct, bt), (roll(ch, lanes - 2), roll(bh, lanes - 2)))
        for end in range(2):
            for member in range(2):
                pack_w[end, s, member, OWN : OWN + rows] = found[end][member]
        for member in range(2):
            at = 2 * levels + 4 + 2 * member
            rows_a[0, s, at : at + 2] = found[1][member][rows - 2 :]
            rows_a[1, s, at : at + 2] = found[1][member][:2]

    def lat_rows(s):
        for side in range(2):
            rows_a[side, s, : 2 * levels] = lat_pass(
                raw_rows[side], rows_w[side, s, 0], rows_w[side, s, 1]
            )

    def lat_pass(a, courant, branch):
        at = lax.broadcasted_iota(jnp.int32, a.shape, 1)
        m2, m1, m0, p1 = face_weights(courant, branch)
        jump = jnp.where(at >= 1, a - roll(a, 1), 0.0)
        out = a + m0 * jump + roll(m1 * jump, lanes - 1)
        out = out + roll(jnp.where(at >= 2, m2 * jump, 0.0), lanes - 2)
        return out + roll(jnp.where(at <= lanes - 2, p1 * jump, 0.0), 1)

    def lat_inner(s):
        def body(level, carry):
            out = lat_pass(y_ref[level], latc[s, level], latb[s, level])
            ext[s, level, OWN : OWN + rows] = out
            return carry

        lax.fori_loop(0, levels, body, 0, unroll=True)

    def lat_edges(s):
        at = 2 * levels
        lane = lax.broadcasted_iota(jnp.int32, (rows + 2 * OWN, lanes), 1)
        even = lax.rem(lane, 2) == 0
        for side, where in enumerate((slice(OWN - 2, OWN), slice(OWN + rows, OWN + rows + 2))):
            for member in range(2):
                pack_a[s, member, where] = far_a[side, s, at + 2 * member : at + 2 * member + 2]
                far = at + 4 + 2 * member
                pack_w[1, s, member, where] = far_a[side, s, far : far + 2]
        tail, head = pack_a[s, 0], pack_a[s, 1]
        before, after = land_a[s, 0], land_a[s, 1]
        m2_after, m1_after, _, _ = face_weights(land_w[1, s, 0], land_w[1, s, 1])
        _, _, m0_head, p1_head = face_weights(pack_w[1, s, 0], pack_w[1, s, 1])
        _, _, _, p1_before = face_weights(land_w[0, s, 0], land_w[0, s, 1])
        jump = after - jnp.where(even, roll(tail, lanes - 1), roll(after, 1))
        top = m2_after * jump + roll(jnp.where(even, m1_after * jump, 0.0), 1)
        top = jnp.where(my_lat < nlat - 1, top, 0.0)
        jump = jnp.where(even, head - roll(before, lanes - 1), before - roll(before, 1))
        flux = jnp.where(even, p1_head, p1_before) * jump
        low = jnp.where(even, m0_head * jump + roll(flux, lanes - 1), roll(flux, 1))
        low = roll(jnp.where(my_lat > 0, low, 0.0), 2)
        first = lax.rem(lane, 4) < 2
        both = (jnp.where(first, top, low), jnp.where(first, low, top))
        edge = jnp.logical_or(lane < 2, lane >= lanes - 2)

        def body(m, carry):
            for odd in range(2):
                level = 2 * m + odd
                turned = jnp.where(edge, roll(both[odd], lanes - 2 - 2 * level), 0.0)
                ext[s, level, OWN : OWN + rows] += turned[OWN : OWN + rows]
                two = pl.ds(2 * level, 2)
                end = OWN + rows
                ext[s, level, OWN - 2 : OWN] = far_a[0, s, two, :] + turned[OWN - 2 : OWN]
                ext[s, level, end : end + 2] = far_a[1, s, two, :] + turned[end : end + 2]
            return carry

        lax.fori_loop(0, levels // 2, body, 0, unroll=True)

    def lon_own_weights(s):
        def body(level, carry):
            found = face_weights(
                lonc[s, level], lonb[s, level]
            )
            for member in range(4):
                lw[s, member, level, OWN : OWN + rows] = found[member]
            return carry

        lax.fori_loop(0, levels, body, 0, unroll=True)

    def lon_level(s, level):
        a = [ext[s, level, OWN + k : OWN + k + rows] for k in range(-2, 3)]
        w = [
            lw[s, member, level, OWN + 2 - member : OWN + 2 - member + rows]
            for member in range(4)
        ]
        out = a[2] + w[0] * (a[4] - a[3]) + w[1] * (a[3] - a[2])
        return out + w[2] * (a[2] - a[1]) + w[3] * (a[1] - a[0])

    def send_lon(s, base):
        end = OWN + rows
        return tuple(
            remote(
                lw.at[s, member, :, pl.ds(src, size), :],
                lw.at[s, member, :, pl.ds(dst, size), :],
                base + k,
                device,
            )
            for k, (member, src, dst, size, device) in enumerate(
                (
                    (0, OWN, end, 2, west),
                    (1, OWN, end, 1, west),
                    (3, end - 1, OWN - 1, 1, east),
                )
            )
        )

    def find_slots(found_rows):
        order = order_ref[...]
        table = jnp.concatenate([order // 128, lax.rem(order, 128)], axis=0)
        table = table.astype(jnp.float32).astype(jnp.bfloat16)
        high = order.shape[0]
        down = lax.broadcasted_iota(jnp.int32, (lanes, lanes), 0)
        row_of = lax.broadcasted_iota(jnp.int32, (high, lanes), 0)
        for i, region in found_rows:
            hit = jnp.where(down == lax.rem(region, 128), 1.0, 0.0).astype(jnp.bfloat16)
            found = jnp.dot(table, hit, preferred_element_type=jnp.float32)
            here = row_of == region // 128
            hi = jnp.sum(jnp.where(here, found[:high], 0.0), axis=0, keepdims=True)
            lo = jnp.sum(jnp.where(here, found[high:], 0.0), axis=0, keepdims=True)
            at = slice(i * lanes, (i + 1) * lanes)
            hot[:, at] = jnp.where(row_of.astype(jnp.float32) == hi, 1.0, 0.0).astype(jnp.bfloat16)
            cht[:, at] = jnp.where(down.astype(jnp.float32) == lo, 1.0, 0.0).astype(jnp.bfloat16)

    def regions(s, first, fields):
        high = order_ref.shape[0]
        coarse = [field.astype(jnp.bfloat16).astype(jnp.float32) for field in fields]
        fine = [field - part for field, part in zip(fields, coarse)]
        at = first
        for field in range(len(fields)):
            for i in range(fields[field].shape[0]):
                here = slice(at * lanes, (at + 1) * lanes)
                for part, values in enumerate((coarse, fine)):
                    value = jnp.broadcast_to(values[field][i : i + 1], (high, lanes))
                    amat[part * high : (part + 1) * high, here] = hot[:, here] * value.astype(
                        jnp.bfloat16
                    )
                at += 1
        every = slice(first * lanes, at * lanes)
        sums = lax.dot_general(
            amat[:, every],
            cht[:, every],
            (((1,), (1,)), ((), ())),
            preferred_element_type=jnp.float32,
        )
        sums = sums[:high] + sums[high:]
        for group in range(high // 2):
            send_ref[group, 2 * s : 2 * s + 2, :] = sums[2 * group : 2 * group + 2]

    tall_rows = rows + 2 * OWN
    few = slice(OWN - 2, OWN + rows + 6)
    has_north, has_south = my_lat < nlat - 1, my_lat > 0

    def push_lat():
        courant = jnp.where(jnp.logical_and(lane == 0, my_lat == 0), 0.0, latc[0, 0])
        m2, m1, m0, p1 = face_weights(courant, latb[0, 0])
        north_c = jnp.where(has_north, land_w[1, 0, 0, OWN : OWN + rows], 0.0)
        n2, n1, n0, np1 = face_weights(north_c, land_w[1, 0, 1, OWN : OWN + rows])
        ahead1 = jnp.where(lane == lanes - 1, roll(n1, lanes - 1), roll(m1, lanes - 1))
        round2 = roll(m2, lanes - 2)
        ahead2 = jnp.where(lane >= lanes - 2, roll(n2, lanes - 2), round2)
        behind = roll(p1, 1)
        lat_c[0, 0] = 1.0 - ahead1 + m0
        lat_c[0, 1] = jnp.where(lane <= lanes - 2, ahead1 - ahead2, 0.0)
        lat_c[0, 2] = jnp.where(lane <= lanes - 3, ahead2, 0.0)
        lat_c[0, 3] = jnp.where(lane >= 1, behind - m0, 0.0)
        lat_c[0, 4] = jnp.where(lane >= 2, -behind, 0.0)
        last, first = jnp.logical_and(lane == lanes - 1, has_south), jnp.logical_and(lane == 0, has_north)
        lat_c[1, 1] = jnp.where(last, roll(m1, lanes - 1) - round2, 0.0)
        lat_c[1, 2] = jnp.where(jnp.logical_and(lane >= lanes - 2, has_south), round2, 0.0)
        lat_c[1, 3] = jnp.where(first, behind - n0, 0.0)
        second = jnp.logical_and(lane == 1, has_north)
        lat_c[1, 4] = jnp.where(first, -behind, jnp.where(second, -roll(np1, 1), 0.0))

    def push_lon():
        down = lax.broadcasted_iota(jnp.int32, (tall_rows, lanes), 0)
        across = lax.broadcasted_iota(jnp.int32, (tall_rows, lanes), 1)
        faces = jnp.logical_and(down >= OWN, down <= OWN + rows)
        here, south_of = cos_ref[my_lat], cos_ref[lax.rem(my_lat + nlat - 1, nlat)]
        north_of = cos_ref[lax.rem(my_lat + 1, nlat)]
        across1 = lax.broadcasted_iota(jnp.int32, (1, lanes), 1)
        at_north = jnp.logical_and(across < 2, has_north)
        at_south = jnp.logical_and(across >= lanes - 2, has_south)
        sides = (
            (ids[0], ids[1], here),
            tuple(jnp.where(at_north, beside[1, m], jnp.where(at_south, beside[0, m], 0.0)) for m in range(2))
            + (jnp.where(across1 < 2, north_of, south_of),),
        )
        for side, (courant, branch, cosine) in enumerate(sides):
            m2, m1, m0, p1 = face_weights(jnp.where(faces, courant, 0.0), branch)
            ahead1 = pltpu.roll(m1, tall_rows - 1, 0)
            ahead2 = pltpu.roll(m2, tall_rows - 2, 0)
            behind = pltpu.roll(p1, 1, 0)
            found = (1.0 - ahead1 + m0, ahead1 - ahead2, ahead2, behind - m0, -behind)
            for k, value in enumerate(found):
                lon_c[side, k] = value[few] * cosine

    def squeeze(value):
        return jnp.sum(pltpu.roll(value, 0, 1, stride=4, stride_axis=0), axis=0, keepdims=True)

    def halo_slots():
        shape = (rows + 8, lanes)
        down = lax.broadcasted_iota(jnp.int32, shape, 0)
        across = lax.broadcasted_iota(jnp.int32, shape, 1)
        at_north = jnp.logical_and(across < 2, has_north)
        at_south = jnp.logical_and(across >= lanes - 2, has_south)
        side = jnp.where(at_north, beside[1, 2, few], jnp.where(at_south, beside[0, 2, few], 0.0))
        side = squeeze(jnp.where(down < rows + 4, side, 0.0)).astype(jnp.int32)
        halo = [
            (i, ids[2, OWN - 2 + i : OWN - 1 + i].astype(jnp.int32))
            for i in (0, 1, rows + 2, rows + 3)
        ]
        find_slots(halo + [(rows + 4, side)])

    def push_totals():
        a = y_ref[0]
        turned = (a, roll(a, lanes - 1), roll(a, lanes - 2), roll(a, 1), roll(a, 2))
        for side in range(2):
            value = lat_c[side, 1] * turned[1]
            for k in range(2, 5):
                value = value + lat_c[side, k] * turned[k]
            if side == 0:
                value = value + lat_c[0, 0] * a
            bext[side, OWN : OWN + rows] = value
        found = []
        for side in range(2):
            value = jnp.zeros((rows + 8, lanes), jnp.float32)
            for k, step in enumerate((0, 1, 2, -1, -2)):
                at = OWN - 2 + step
                value = value + lon_c[side, k] * bext[side, at : at + rows + 8]
            found.append(value)
        regions(0, 0, [found[0][: rows + 4], squeeze(found[1])])

    get_mix[1].wait()
    coefficients(1)
    get_adj.wait()
    solve(1)
    for copy in get_lat[1]:
        copy.wait()
    pack_weights(1)
    lat_rows(1)
    for copy in get_lon[1]:
        copy.wait()
    lon_own_weights(1)
    for copy in get_lat[0]:
        copy.wait()
    pack_weights(0)
    for copy in get_lon[0] + get_small:
        copy.wait()
    ids[0, OWN : OWN + rows] = lonc[0, 0]
    ids[1, OWN : OWN + rows] = lonb[0, 0].astype(jnp.float32)
    ids[2, OWN : OWN + rows] = rmap_ref[...].astype(jnp.float32)
    bext[...] = jnp.zeros_like(bext)
    pl.semaphore_wait(barrier, count - 1)

    turn = {1: lax.rem(my_lon + 1, nlon), -1: lax.rem(my_lon + nlon - 1, nlon)}
    own_rows, first, last_two = pl.ds(OWN, rows), pl.ds(OWN, 2), pl.ds(OWN + rows - 2, 2)
    low, high = pl.ds(OWN - 2, 2), pl.ds(OWN + rows, 2)

    class Guarded:
        def __init__(self, copy, send_if, recv_if):
            self.copy, self.send_if, self.recv_if = copy, send_if, recv_if

        def start(self):
            pl.when(self.send_if)(self.copy.start)

        def wait_recv(self):
            pl.when(self.recv_if)(self.copy.wait_recv)

        def wait_send(self):
            pl.when(self.send_if)(self.copy.wait_send)

    def send_columns(source, target, base):
        copies = []
        for end in range(2):
            toward = (north, south)[end][1]
            guards = ((has_north, has_south), (has_south, has_north))[end]
            for k, (lon, src, dst) in enumerate(
                (
                    (my_lon, own_rows, own_rows),
                    (turn[1], last_two, low),
                    (turn[-1], first, high),
                )
            ):
                copy = remote(source(end, src), target(end, dst), base + 3 * end + k, (lon, toward), False)
                copy = Guarded(copy, *guards)
                copy.start()
                copies.append(copy)
        return tuple(copies)

    def exchange(s, base):
        return (
            remote(rows_a.at[0, s], far_a.at[0, s], base, east),
            remote(rows_a.at[1, s], far_a.at[1, s], base + 1, west),
        ) + send_columns(
            lambda end, at: pack_a.at[s, end, at, :],
            lambda end, at: land_a.at[s, end, at, :],
            base + 2,
        )

    def send_lat_weights(s, base):
        return send_columns(
            lambda end, at: pack_w.at[end, s, :, at, :],
            lambda end, at: land_w.at[end, s, :, at, :],
            base,
        )

    def group_of(device):
        return (device * width) // blk

    def scatter(k, carry):
        device = lax.rem(me + k, count)
        pltpu.make_async_remote_copy(
            src_ref=send_ref.at[group_of(device)],
            dst_ref=land.at[me],
            send_sem=all_sem.at[0],
            recv_sem=all_sem.at[1],
            device_id=place(device),
            device_id_type=MESH,
        ).start()
        return carry

    def send_ids(base):
        return (
            remote(ids.at[:, last_two, :], ids.at[:, low, :], base, east),
            remote(ids.at[:, first, :], ids.at[:, high, :], base + 1, west),
        ) + send_columns(
            lambda end, at: ids.at[:, at, :],
            lambda end, at: beside.at[end, :, at, :],
            base + 2,
        )

    sent_a = {1: exchange(1, 0)}
    sent_w = {1: send_lat_weights(1, 16)}
    sent_ids = send_ids(34)
    sent_lon = {1: send_lon(1, 28)}
    sent_w[0] = send_lat_weights(0, 22)
    lat_inner(1)
    get_mix[0].wait()
    coefficients(0)
    lon_own_weights(0)
    sent_lon[0] = send_lon(0, 31)
    find_slots([(2 + i, rmap_ref[i : i + 1, :]) for i in range(rows)])
    for copy in sent_w[0]:
        copy.wait_recv()
    push_lat()
    for copy in sent_ids + sent_a[1] + sent_w[1]:
        copy.wait_recv()
    push_lon()
    halo_slots()
    lat_edges(1)
    for copy in sent_lon[1]:
        copy.wait_recv()

    def middle(level, carry):
        x_ref[level] = lon_level(1, level)
        return carry

    lax.fori_loop(0, levels, middle, 0, unroll=True)
    solve(0)
    lat_rows(0)
    sent_a[0] = exchange(0, 8)
    push_totals()
    regions(1, 2, [x_ref[0] * cos_ref[my_lat]])
    lax.fori_loop(1, count, scatter, 0)
    land[me] = send_ref[group_of(me)]
    lat_inner(0)
    get_cov.wait()
    covh[...] = covv[...].astype(jnp.bfloat16)
    covl[...] = (covv[...] - covh[...].astype(jnp.float32)).astype(jnp.bfloat16)
    for copy in sent_a[0]:
        copy.wait_recv()
    lat_edges(0)
    for copy in sent_lon[0]:
        copy.wait_recv()

    def last(level, carry):
        out_ref[level] = lon_level(0, level)
        return carry

    lax.fori_loop(0, levels, last, 0, unroll=True)
    put_out = fetch(out_ref, out_h, 15)
    for s in range(steps):
        for copy in sent_a[s] + sent_w[s] + sent_lon[s]:
            copy.wait_send()
    for copy in sent_ids:
        copy.wait_send()
    every = land.at[pl.ds(0, count - 1)]
    pltpu.make_async_copy(every, every, all_sem.at[0]).wait()
    pltpu.make_async_copy(every, every, all_sem.at[1]).wait()
    totals = jnp.sum(land[...], axis=0)
    coarse = totals.astype(jnp.bfloat16).astype(jnp.float32)
    both = jnp.concatenate([coarse, totals - coarse, jnp.zeros((8, lanes), jnp.float32)], axis=0)
    both = both.astype(jnp.bfloat16)
    half = blk // 2

    def product(at):
        found = jnp.dot(both, covh[at], preferred_element_type=jnp.float32)
        found = found + jnp.dot(both, covl[at], preferred_element_type=jnp.float32)
        return found[:4] + found[4:8]

    one, two = product(slice(0, half)), product(slice(half, blk))
    for s in range(steps):
        flux_ref[s : s + 1, :] = one[2 * s : 2 * s + 1] + two[2 * s + 1 : 2 * s + 2]
    put_flux = fetch(flux_ref, flux_h, 16)
    put_out.wait()
    put_flux.wait()


def store(adjoint_v, flux_v, adjoint_h, flux_h, sem):
    copies = (
        pltpu.make_async_copy(adjoint_v, adjoint_h, sem.at[0]),
        pltpu.make_async_copy(flux_v, flux_h, sem.at[1]),
    )
    for copy in copies:
        copy.start()
    for copy in copies:
        copy.wait()


def per_device(
    nlon,
    nlat,
    adjoint_final,
    lon_courant,
    lon_branch,
    lat_courant,
    lat_branch,
    mixing,
    region_map,
    region_order,
    prior_cov,
):
    steps, levels, rows, lanes = lon_courant.shape
    regions = region_order.shape[0]
    blk = prior_cov.shape[1]
    width = regions // (nlon * nlat)
    lat_total = lanes * nlat
    lat_index = np.arange(lat_total, dtype=np.float32)
    angle = (lat_index + np.float32(0.5)) * np.float32(math.pi / lat_total)
    cosines = np.cos((angle - np.float32(0.5 * math.pi)).astype(np.float32))
    cosines = jnp.asarray(cosines.astype(np.float32).reshape(nlat, 1, lanes))
    f32, i32, b16 = jnp.float32, jnp.int32, jnp.bfloat16
    field = (levels, rows, lanes)
    tall = (levels, rows + 2 * OWN, lanes)
    vm = pltpu.VMEM
    scratch = [
        vm(field, f32),
        vm((steps, blk), f32),
        vm((rows, lanes), i32),
        vm((regions // 128, 128), i32),
        vm((nlat, 1, lanes), f32),
        vm(field, f32),
        vm((steps, levels - 1, rows, lanes), f32),
        vm((steps,) + field, f32),
        vm((steps,) + field, i32),
        vm((steps,) + field, f32),
        vm((steps,) + field, i32),
        vm((blk, blk), f32),
        vm((blk, blk), b16),
        vm((blk, blk), b16),
        vm((steps,) + field, f32),
        vm((steps,) + field, f32),
        vm((steps,) + field, f32),
        vm(field, f32),
        vm((steps,) + tall, f32),
        vm((steps, 4) + tall, f32),
        vm((2, steps, 2, rows + 2 * OWN, lanes), f32),
        vm((2, steps, 2, rows + 2 * OWN, lanes), f32),
        vm((steps, 2, rows + 2 * OWN, lanes), f32),
        vm((steps, 2, rows + 2 * OWN, lanes), f32),
        vm((2, 2 * levels, lanes), f32),
        vm((2, steps, 2 * levels + 8, lanes), f32),
        vm((2, steps, 2 * levels + 8, lanes), f32),
        vm((2, steps, 2, 2 * levels, lanes), f32),
        vm((3, rows + 2 * OWN, lanes), f32),
        vm((2, 3, rows + 2 * OWN, lanes), f32),
        vm((2, 5, rows, lanes), f32),
        vm((2, 5, rows + 8, lanes), f32),
        vm((2, rows + 2 * OWN, lanes), f32),
        vm((regions // 128, (rows + 5) * lanes), b16),
        vm((128, (rows + 5) * lanes), b16),
        vm((2 * (regions // 128), (rows + 5) * lanes), b16),
        vm((regions // blk, 4, 128), f32),
        vm((nlon * nlat, 4, 128), f32),
        pltpu.SemaphoreType.DMA((17,)),
        pltpu.SemaphoreType.DMA((42,)),
        pltpu.SemaphoreType.DMA((42,)),
        pltpu.SemaphoreType.DMA((2,)),
    ]
    adjoint, flux = pl.pallas_call(
        functools.partial(kernel, nlon, nlat, width),
        out_shape=(
            pltpu.VMEM(field, f32),
            pltpu.VMEM((steps, blk), f32),
        ),
        in_specs=[pl.BlockSpec(memory_space=pltpu.HBM)] * 10,
        out_specs=(
            pl.BlockSpec(memory_space=pl.ANY),
            pl.BlockSpec(memory_space=pl.ANY),
        ),
        scratch_shapes=scratch,
        compiler_params=pltpu.CompilerParams(
            collective_id=0, has_side_effects=True, vmem_limit_bytes=61 * 1024 * 1024
        ),
    )(
        adjoint_final,
        lon_courant,
        lon_branch,
        lat_courant,
        lat_branch,
        mixing,
        prior_cov,
        region_map,
        region_order.reshape(regions // 128, 128),
        cosines,
    )
    adjoint, flux = pl.pallas_call(
        store,
        out_shape=(
            jax.ShapeDtypeStruct(field, f32),
            jax.ShapeDtypeStruct((steps, blk), f32),
        ),
        in_specs=[pl.BlockSpec(memory_space=pl.ANY)] * 2,
        out_specs=(pl.BlockSpec(memory_space=pl.ANY),) * 2,
        scratch_shapes=[pltpu.SemaphoreType.DMA((2,))],
    )(pltpu.with_memory_space_constraint(adjoint, pltpu.VMEM), pltpu.with_memory_space_constraint(flux, pltpu.VMEM))
    if width < blk:
        start = lax.rem(lax.axis_index("lat") * width, blk)
        flux = lax.dynamic_slice_in_dim(flux, start, width, 1)
    return adjoint, flux


def solution(mesh):
    four = P(None, None, "lon", "lat")
    placed = (
        P(None, "lon", "lat"),
        four,
        four,
        four,
        four,
        four,
        P("lon", "lat"),
        P(),
        P("lon", None, None),
    )
    return jax.shard_map(
        functools.partial(per_device, mesh.shape["lon"], mesh.shape["lat"]),
        mesh=mesh,
        in_specs=placed,
        out_specs=(P(None, "lon", "lat"), P(None, ("lon", "lat"))),
        check_vma=False,
    )
```

```python
import functools
import math

import jax
import jax.numpy as jnp
import numpy as np
from jax import lax
from jax.experimental import pallas as pl
from jax.experimental.pallas import tpu as pltpu
from jax.sharding import PartitionSpec as P

MESH = pl.DeviceIdType.MESH
OWN = 8


def face_weights(courant, branch):
    lean_part = courant * (0.5 * (1.0 - jnp.abs(courant)))
    one_part = jnp.where(branch == 1, lean_part, 0.0)
    two_part = jnp.where(branch == 2, lean_part, 0.0)
    donor = courant - one_part + two_part
    left = courant > 0.0
    return (
        jnp.where(left, -two_part, 0.0),
        jnp.where(left, donor, one_part),
        jnp.where(left, one_part, donor),
        jnp.where(left, 0.0, -two_part),
    )


def kernel(
    nlon,
    nlat,
    width,
    adj_h,
    lonc_h,
    lonb_h,
    latc_h,
    latb_h,
    mix_h,
    cov_h,
    rmap_h,
    order_h,
    cos_h,
    out_h,
    flux_h,
    out_ref,
    flux_ref,
    rmap_ref,
    order_ref,
    cos_ref,
    x_ref,
    mixv,
    latc,
    latb,
    lonc,
    lonb,
    covv,
    covh,
    covl,
    inv_ref,
    kin_ref,
    nr_ref,
    y_ref,
    ext,
    lw,
    pack,
    land_p,
    raw_rows,
    rows_a,
    far_a,
    rows_w,
    ids,
    beside,
    lat_c,
    lon_c,
    bext,
    hot,
    cht,
    amat,
    send_ref,
    land,
    sizer,
    local_sem,
    send_sem,
    recv_sem,
    all_sem,
):
    steps, levels, rows, lanes = latc.shape
    count = nlon * nlat
    my_lon, my_lat = lax.axis_index("lon"), lax.axis_index("lat")
    me = my_lon * nlat + my_lat
    blk = covv.shape[0]

    def place(device):
        return (device // nlat, lax.rem(device, nlat))

    barrier = pltpu.get_barrier_semaphore()

    def fetch(src, dst, slot):
        pltpu.make_async_copy(src, dst, local_sem.at[slot]).start()

    def drain(sem, count_rows):
        part = sizer.at[pl.ds(0, count_rows)]
        pltpu.make_async_copy(part, part, sem).wait()

    def got(slot, count_rows):
        drain(local_sem.at[slot], count_rows)

    fetch(mix_h.at[1], mixv.at[1], 0)
    fetch(adj_h, x_ref, 1)
    fetch(latc_h.at[1], latc.at[1], 2)
    fetch(latb_h.at[1], latb.at[1], 2)
    fetch(lonc_h.at[1], lonc.at[1], 3)
    fetch(lonb_h.at[1], lonb.at[1], 3)
    fetch(latc_h.at[0], latc.at[0], 4)
    fetch(latb_h.at[0], latb.at[0], 4)
    fetch(lonc_h.at[0], lonc.at[0], 4)
    fetch(lonb_h.at[0], lonb.at[0], 4)
    fetch(rmap_h, rmap_ref, 5)
    fetch(order_h, order_ref, 5)
    fetch(cos_h, cos_ref, 5)
    fetch(mix_h.at[0], mixv.at[0], 6)
    fetch(cov_h.at[(my_lat * width) // blk], covv, 7)

    far_first = jnp.where(my_lon >= nlon // 2, 1, 0)

    def greet(k, carry):
        device = far_first * k + (1 - far_first) * (count - 1 - k)

        @pl.when(device != me)
        def _():
            pl.semaphore_signal(barrier, inc=1, device_id=place(device), device_id_type=MESH)

        return carry

    lax.fori_loop(0, count, greet, 0)

    lane = lax.broadcasted_iota(jnp.int32, (rows, lanes), 1)
    pair = lane // 2
    even = lax.rem(lane, 2) == 0
    zero = jnp.zeros((rows, lanes), jnp.float32)

    def roll(value, shift):
        return pltpu.roll(value, shift, 1)

    def remote(src, dst, send_slot, recv_slot, device):
        pltpu.make_async_remote_copy(
            src_ref=src,
            dst_ref=dst,
            send_sem=send_sem.at[send_slot],
            recv_sem=recv_sem.at[recv_slot],
            device_id=device,
            device_id_type=MESH,
        ).start()

    north = (my_lon, lax.rem(my_lat + 1, nlat))
    south = (my_lon, lax.rem(my_lat + nlat - 1, nlat))
    east = (lax.rem(my_lon + 1, nlon), my_lat)
    west = (lax.rem(my_lon + nlon - 1, nlon), my_lat)

    def coefficients(s):
        k = mixv[s, 0]
        inv = 1.0 / (1.0 + k)
        inv_ref[s, 0] = inv
        kin_ref[s, 0] = zero
        nr_ref[s, 0] = k * inv

        def body(level, ahead):
            lower, k = mixv[s, level - 1], mixv[s, level]
            inv = 1.0 / ((1.0 + k) + lower * (1.0 - ahead))
            inv_ref[s, level] = inv
            kin_ref[s, level] = lower * inv
            ahead = k * inv
            nr_ref[s, level] = ahead
            return ahead

        ahead = lax.fori_loop(1, levels - 1, body, k * inv, unroll=True)
        lower = mixv[s, levels - 2]
        inv = 1.0 / (1.0 + lower * (1.0 - ahead))
        inv_ref[s, levels - 1] = inv
        kin_ref[s, levels - 1] = lower * inv
        nr_ref[s, levels - 1] = zero

    def tail_head(value, level, tail, head):
        turned = roll(value, 2 * level + 2)
        return jnp.where(pair == level, turned, tail), jnp.where(pair == level + 1, turned, head)

    def solve(s):
        def up(level, carried):
            carried = x_ref[level] * inv_ref[s, level] + kin_ref[s, level] * carried
            y_ref[level] = carried
            return carried

        lax.fori_loop(0, levels, up, zero, unroll=True)

        def down(i, carry):
            value, tail, head = carry
            level = levels - 1 - i
            value = y_ref[level] + nr_ref[s, level] * value
            y_ref[level] = value
            raw_rows[0, pl.ds(2 * level, 2), :] = value[rows - 2 :]
            raw_rows[1, pl.ds(2 * level, 2), :] = value[:2]
            return (value,) + tail_head(value, level, tail, head)

        _, tail, head = lax.fori_loop(0, levels, down, (zero, zero, zero), unroll=True)
        head = roll(head, lanes - 2)
        for member, value in enumerate((tail, head)):
            pack[s, member, 0, OWN : OWN + rows] = value
            at = 2 * levels + 2 * member
            rows_a[0, s, at : at + 2] = value[rows - 2 :]
            rows_a[1, s, at : at + 2] = value[:2]

    def pack_weights(s):
        def body(level, carry):
            ct, ch, bt, bh = carry
            ct, ch = tail_head(latc[s, level], level, ct, ch)
            both = (latc[s, level], latb[s, level].astype(jnp.float32))
            bt, bh = tail_head(both[1], level, bt, bh)
            for member in range(2):
                rows_w[0, s, member, pl.ds(2 * level, 2), :] = both[member][rows - 2 :]
                rows_w[1, s, member, pl.ds(2 * level, 2), :] = both[member][:2]
            return ct, ch, bt, bh

        ct, ch, bt, bh = lax.fori_loop(0, levels, body, (zero,) * 4, unroll=True)
        found = ((ct, bt), (roll(ch, lanes - 2), roll(bh, lanes - 2)))
        for end in range(2):
            for member in range(2):
                pack[s, end, 1 + member, OWN : OWN + rows] = found[end][member]
        for member in range(2):
            at = 2 * levels + 4 + 2 * member
            rows_a[0, s, at : at + 2] = found[1][member][rows - 2 :]
            rows_a[1, s, at : at + 2] = found[1][member][:2]

    def lat_rows(s):
        for side in range(2):
            rows_a[side, s, : 2 * levels] = lat_pass(
                raw_rows[side], rows_w[side, s, 0], rows_w[side, s, 1]
            )

    def lat_pass(a, courant, branch):
        at = lax.broadcasted_iota(jnp.int32, a.shape, 1)
        m2, m1, m0, p1 = face_weights(courant, branch)
        jump = jnp.where(at >= 1, a - roll(a, 1), 0.0)
        out = a + m0 * jump + roll(m1 * jump, lanes - 1)
        out = out + roll(jnp.where(at >= 2, m2 * jump, 0.0), lanes - 2)
        return out + roll(jnp.where(at <= lanes - 2, p1 * jump, 0.0), 1)

    def lat_inner(s):
        def body(level, carry):
            out = lat_pass(y_ref[level], latc[s, level], latb[s, level])
            ext[s, level, OWN : OWN + rows] = out
            return carry

        lax.fori_loop(0, levels, body, 0, unroll=True)

    def lat_edges(s):
        at = 2 * levels
        lane = lax.broadcasted_iota(jnp.int32, (rows + 2 * OWN, lanes), 1)
        even = lax.rem(lane, 2) == 0
        for side, where in enumerate((slice(OWN - 2, OWN), slice(OWN + rows, OWN + rows + 2))):
            for member in range(2):
                pack[s, member, 0, where] = far_a[side, s, at + 2 * member : at + 2 * member + 2]
                far = at + 4 + 2 * member
                pack[s, 1, 1 + member, where] = far_a[side, s, far : far + 2]
        tail, head = pack[s, 0, 0], pack[s, 1, 0]
        before, after = land_p[s, 0, 0], land_p[s, 1, 0]
        m2_after, m1_after, _, _ = face_weights(land_p[s, 1, 1], land_p[s, 1, 2])
        _, _, m0_head, p1_head = face_weights(pack[s, 1, 1], pack[s, 1, 2])
        _, _, _, p1_before = face_weights(land_p[s, 0, 1], land_p[s, 0, 2])
        jump = after - jnp.where(even, roll(tail, lanes - 1), roll(after, 1))
        top = m2_after * jump + roll(jnp.where(even, m1_after * jump, 0.0), 1)
        top = jnp.where(my_lat < nlat - 1, top, 0.0)
        jump = jnp.where(even, head - roll(before, lanes - 1), before - roll(before, 1))
        flux = jnp.where(even, p1_head, p1_before) * jump
        low = jnp.where(even, m0_head * jump + roll(flux, lanes - 1), roll(flux, 1))
        low = roll(jnp.where(my_lat > 0, low, 0.0), 2)
        first = lax.rem(lane, 4) < 2
        both = (jnp.where(first, top, low), jnp.where(first, low, top))
        edge = jnp.logical_or(lane < 2, lane >= lanes - 2)

        def body(m, carry):
            for odd in range(2):
                level = 2 * m + odd
                turned = jnp.where(edge, roll(both[odd], lanes - 2 - 2 * level), 0.0)
                ext[s, level, OWN : OWN + rows] += turned[OWN : OWN + rows]
                two = pl.ds(2 * level, 2)
                end = OWN + rows
                ext[s, level, OWN - 2 : OWN] = far_a[0, s, two, :] + turned[OWN - 2 : OWN]
                ext[s, level, end : end + 2] = far_a[1, s, two, :] + turned[end : end + 2]
            return carry

        lax.fori_loop(0, levels // 2, body, 0, unroll=True)

    def lon_own_weights(s):
        def body(level, carry):
            found = face_weights(
                lonc[s, level], lonb[s, level]
            )
            for member in range(4):
                lw[s, member, level, OWN : OWN + rows] = found[member]
            return carry

        lax.fori_loop(0, levels, body, 0, unroll=True)

    def lon_level(s, level):
        a = [ext[s, level, OWN + k : OWN + k + rows] for k in range(-2, 3)]
        w = [
            lw[s, member, level, OWN + 2 - member : OWN + 2 - member + rows]
            for member in range(4)
        ]
        out = a[2] + w[0] * (a[4] - a[3]) + w[1] * (a[3] - a[2])
        return out + w[2] * (a[2] - a[1]) + w[3] * (a[1] - a[0])

    def send_lon(s):
        end = OWN + rows
        for member, src, dst, size, device in (
            (0, OWN, end, 2, west),
            (1, OWN, end, 1, west),
            (3, end - 1, OWN - 1, 1, east),
        ):
            remote(
                lw.at[s, member, :, pl.ds(src, size), :],
                lw.at[s, member, :, pl.ds(dst, size), :],
                0,
                s,
                device,
            )

    def find_slots(found_rows):
        order = order_ref[...]
        table = jnp.concatenate([order // 128, lax.rem(order, 128)], axis=0)
        table = table.astype(jnp.float32).astype(jnp.bfloat16)
        high = order.shape[0]
        down = lax.broadcasted_iota(jnp.int32, (lanes, lanes), 0)
        row_of = lax.broadcasted_iota(jnp.int32, (high, lanes), 0)
        for i, region in found_rows:
            hit = jnp.where(down == lax.rem(region, 128), 1.0, 0.0).astype(jnp.bfloat16)
            found = jnp.dot(table, hit, preferred_element_type=jnp.float32)
            here = row_of == region // 128
            hi = jnp.sum(jnp.where(here, found[:high], 0.0), axis=0, keepdims=True)
            lo = jnp.sum(jnp.where(here, found[high:], 0.0), axis=0, keepdims=True)
            at = slice(i * lanes, (i + 1) * lanes)
            hot[:, at] = jnp.where(row_of.astype(jnp.float32) == hi, 1.0, 0.0).astype(jnp.bfloat16)
            cht[:, at] = jnp.where(down.astype(jnp.float32) == lo, 1.0, 0.0).astype(jnp.bfloat16)

    def regions(s, first, fields):
        high = order_ref.shape[0]
        coarse = [field.astype(jnp.bfloat16).astype(jnp.float32) for field in fields]
        fine = [field - part for field, part in zip(fields, coarse)]
        at = first
        for field in range(len(fields)):
            for i in range(fields[field].shape[0]):
                here = slice(at * lanes, (at + 1) * lanes)
                for part, values in enumerate((coarse, fine)):
                    value = jnp.broadcast_to(values[field][i : i + 1], (high, lanes))
                    amat[part * high : (part + 1) * high, here] = hot[:, here] * value.astype(
                        jnp.bfloat16
                    )
                at += 1
        every = slice(first * lanes, at * lanes)
        sums = lax.dot_general(
            amat[:, every],
            cht[:, every],
            (((1,), (1,)), ((), ())),
            preferred_element_type=jnp.float32,
        )
        sums = sums[:high] + sums[high:]
        for group in range(high // 2):
            send_ref[group, 2 * s : 2 * s + 2, :] = sums[2 * group : 2 * group + 2]

    tall_rows = rows + 2 * OWN
    few = slice(OWN - 2, OWN + rows + 6)
    has_north, has_south = my_lat < nlat - 1, my_lat > 0

    def push_lat():
        courant = jnp.where(jnp.logical_and(lane == 0, my_lat == 0), 0.0, latc[0, 0])
        m2, m1, m0, p1 = face_weights(courant, latb[0, 0])
        north_c = jnp.where(has_north, land_p[0, 1, 1, OWN : OWN + rows], 0.0)
        n2, n1, n0, np1 = face_weights(north_c, land_p[0, 1, 2, OWN : OWN + rows])
        ahead1 = jnp.where(lane == lanes - 1, roll(n1, lanes - 1), roll(m1, lanes - 1))
        round2 = roll(m2, lanes - 2)
        ahead2 = jnp.where(lane >= lanes - 2, roll(n2, lanes - 2), round2)
        behind = roll(p1, 1)
        lat_c[0, 0] = 1.0 - ahead1 + m0
        lat_c[0, 1] = jnp.where(lane <= lanes - 2, ahead1 - ahead2, 0.0)
        lat_c[0, 2] = jnp.where(lane <= lanes - 3, ahead2, 0.0)
        lat_c[0, 3] = jnp.where(lane >= 1, behind - m0, 0.0)
        lat_c[0, 4] = jnp.where(lane >= 2, -behind, 0.0)
        last, first = jnp.logical_and(lane == lanes - 1, has_south), jnp.logical_and(lane == 0, has_north)
        lat_c[1, 1] = jnp.where(last, roll(m1, lanes - 1) - round2, 0.0)
        lat_c[1, 2] = jnp.where(jnp.logical_and(lane >= lanes - 2, has_south), round2, 0.0)
        lat_c[1, 3] = jnp.where(first, behind - n0, 0.0)
        second = jnp.logical_and(lane == 1, has_north)
        lat_c[1, 4] = jnp.where(first, -behind, jnp.where(second, -roll(np1, 1), 0.0))

    def push_lon():
        down = lax.broadcasted_iota(jnp.int32, (tall_rows, lanes), 0)
        across = lax.broadcasted_iota(jnp.int32, (tall_rows, lanes), 1)
        faces = jnp.logical_and(down >= OWN, down <= OWN + rows)
        here, south_of = cos_ref[my_lat], cos_ref[lax.rem(my_lat + nlat - 1, nlat)]
        north_of = cos_ref[lax.rem(my_lat + 1, nlat)]
        across1 = lax.broadcasted_iota(jnp.int32, (1, lanes), 1)
        at_north = jnp.logical_and(across < 2, has_north)
        at_south = jnp.logical_and(across >= lanes - 2, has_south)
        sides = (
            (ids[0], ids[1], here),
            tuple(jnp.where(at_north, beside[1, m], jnp.where(at_south, beside[0, m], 0.0)) for m in range(2))
            + (jnp.where(across1 < 2, north_of, south_of),),
        )
        for side, (courant, branch, cosine) in enumerate(sides):
            m2, m1, m0, p1 = face_weights(jnp.where(faces, courant, 0.0), branch)
            ahead1 = pltpu.roll(m1, tall_rows - 1, 0)
            ahead2 = pltpu.roll(m2, tall_rows - 2, 0)
            behind = pltpu.roll(p1, 1, 0)
            found = (1.0 - ahead1 + m0, ahead1 - ahead2, ahead2, behind - m0, -behind)
            for k, value in enumerate(found):
                lon_c[side, k] = value[few] * cosine

    def squeeze(value):
        return jnp.sum(pltpu.roll(value, 0, 1, stride=4, stride_axis=0), axis=0, keepdims=True)

    def halo_slots():
        shape = (rows + 8, lanes)
        down = lax.broadcasted_iota(jnp.int32, shape, 0)
        across = lax.broadcasted_iota(jnp.int32, shape, 1)
        at_north = jnp.logical_and(across < 2, has_north)
        at_south = jnp.logical_and(across >= lanes - 2, has_south)
        side = jnp.where(at_north, beside[1, 2, few], jnp.where(at_south, beside[0, 2, few], 0.0))
        side = squeeze(jnp.where(down < rows + 4, side, 0.0)).astype(jnp.int32)
        halo = [
            (i, ids[2, OWN - 2 + i : OWN - 1 + i].astype(jnp.int32))
            for i in (0, 1, rows + 2, rows + 3)
        ]
        find_slots(halo + [(rows + 4, side)])

    def push_totals():
        a = y_ref[0]
        turned = (a, roll(a, lanes - 1), roll(a, lanes - 2), roll(a, 1), roll(a, 2))
        for side in range(2):
            value = lat_c[side, 1] * turned[1]
            for k in range(2, 5):
                value = value + lat_c[side, k] * turned[k]
            if side == 0:
                value = value + lat_c[0, 0] * a
            bext[side, OWN : OWN + rows] = value
        found = []
        for side in range(2):
            value = jnp.zeros((rows + 8, lanes), jnp.float32)
            for k, step in enumerate((0, 1, 2, -1, -2)):
                at = OWN - 2 + step
                value = value + lon_c[side, k] * bext[side, at : at + rows + 8]
            found.append(value)
        regions(0, 0, [found[0][: rows + 4], squeeze(found[1])])

    got(0, (levels - 1) * rows)
    coefficients(1)
    got(1, levels * rows)
    solve(1)
    got(2, 2 * levels * rows)
    pack_weights(1)
    lat_rows(1)
    got(3, 2 * levels * rows)
    lon_own_weights(1)
    got(4, 4 * levels * rows)
    pack_weights(0)
    got(5, rows + order_ref.shape[0] + nlat)
    ids[0, OWN : OWN + rows] = lonc[0, 0]
    ids[1, OWN : OWN + rows] = lonb[0, 0].astype(jnp.float32)
    ids[2, OWN : OWN + rows] = rmap_ref[...].astype(jnp.float32)
    bext[...] = jnp.zeros_like(bext)
    pl.semaphore_wait(barrier, count - 1)

    turn = {1: lax.rem(my_lon + 1, nlon), -1: lax.rem(my_lon + nlon - 1, nlon)}
    own_rows, first, last_two = pl.ds(OWN, rows), pl.ds(OWN, 2), pl.ds(OWN + rows - 2, 2)
    low, high = pl.ds(OWN - 2, 2), pl.ds(OWN + rows, 2)

    toward = (north[1], south[1])
    send_if, recv_if = (has_north, has_south), (has_south, has_north)
    column_rows = rows + 4

    def send_columns(source, target, recv_base):
        for end in range(2):

            @pl.when(send_if[end])
            def _():
                for lon, src, dst in (
                    (turn[1], last_two, low),
                    (turn[-1], first, high),
                    (my_lon, own_rows, own_rows),
                ):
                    remote(
                        source(end, src),
                        target(end, dst),
                        1 + end,
                        recv_base + end,
                        (lon, toward[end]),
                    )

    def got_columns(recv_base, members):
        for end in range(2):

            @pl.when(recv_if[end])
            def _():
                drain(recv_sem.at[recv_base + end], members * column_rows)

    def send_border(s):
        remote(rows_a.at[0, s], far_a.at[0, s], 0, 2 + s, east)
        remote(rows_a.at[1, s], far_a.at[1, s], 0, 2 + s, west)

    border_rows = 2 * rows_a.shape[2]
    lon_rows = 4 * levels

    def group_of(device):
        return (device * width) // blk

    def scatter(k, carry):
        device = lax.rem(me + k, count)
        pltpu.make_async_remote_copy(
            src_ref=send_ref.at[group_of(device)],
            dst_ref=land.at[me],
            send_sem=all_sem.at[0],
            recv_sem=all_sem.at[1],
            device_id=place(device),
            device_id_type=MESH,
        ).start()
        return carry

    send_columns(
        lambda end, at: pack.at[1, end, :, at, :], lambda end, at: land_p.at[1, end, :, at, :], 5
    )
    remote(ids.at[:, last_two, :], ids.at[:, low, :], 0, 4, east)
    remote(ids.at[:, first, :], ids.at[:, high, :], 0, 4, west)
    send_columns(lambda end, at: ids.at[:, at, :], lambda end, at: beside.at[end, :, at, :], 7)
    send_columns(
        lambda end, at: pack.at[0, end, 1:3, at, :],
        lambda end, at: land_p.at[0, end, 1:3, at, :],
        7,
    )
    send_border(1)
    send_lon(1)
    lat_inner(1)
    got(6, (levels - 1) * rows)
    coefficients(0)
    lon_own_weights(0)
    send_lon(0)
    find_slots([(2 + i, rmap_ref[i : i + 1, :]) for i in range(rows)])
    drain(recv_sem.at[4], 12)
    got_columns(7, 5)
    push_lat()
    push_lon()
    halo_slots()
    got_columns(5, 3)
    drain(recv_sem.at[3], border_rows)
    drain(recv_sem.at[1], lon_rows)
    lat_edges(1)

    def middle(level, carry):
        x_ref[level] = lon_level(1, level)
        return carry

    lax.fori_loop(0, levels, middle, 0, unroll=True)
    regions(1, 2, [x_ref[0] * cos_ref[my_lat]])
    solve(0)
    lat_rows(0)
    send_columns(
        lambda end, at: pack.at[0, end, 0, at, :], lambda end, at: land_p.at[0, end, 0, at, :], 9
    )
    send_border(0)
    push_totals()
    lax.fori_loop(1, count, scatter, 0)
    land[me] = send_ref[group_of(me)]
    lat_inner(0)
    got(7, blk * blk // lanes)
    covh[...] = covv[...].astype(jnp.bfloat16)
    covl[...] = (covv[...] - covh[...].astype(jnp.float32)).astype(jnp.bfloat16)
    got_columns(9, 1)
    drain(recv_sem.at[2], border_rows)
    drain(recv_sem.at[0], lon_rows)
    lat_edges(0)

    def last(level, carry):
        out_ref[level] = lon_level(0, level)
        return carry

    lax.fori_loop(0, levels, last, 0, unroll=True)
    fetch(out_ref, out_h, 8)
    drain(send_sem.at[0], 2 * (border_rows + lon_rows) + 12)
    for end in range(2):

        @pl.when(send_if[end])
        def _():
            drain(send_sem.at[1 + end], 9 * column_rows)

    every = land.at[pl.ds(0, count - 1)]
    pltpu.make_async_copy(every, every, all_sem.at[0]).wait()
    pltpu.make_async_copy(every, every, all_sem.at[1]).wait()
    totals = jnp.sum(land[...], axis=0)
    coarse = totals.astype(jnp.bfloat16).astype(jnp.float32)
    both = jnp.concatenate([coarse, totals - coarse, jnp.zeros((8, lanes), jnp.float32)], axis=0)
    both = both.astype(jnp.bfloat16)
    half = blk // 2

    def product(at):
        found = jnp.dot(both, covh[at], preferred_element_type=jnp.float32)
        found = found + jnp.dot(both, covl[at], preferred_element_type=jnp.float32)
        return found[:4] + found[4:8]

    one, two = product(slice(0, half)), product(slice(half, blk))
    for s in range(steps):
        flux_ref[s : s + 1, :] = one[2 * s : 2 * s + 1] + two[2 * s + 1 : 2 * s + 2]
    fetch(flux_ref, flux_h, 8)
    got(8, levels * rows + steps * blk // lanes)


def store(adjoint_v, flux_v, adjoint_h, flux_h, sem):
    copies = (
        pltpu.make_async_copy(adjoint_v, adjoint_h, sem.at[0]),
        pltpu.make_async_copy(flux_v, flux_h, sem.at[1]),
    )
    for copy in copies:
        copy.start()
    for copy in copies:
        copy.wait()


def per_device(
    nlon,
    nlat,
    adjoint_final,
    lon_courant,
    lon_branch,
    lat_courant,
    lat_branch,
    mixing,
    region_map,
    region_order,
    prior_cov,
):
    steps, levels, rows, lanes = lon_courant.shape
    regions = region_order.shape[0]
    blk = prior_cov.shape[1]
    width = regions // (nlon * nlat)
    lat_total = lanes * nlat
    lat_index = np.arange(lat_total, dtype=np.float32)
    angle = (lat_index + np.float32(0.5)) * np.float32(math.pi / lat_total)
    cosines = np.cos((angle - np.float32(0.5 * math.pi)).astype(np.float32))
    cosines = jnp.asarray(cosines.astype(np.float32).reshape(nlat, 1, lanes))
    f32, i32, b16 = jnp.float32, jnp.int32, jnp.bfloat16
    field = (levels, rows, lanes)
    tall = (levels, rows + 2 * OWN, lanes)
    vm = pltpu.VMEM
    scratch = [
        vm(field, f32),
        vm((steps, blk), f32),
        vm((rows, lanes), i32),
        vm((regions // 128, 128), i32),
        vm((nlat, 1, lanes), f32),
        vm(field, f32),
        vm((steps, levels - 1, rows, lanes), f32),
        vm((steps,) + field, f32),
        vm((steps,) + field, i32),
        vm((steps,) + field, f32),
        vm((steps,) + field, i32),
        vm((blk, blk), f32),
        vm((blk, blk), b16),
        vm((blk, blk), b16),
        vm((steps,) + field, f32),
        vm((steps,) + field, f32),
        vm((steps,) + field, f32),
        vm(field, f32),
        vm((steps,) + tall, f32),
        vm((steps, 4) + tall, f32),
        vm((steps, 2, 3, rows + 2 * OWN, lanes), f32),
        vm((steps, 2, 3, rows + 2 * OWN, lanes), f32),
        vm((2, 2 * levels, lanes), f32),
        vm((2, steps, 2 * levels + 8, lanes), f32),
        vm((2, steps, 2 * levels + 8, lanes), f32),
        vm((2, steps, 2, 2 * levels, lanes), f32),
        vm((3, rows + 2 * OWN, lanes), f32),
        vm((2, 3, rows + 2 * OWN, lanes), f32),
        vm((2, 5, rows, lanes), f32),
        vm((2, 5, rows + 8, lanes), f32),
        vm((2, rows + 2 * OWN, lanes), f32),
        vm((regions // 128, (rows + 5) * lanes), b16),
        vm((128, (rows + 5) * lanes), b16),
        vm((2 * (regions // 128), (rows + 5) * lanes), b16),
        vm((regions // blk, 4, 128), f32),
        vm((nlon * nlat, 4, 128), f32),
        vm((4 * levels * rows, lanes), f32),
        pltpu.SemaphoreType.DMA((9,)),
        pltpu.SemaphoreType.DMA((3,)),
        pltpu.SemaphoreType.DMA((11,)),
        pltpu.SemaphoreType.DMA((2,)),
    ]
    adjoint, flux = pl.pallas_call(
        functools.partial(kernel, nlon, nlat, width),
        out_shape=(
            pltpu.VMEM(field, f32),
            pltpu.VMEM((steps, blk), f32),
        ),
        in_specs=[pl.BlockSpec(memory_space=pltpu.HBM)] * 10,
        out_specs=(
            pl.BlockSpec(memory_space=pl.ANY),
            pl.BlockSpec(memory_space=pl.ANY),
        ),
        scratch_shapes=scratch,
        compiler_params=pltpu.CompilerParams(
            collective_id=0, has_side_effects=True, vmem_limit_bytes=61 * 1024 * 1024
        ),
    )(
        adjoint_final,
        lon_courant,
        lon_branch,
        lat_courant,
        lat_branch,
        mixing,
        prior_cov,
        region_map,
        region_order.reshape(regions // 128, 128),
        cosines,
    )
    adjoint, flux = pl.pallas_call(
        store,
        out_shape=(
            jax.ShapeDtypeStruct(field, f32),
            jax.ShapeDtypeStruct((steps, blk), f32),
        ),
        in_specs=[pl.BlockSpec(memory_space=pl.ANY)] * 2,
        out_specs=(pl.BlockSpec(memory_space=pl.ANY),) * 2,
        scratch_shapes=[pltpu.SemaphoreType.DMA((2,))],
    )(pltpu.with_memory_space_constraint(adjoint, pltpu.VMEM), pltpu.with_memory_space_constraint(flux, pltpu.VMEM))
    if width < blk:
        start = lax.rem(lax.axis_index("lat") * width, blk)
        flux = lax.dynamic_slice_in_dim(flux, start, width, 1)
    return adjoint, flux


def solution(mesh):
    four = P(None, None, "lon", "lat")
    placed = (
        P(None, "lon", "lat"),
        four,
        four,
        four,
        four,
        four,
        P("lon", "lat"),
        P(),
        P("lon", None, None),
    )
    return jax.shard_map(
        functools.partial(per_device, mesh.shape["lon"], mesh.shape["lat"]),
        mesh=mesh,
        in_specs=placed,
        out_specs=(P(None, "lon", "lat"), P(None, ("lon", "lat"))),
        check_vma=False,
    )
```

```python
import functools
import math

import jax
import jax.numpy as jnp
import numpy as np
from jax import lax
from jax.experimental import pallas as pl
from jax.experimental.pallas import tpu as pltpu
from jax.sharding import PartitionSpec as P

MESH = pl.DeviceIdType.MESH
OWN = 8


def face_weights(courant, branch):
    lean_part = courant * (0.5 * (1.0 - jnp.abs(courant)))
    one_part = jnp.where(branch == 1, lean_part, 0.0)
    two_part = jnp.where(branch == 2, lean_part, 0.0)
    donor = courant - one_part + two_part
    left = courant > 0.0
    return (
        jnp.where(left, -two_part, 0.0),
        jnp.where(left, donor, one_part),
        jnp.where(left, one_part, donor),
        jnp.where(left, 0.0, -two_part),
    )


def kernel(
    nlon,
    nlat,
    width,
    adj_h,
    lonc_h,
    lonb_h,
    latc_h,
    latb_h,
    mix_h,
    cov_h,
    rmap_h,
    order_h,
    cos_h,
    out_h,
    flux_h,
    out_ref,
    flux_ref,
    rmap_ref,
    order_ref,
    cos_ref,
    x_ref,
    mixv,
    latc,
    latb,
    lonc,
    lonb,
    covv,
    covh,
    covl,
    inv_ref,
    kin_ref,
    nr_ref,
    y_ref,
    ext,
    lw,
    pack,
    land_p,
    raw_rows,
    rows_a,
    far_a,
    rows_w,
    ids,
    beside,
    lat_c,
    lon_c,
    bext,
    hot,
    cht,
    amat,
    send_ref,
    land,
    sizer,
    local_sem,
    send_sem,
    recv_sem,
    all_sem,
):
    steps, levels, rows, lanes = latc.shape
    count = nlon * nlat
    my_lon, my_lat = lax.axis_index("lon"), lax.axis_index("lat")
    me = my_lon * nlat + my_lat
    blk = covv.shape[0]

    def place(device):
        return (device // nlat, lax.rem(device, nlat))

    barrier = pltpu.get_barrier_semaphore()

    def fetch(src, dst, slot):
        pltpu.make_async_copy(src, dst, local_sem.at[slot]).start()

    def drain(sem, count_rows):
        part = sizer.at[pl.ds(0, count_rows)]
        pltpu.make_async_copy(part, part, sem).wait()

    def got(slot, count_rows):
        drain(local_sem.at[slot], count_rows)

    far_first = jnp.where(my_lon >= nlon // 2, 1, 0)

    def greet(k, carry):
        device = far_first * k + (1 - far_first) * (count - 1 - k)

        @pl.when(device != me)
        def _():
            pl.semaphore_signal(barrier, inc=1, device_id=place(device), device_id_type=MESH)

        return carry

    lax.fori_loop(0, count // 4, greet, 0)
    fetch(mix_h.at[1], mixv.at[1], 0)
    fetch(adj_h, x_ref, 1)
    fetch(latc_h.at[1], latc.at[1], 2)
    fetch(latb_h.at[1], latb.at[1], 2)
    fetch(lonc_h.at[1], lonc.at[1], 3)
    fetch(lonb_h.at[1], lonb.at[1], 3)
    fetch(latc_h.at[0], latc.at[0], 4)
    fetch(latb_h.at[0], latb.at[0], 4)
    fetch(lonc_h.at[0], lonc.at[0], 4)
    fetch(lonb_h.at[0], lonb.at[0], 4)
    fetch(rmap_h, rmap_ref, 5)
    fetch(order_h, order_ref, 5)
    fetch(cos_h, cos_ref, 5)
    fetch(mix_h.at[0], mixv.at[0], 6)
    fetch(cov_h.at[(my_lat * width) // blk], covv, 7)
    lax.fori_loop(count // 4, count, greet, 0)

    lane = lax.broadcasted_iota(jnp.int32, (rows, lanes), 1)
    pair = lane // 2
    even = lax.rem(lane, 2) == 0
    zero = jnp.zeros((rows, lanes), jnp.float32)

    def roll(value, shift):
        return pltpu.roll(value, shift, 1)

    def remote(src, dst, send_slot, recv_slot, device):
        pltpu.make_async_remote_copy(
            src_ref=src,
            dst_ref=dst,
            send_sem=send_sem.at[send_slot],
            recv_sem=recv_sem.at[recv_slot],
            device_id=device,
            device_id_type=MESH,
        ).start()

    north = (my_lon, lax.rem(my_lat + 1, nlat))
    south = (my_lon, lax.rem(my_lat + nlat - 1, nlat))
    east = (lax.rem(my_lon + 1, nlon), my_lat)
    west = (lax.rem(my_lon + nlon - 1, nlon), my_lat)

    def coefficients(s):
        k = mixv[s, 0]
        inv = 1.0 / (1.0 + k)
        inv_ref[s, 0] = inv
        kin_ref[s, 0] = zero
        nr_ref[s, 0] = k * inv

        def body(level, ahead):
            lower, k = mixv[s, level - 1], mixv[s, level]
            inv = 1.0 / ((1.0 + k) + lower * (1.0 - ahead))
            inv_ref[s, level] = inv
            kin_ref[s, level] = lower * inv
            ahead = k * inv
            nr_ref[s, level] = ahead
            return ahead

        ahead = lax.fori_loop(1, levels - 1, body, k * inv, unroll=True)
        lower = mixv[s, levels - 2]
        inv = 1.0 / (1.0 + lower * (1.0 - ahead))
        inv_ref[s, levels - 1] = inv
        kin_ref[s, levels - 1] = lower * inv
        nr_ref[s, levels - 1] = zero

    def tail_head(value, level, tail, head):
        turned = roll(value, 2 * level + 2)
        return jnp.where(pair == level, turned, tail), jnp.where(pair == level + 1, turned, head)

    def solve(s):
        def up(level, carried):
            carried = x_ref[level] * inv_ref[s, level] + kin_ref[s, level] * carried
            y_ref[level] = carried
            return carried

        lax.fori_loop(0, levels, up, zero, unroll=True)

        def down(i, carry):
            value, tail, head = carry
            level = levels - 1 - i
            value = y_ref[level] + nr_ref[s, level] * value
            y_ref[level] = value
            raw_rows[0, pl.ds(2 * level, 2), :] = value[rows - 2 :]
            raw_rows[1, pl.ds(2 * level, 2), :] = value[:2]
            return (value,) + tail_head(value, level, tail, head)

        _, tail, head = lax.fori_loop(0, levels, down, (zero, zero, zero), unroll=True)
        head = roll(head, lanes - 2)
        for member, value in enumerate((tail, head)):
            pack[s, member, 0, OWN : OWN + rows] = value
            at = 2 * member
            rows_a[0, s, at : at + 2] = value[rows - 2 :]
            rows_a[1, s, at : at + 2] = value[:2]

    def pack_weights(s):
        def body(level, carry):
            ct, ch, bt, bh = carry
            ct, ch = tail_head(latc[s, level], level, ct, ch)
            both = (latc[s, level], latb[s, level].astype(jnp.float32))
            bt, bh = tail_head(both[1], level, bt, bh)
            for member in range(2):
                rows_w[0, s, member, pl.ds(2 * level, 2), :] = both[member][rows - 2 :]
                rows_w[1, s, member, pl.ds(2 * level, 2), :] = both[member][:2]
            return ct, ch, bt, bh

        ct, ch, bt, bh = lax.fori_loop(0, levels, body, (zero,) * 4, unroll=True)
        found = ((ct, bt), (roll(ch, lanes - 2), roll(bh, lanes - 2)))
        for end in range(2):
            for member in range(2):
                pack[s, end, 1 + member, OWN : OWN + rows] = found[end][member]
        for member in range(2):
            at = 4 + 2 * member
            rows_a[0, s, at : at + 2] = found[1][member][rows - 2 :]
            rows_a[1, s, at : at + 2] = found[1][member][:2]

    def lat_rows(s):
        for side in range(2):
            rows_a[side, s, 8:] = lat_pass(
                raw_rows[side], rows_w[side, s, 0], rows_w[side, s, 1]
            )

    def lat_pass(a, courant, branch):
        at = lax.broadcasted_iota(jnp.int32, a.shape, 1)
        m2, m1, m0, p1 = face_weights(courant, branch)
        jump = jnp.where(at >= 1, a - roll(a, 1), 0.0)
        out = a + m0 * jump + roll(m1 * jump, lanes - 1)
        out = out + roll(jnp.where(at >= 2, m2 * jump, 0.0), lanes - 2)
        return out + roll(jnp.where(at <= lanes - 2, p1 * jump, 0.0), 1)

    def lat_inner(s):
        def body(level, carry):
            out = lat_pass(y_ref[level], latc[s, level], latb[s, level])
            ext[s, level, OWN : OWN + rows] = out
            return carry

        lax.fori_loop(0, levels, body, 0, unroll=True)

    def edge_terms(s, at):
        count_rows = at.stop - at.start
        lane = lax.broadcasted_iota(jnp.int32, (count_rows, lanes), 1)
        even = lax.rem(lane, 2) == 0
        tail, head = pack[s, 0, 0, at], pack[s, 1, 0, at]
        before, after = land_p[s, 0, 0, at], land_p[s, 1, 0, at]
        m2_after, m1_after, _, _ = face_weights(land_p[s, 1, 1, at], land_p[s, 1, 2, at])
        _, _, m0_head, p1_head = face_weights(pack[s, 1, 1, at], pack[s, 1, 2, at])
        _, _, _, p1_before = face_weights(land_p[s, 0, 1, at], land_p[s, 0, 2, at])
        jump = after - jnp.where(even, roll(tail, lanes - 1), roll(after, 1))
        top = m2_after * jump + roll(jnp.where(even, m1_after * jump, 0.0), 1)
        top = jnp.where(my_lat < nlat - 1, top, 0.0)
        jump = jnp.where(even, head - roll(before, lanes - 1), before - roll(before, 1))
        flux = jnp.where(even, p1_head, p1_before) * jump
        low = jnp.where(even, m0_head * jump + roll(flux, lanes - 1), roll(flux, 1))
        low = roll(jnp.where(my_lat > 0, low, 0.0), 2)
        first = lax.rem(lane, 4) < 2
        both = (jnp.where(first, top, low), jnp.where(first, low, top))
        edge = jnp.logical_or(lane < 2, lane >= lanes - 2)

        def at_level(level):
            return jnp.where(edge, roll(both[level % 2], lanes - 2 - 2 * level), 0.0)

        return at_level

    def own_edges(s):
        terms = edge_terms(s, slice(OWN, OWN + rows))
        for level in range(levels):
            ext[s, level, OWN : OWN + rows] += terms(level)

    def far_terms(s):
        for side, where in enumerate((slice(OWN - 2, OWN), slice(OWN + rows, OWN + rows + 2))):
            for member in range(2):
                pack[s, member, 0, where] = far_a[side, s, 2 * member : 2 * member + 2]
                far = 4 + 2 * member
                pack[s, 1, 1 + member, where] = far_a[side, s, far : far + 2]
        return edge_terms(s, slice(0, OWN)), edge_terms(s, slice(OWN + rows, 2 * OWN + rows))

    def edges_and_lon(s, target, terms, part):
        end = OWN + rows
        for level in range(*part):
            two = slice(8 + 2 * level, 10 + 2 * level)
            ext[s, level, OWN - 2 : OWN] = far_a[0, s, two] + terms[0](level)[OWN - 2 :]
            ext[s, level, end : end + 2] = far_a[1, s, two] + terms[1](level)[:2]
        for level in range(*part):
            target[level] = lon_level(s, level)

    def lon_own_weights(s):
        def body(level, carry):
            found = face_weights(
                lonc[s, level], lonb[s, level]
            )
            for member in range(4):
                lw[s, member, level, OWN : OWN + rows] = found[member]
            return carry

        lax.fori_loop(0, levels, body, 0, unroll=True)

    def lon_level(s, level):
        a = [ext[s, level, OWN + k : OWN + k + rows] for k in range(-2, 3)]
        w = [
            lw[s, member, level, OWN + 2 - member : OWN + 2 - member + rows]
            for member in range(4)
        ]
        out = a[2] + w[0] * (a[4] - a[3]) + w[1] * (a[3] - a[2])
        return out + w[2] * (a[2] - a[1]) + w[3] * (a[1] - a[0])

    def send_lon(s, part, slot):
        end = OWN + rows
        for member, src, dst, size, device in (
            (0, OWN, end, 2, west),
            (1, OWN, end, 1, west),
            (3, end - 1, OWN - 1, 1, east),
        ):
            at = pl.ds(part[0], part[1] - part[0])
            remote(
                lw.at[s, member, at, pl.ds(src, size), :],
                lw.at[s, member, at, pl.ds(dst, size), :],
                0,
                slot,
                device,
            )

    def find_slots():
        order = order_ref[...]
        table = jnp.concatenate([order // blk, lax.rem(order, blk)], axis=0)
        table = table.astype(jnp.float32).astype(jnp.bfloat16)
        high = order.shape[0]
        down = lax.broadcasted_iota(jnp.int32, (lanes, lanes), 0)
        row_of = lax.broadcasted_iota(jnp.int32, (high, lanes), 0)
        for i in range(rows):
            region = rmap_ref[i : i + 1, :]
            hit = jnp.where(down == lax.rem(region, 128), 1.0, 0.0).astype(jnp.bfloat16)
            found = jnp.dot(table, hit, preferred_element_type=jnp.float32)
            both = found[:high] * float(blk) + found[high:]
            both = jnp.where(row_of == region // 128, both, 0.0)
            ids[2, OWN + i : OWN + i + 1] = jnp.sum(both, axis=0, keepdims=True)

    def spread(i, slot):
        groups = hot.shape[0] // 2
        slot = slot.astype(jnp.int32)
        high = lax.broadcasted_iota(jnp.int32, (2 * groups, lanes), 0) // 2
        low = lax.broadcasted_iota(jnp.int32, (blk, lanes), 0)
        at = slice(i * lanes, (i + 1) * lanes)
        hot[:, at] = jnp.where(high == slot // blk, 1.0, 0.0).astype(jnp.bfloat16)
        cht[:, at] = jnp.where(low == lax.rem(slot, blk), 1.0, 0.0).astype(jnp.bfloat16)

    def regions(pushed, side, later):
        tile, many = 16, hot.shape[0]
        step0 = lax.rem(lax.broadcasted_iota(jnp.int32, (tile, lanes), 0), 2) == 0
        for i in range(rows + 5):
            here = slice(i * lanes, (i + 1) * lanes)
            first = pushed[i : i + 1] if i < rows + 4 else side
            second = later[i - 2 : i - 1] if 2 <= i < rows + 2 else jnp.zeros_like(first)
            value = jnp.where(
                step0, jnp.broadcast_to(first, (tile, lanes)), jnp.broadcast_to(second, (tile, lanes))
            )
            coarse = value.astype(jnp.bfloat16)
            fine = (value - coarse.astype(jnp.float32)).astype(jnp.bfloat16)
            for part, piece in enumerate((coarse, fine)):
                for at in range(0, many, tile):
                    amat[part * many + at : part * many + at + tile, here] = (
                        hot[at : at + tile, here] * piece
                    )
        sums = lax.dot_general(
            amat[...], cht[...], (((1,), (1,)), ((), ())), preferred_element_type=jnp.float32
        )
        sums = sums[:many] + sums[many:]
        for group in range(many // 2):
            send_ref[group] = sums[2 * group : 2 * group + 2]

    tall_rows = rows + 2 * OWN
    few = slice(OWN - 2, OWN + rows + 6)
    has_north, has_south = my_lat < nlat - 1, my_lat > 0

    def push_lat():
        courant = jnp.where(jnp.logical_and(lane == 0, my_lat == 0), 0.0, latc[0, 0])
        m2, m1, m0, p1 = face_weights(courant, latb[0, 0])
        north_c = jnp.where(has_north, beside[1, 3, OWN : OWN + rows], 0.0)
        n2, n1, n0, np1 = face_weights(north_c, beside[1, 4, OWN : OWN + rows])
        ahead1 = jnp.where(lane == lanes - 1, roll(n1, lanes - 1), roll(m1, lanes - 1))
        round2 = roll(m2, lanes - 2)
        ahead2 = jnp.where(lane >= lanes - 2, roll(n2, lanes - 2), round2)
        behind = roll(p1, 1)
        lat_c[0, 0] = 1.0 - ahead1 + m0
        lat_c[0, 1] = jnp.where(lane <= lanes - 2, ahead1 - ahead2, 0.0)
        lat_c[0, 2] = jnp.where(lane <= lanes - 3, ahead2, 0.0)
        lat_c[0, 3] = jnp.where(lane >= 1, behind - m0, 0.0)
        lat_c[0, 4] = jnp.where(lane >= 2, -behind, 0.0)
        last, first = jnp.logical_and(lane == lanes - 1, has_south), jnp.logical_and(lane == 0, has_north)
        lat_c[1, 1] = jnp.where(last, roll(m1, lanes - 1) - round2, 0.0)
        lat_c[1, 2] = jnp.where(jnp.logical_and(lane >= lanes - 2, has_south), round2, 0.0)
        lat_c[1, 3] = jnp.where(first, behind - n0, 0.0)
        second = jnp.logical_and(lane == 1, has_north)
        lat_c[1, 4] = jnp.where(first, -behind, jnp.where(second, -roll(np1, 1), 0.0))

    def push_lon(side):
        down = lax.broadcasted_iota(jnp.int32, (tall_rows, lanes), 0)
        across = lax.broadcasted_iota(jnp.int32, (tall_rows, lanes), 1)
        faces = jnp.logical_and(down >= OWN, down <= OWN + rows)
        here, south_of = cos_ref[my_lat], cos_ref[lax.rem(my_lat + nlat - 1, nlat)]
        north_of = cos_ref[lax.rem(my_lat + 1, nlat)]
        across1 = lax.broadcasted_iota(jnp.int32, (1, lanes), 1)
        at_north = jnp.logical_and(across < 2, has_north)
        at_south = jnp.logical_and(across >= lanes - 2, has_south)
        if side == 0:
            courant, branch, cosine = ids[0], ids[1], here
        else:
            courant, branch = (
                jnp.where(at_north, beside[1, m], jnp.where(at_south, beside[0, m], 0.0))
                for m in range(2)
            )
            cosine = jnp.where(across1 < 2, north_of, south_of)
        m2, m1, m0, p1 = face_weights(jnp.where(faces, courant, 0.0), branch)
        ahead1 = pltpu.roll(m1, tall_rows - 1, 0)
        ahead2 = pltpu.roll(m2, tall_rows - 2, 0)
        behind = pltpu.roll(p1, 1, 0)
        found = (1.0 - ahead1 + m0, ahead1 - ahead2, ahead2, behind - m0, -behind)
        for k, value in enumerate(found):
            lon_c[side, k] = value[few] * cosine

    def squeeze(value):
        return jnp.sum(pltpu.roll(value, 0, 1, stride=4, stride_axis=0), axis=0, keepdims=True)

    def side_slots():
        shape = (rows + 8, lanes)
        down = lax.broadcasted_iota(jnp.int32, shape, 0)
        across = lax.broadcasted_iota(jnp.int32, shape, 1)
        at_north = jnp.logical_and(across < 2, has_north)
        at_south = jnp.logical_and(across >= lanes - 2, has_south)
        side = jnp.where(at_north, beside[1, 2, few], jnp.where(at_south, beside[0, 2, few], 0.0))
        side = squeeze(jnp.where(down < rows + 4, side, 0.0))
        spread(rows + 4, side)

    def push_totals():
        a = y_ref[0]
        turned = (a, roll(a, lanes - 1), roll(a, lanes - 2), roll(a, 1), roll(a, 2))
        for side in range(2):
            value = lat_c[side, 1] * turned[1]
            for k in range(2, 5):
                value = value + lat_c[side, k] * turned[k]
            if side == 0:
                value = value + lat_c[0, 0] * a
            bext[side, OWN : OWN + rows] = value
        found = []
        for side in range(2):
            value = jnp.zeros((rows + 8, lanes), jnp.float32)
            for k, step in enumerate((0, 1, 2, -1, -2)):
                at = OWN - 2 + step
                value = value + lon_c[side, k] * bext[side, at : at + rows + 8]
            found.append(value)
        regions(found[0], squeeze(found[1]), x_ref[0] * cos_ref[my_lat])

    got(0, (levels - 1) * rows)
    coefficients(1)
    got(1, levels * rows)
    solve(1)
    got(2, 2 * levels * rows)
    pack_weights(1)
    lat_rows(1)
    got(3, 2 * levels * rows)
    lon_own_weights(1)
    got(4, 4 * levels * rows)
    got(5, rows + order_ref.shape[0] + nlat)
    ids[0, OWN : OWN + rows] = lonc[0, 0]
    ids[1, OWN : OWN + rows] = lonb[0, 0].astype(jnp.float32)
    ids[3, OWN : OWN + rows] = latc[0, 0]
    ids[4, OWN : OWN + rows] = latb[0, 0].astype(jnp.float32)
    find_slots()
    bext[...] = jnp.zeros_like(bext)
    pl.semaphore_wait(barrier, count - 1)

    turn = {1: lax.rem(my_lon + 1, nlon), -1: lax.rem(my_lon + nlon - 1, nlon)}
    own_rows, first, last_two = pl.ds(OWN, rows), pl.ds(OWN, 2), pl.ds(OWN + rows - 2, 2)
    low, high = pl.ds(OWN - 2, 2), pl.ds(OWN + rows, 2)

    toward = (north[1], south[1])
    send_if, recv_if = (has_north, has_south), (has_south, has_north)
    column_rows = rows + 4

    def send_columns(source, target, recv_base, diagonal):
        for end in range(2):

            @pl.when(send_if[end])
            def _():
                for lon, src, dst in (
                    ((turn[1], last_two, low), (turn[-1], first, high))
                    if diagonal
                    else ((my_lon, own_rows, own_rows),)
                ):
                    remote(
                        source(end, src),
                        target(end, dst),
                        1,
                        recv_base + (1 if diagonal else 0),
                        (lon, toward[end]),
                    )

    beside_count = jnp.where(has_north, 1, 0) + jnp.where(has_south, 1, 0)

    def drain_beside(sem, count_rows):
        for ends in (1, 2):

            @pl.when(beside_count == ends)
            def _():
                drain(sem, ends * count_rows)

    half = levels // 2
    parts = ((0, half), (half, levels))
    spans = (pl.ds(0, 8 + 2 * half), pl.ds(8 + 2 * half, 2 * (levels - half)))
    border = (2 * (8 + 2 * half), 4 * (levels - half))

    def send_border(s, part, slot):
        at = spans[part]
        remote(rows_a.at[0, s, at, :], far_a.at[0, s, at, :], 0, slot, east)
        remote(rows_a.at[1, s, at, :], far_a.at[1, s, at, :], 0, slot, west)

    border_rows = sum(border)
    lon_rows = 4 * levels

    def group_of(device):
        return (device * width) // blk

    def scatter(k, carry):
        device = lax.rem(me + k, count)
        pltpu.make_async_remote_copy(
            src_ref=send_ref.at[group_of(device)],
            dst_ref=land.at[me],
            send_sem=all_sem.at[0],
            recv_sem=all_sem.at[1],
            device_id=place(device),
            device_id_type=MESH,
        ).start()
        return carry

    three = pl.ds(0, 3)

    def send_packs(diagonal):
        send_columns(
            lambda end, at: pack.at[1, end, :, at, :],
            lambda end, at: land_p.at[1, end, :, at, :],
            5,
            diagonal,
        )
        if diagonal:
            send_columns(
                lambda end, at: ids.at[three, at, :],
                lambda end, at: beside.at[end, three, at, :],
                7,
                True,
            )
        else:
            send_columns(
                lambda end, at: ids.at[:, at, :], lambda end, at: beside.at[end, :, at, :], 7, False
            )

    send_packs(True)
    remote(ids.at[three, last_two, :], ids.at[three, low, :], 0, 4, east)
    remote(ids.at[three, first, :], ids.at[three, high, :], 0, 4, west)
    for part, slot in ((0, 1), (1, 3)):
        send_border(1, part, slot)
        if part == 0:
            send_packs(False)
        send_lon(1, parts[part], slot)
    lat_inner(1)
    got(6, (levels - 1) * rows)
    coefficients(0)
    lon_own_weights(0)
    send_lon(0, (0, levels), 0)
    pack_weights(0)
    for diagonal in (True, False):
        send_columns(
            lambda end, at: pack.at[0, end, 1:3, at, :],
            lambda end, at: land_p.at[0, end, 1:3, at, :],
            9,
            diagonal,
        )
    for i in range(rows):
        spread(2 + i, ids[2, OWN + i : OWN + i + 1])
    drain_beside(recv_sem.at[5], 3 * rows)
    own_edges(1)
    drain_beside(recv_sem.at[7], 5 * rows)
    push_lat()
    drain(recv_sem.at[4], 12)
    push_lon(0)
    for i in (0, 1, rows + 2, rows + 3):
        spread(i, ids[2, OWN - 2 + i : OWN - 1 + i])
    drain_beside(recv_sem.at[8], 12)
    push_lon(1)
    side_slots()
    drain_beside(recv_sem.at[6], 12)
    for part, slot in ((0, 1), (1, 3)):
        drain(recv_sem.at[slot], border[part] + 4 * (parts[part][1] - parts[part][0]))
        if part == 0:
            terms = far_terms(1)
        edges_and_lon(1, x_ref, terms, parts[part])
    solve(0)
    lat_rows(0)
    for diagonal in (True, False):
        send_columns(
            lambda end, at: pack.at[0, end, 0, at, :],
            lambda end, at: land_p.at[0, end, 0, at, :],
            9,
            diagonal,
        )
    send_border(0, 0, 2)
    send_border(0, 1, 11)
    push_totals()
    lax.fori_loop(1, count, scatter, 0)
    land[me] = send_ref[group_of(me)]
    lat_inner(0)
    got(7, blk * blk // lanes)
    covh[...] = covv[...].astype(jnp.bfloat16)
    covl[...] = (covv[...] - covh[...].astype(jnp.float32)).astype(jnp.bfloat16)
    drain(recv_sem.at[0], lon_rows)
    drain_beside(recv_sem.at[9], 3 * rows)
    own_edges(0)
    drain_beside(recv_sem.at[10], 12)
    for part, slot in ((0, 2), (1, 11)):
        drain(recv_sem.at[slot], border[part])
        if part == 0:
            terms = far_terms(0)
        edges_and_lon(0, out_ref, terms, parts[part])
    fetch(out_ref, out_h, 8)
    drain(send_sem.at[0], 2 * (border_rows + lon_rows) + 12)
    drain_beside(send_sem.at[1], 9 * column_rows + 2 * rows)
    every = land.at[pl.ds(0, count - 1)]
    pltpu.make_async_copy(every, every, all_sem.at[0]).wait()
    pltpu.make_async_copy(every, every, all_sem.at[1]).wait()
    totals = jnp.sum(land[...], axis=0)
    coarse = totals.astype(jnp.bfloat16).astype(jnp.float32)
    both = jnp.concatenate([coarse, totals - coarse, jnp.zeros((12, blk), jnp.float32)], axis=0)
    both = both.astype(jnp.bfloat16)
    found = jnp.dot(both, covh[...], preferred_element_type=jnp.float32)
    found = found + jnp.dot(both, covl[...], preferred_element_type=jnp.float32)
    flux_ref[...] = found[:2] + found[2:4]
    fetch(flux_ref, flux_h, 8)
    got(8, levels * rows + steps * blk // lanes)


def store(adjoint_v, flux_v, adjoint_h, flux_h, sem):
    copies = (
        pltpu.make_async_copy(adjoint_v, adjoint_h, sem.at[0]),
        pltpu.make_async_copy(flux_v, flux_h, sem.at[1]),
    )
    for copy in copies:
        copy.start()
    for copy in copies:
        copy.wait()


def per_device(
    nlon,
    nlat,
    adjoint_final,
    lon_courant,
    lon_branch,
    lat_courant,
    lat_branch,
    mixing,
    region_map,
    region_order,
    prior_cov,
):
    steps, levels, rows, lanes = lon_courant.shape
    regions = region_order.shape[0]
    blk = prior_cov.shape[1]
    width = regions // (nlon * nlat)
    lat_total = lanes * nlat
    lat_index = np.arange(lat_total, dtype=np.float32)
    angle = (lat_index + np.float32(0.5)) * np.float32(math.pi / lat_total)
    cosines = np.cos((angle - np.float32(0.5 * math.pi)).astype(np.float32))
    cosines = jnp.asarray(cosines.astype(np.float32).reshape(nlat, 1, lanes))
    f32, i32, b16 = jnp.float32, jnp.int32, jnp.bfloat16
    field = (levels, rows, lanes)
    tall = (levels, rows + 2 * OWN, lanes)
    vm = pltpu.VMEM
    scratch = [
        vm(field, f32),
        vm((steps, blk), f32),
        vm((rows, lanes), i32),
        vm((regions // 128, 128), i32),
        vm((nlat, 1, lanes), f32),
        vm(field, f32),
        vm((steps, levels - 1, rows, lanes), f32),
        vm((steps,) + field, f32),
        vm((steps,) + field, i32),
        vm((steps,) + field, f32),
        vm((steps,) + field, i32),
        vm((blk, blk), f32),
        vm((blk, blk), b16),
        vm((blk, blk), b16),
        vm((steps,) + field, f32),
        vm((steps,) + field, f32),
        vm((steps,) + field, f32),
        vm(field, f32),
        vm((steps,) + tall, f32),
        vm((steps, 4) + tall, f32),
        vm((steps, 2, 3, rows + 2 * OWN, lanes), f32),
        vm((steps, 2, 3, rows + 2 * OWN, lanes), f32),
        vm((2, 2 * levels, lanes), f32),
        vm((2, steps, 2 * levels + 8, lanes), f32),
        vm((2, steps, 2 * levels + 8, lanes), f32),
        vm((2, steps, 2, 2 * levels, lanes), f32),
        vm((5, rows + 2 * OWN, lanes), f32),
        vm((2, 5, rows + 2 * OWN, lanes), f32),
        vm((2, 5, rows, lanes), f32),
        vm((2, 5, rows + 8, lanes), f32),
        vm((2, rows + 2 * OWN, lanes), f32),
        vm((2 * (regions // blk), (rows + 5) * lanes), b16),
        vm((blk, (rows + 5) * lanes), b16),
        vm((4 * (regions // blk), (rows + 5) * lanes), b16),
        vm((regions // blk, 2, blk), f32),
        vm((nlon * nlat, 2, blk), f32),
        vm((4 * levels * rows, lanes), f32),
        pltpu.SemaphoreType.DMA((9,)),
        pltpu.SemaphoreType.DMA((2,)),
        pltpu.SemaphoreType.DMA((12,)),
        pltpu.SemaphoreType.DMA((2,)),
    ]
    adjoint, flux = pl.pallas_call(
        functools.partial(kernel, nlon, nlat, width),
        out_shape=(
            pltpu.VMEM(field, f32),
            pltpu.VMEM((steps, blk), f32),
        ),
        in_specs=[pl.BlockSpec(memory_space=pltpu.HBM)] * 10,
        out_specs=(
            pl.BlockSpec(memory_space=pl.ANY),
            pl.BlockSpec(memory_space=pl.ANY),
        ),
        scratch_shapes=scratch,
        compiler_params=pltpu.CompilerParams(
            collective_id=0, has_side_effects=True, vmem_limit_bytes=61 * 1024 * 1024
        ),
    )(
        adjoint_final,
        lon_courant,
        lon_branch,
        lat_courant,
        lat_branch,
        mixing,
        prior_cov,
        region_map,
        region_order.reshape(regions // 128, 128),
        cosines,
    )
    adjoint, flux = pl.pallas_call(
        store,
        out_shape=(
            jax.ShapeDtypeStruct(field, f32),
            jax.ShapeDtypeStruct((steps, blk), f32),
        ),
        in_specs=[pl.BlockSpec(memory_space=pl.ANY)] * 2,
        out_specs=(pl.BlockSpec(memory_space=pl.ANY),) * 2,
        scratch_shapes=[pltpu.SemaphoreType.DMA((2,))],
    )(pltpu.with_memory_space_constraint(adjoint, pltpu.VMEM), pltpu.with_memory_space_constraint(flux, pltpu.VMEM))
    if width < blk:
        start = lax.rem(lax.axis_index("lat") * width, blk)
        flux = lax.dynamic_slice_in_dim(flux, start, width, 1)
    return adjoint, flux


def solution(mesh):
    four = P(None, None, "lon", "lat")
    placed = (
        P(None, "lon", "lat"),
        four,
        four,
        four,
        four,
        four,
        P("lon", "lat"),
        P(),
        P("lon", None, None),
    )
    return jax.shard_map(
        functools.partial(per_device, mesh.shape["lon"], mesh.shape["lat"]),
        mesh=mesh,
        in_specs=placed,
        out_specs=(P(None, "lon", "lat"), P(None, ("lon", "lat"))),
        check_vma=False,
    )
```

```python
import functools
import math

import jax
import jax.numpy as jnp
import numpy as np
from jax import lax
from jax.experimental import pallas as pl
from jax.experimental.pallas import tpu as pltpu
from jax.sharding import PartitionSpec as P

MESH = pl.DeviceIdType.MESH
OWN = 8


def face_weights(courant, branch):
    lean_part = courant * (0.5 * (1.0 - jnp.abs(courant)))
    one_part = jnp.where(branch == 1, lean_part, 0.0)
    two_part = jnp.where(branch == 2, lean_part, 0.0)
    donor = courant - one_part + two_part
    left = courant > 0.0
    return (
        jnp.where(left, -two_part, 0.0),
        jnp.where(left, donor, one_part),
        jnp.where(left, one_part, donor),
        jnp.where(left, 0.0, -two_part),
    )


def kernel(
    nlon,
    nlat,
    width,
    adj_h,
    lonc_h,
    lonb_h,
    latc_h,
    latb_h,
    mix_h,
    cov_h,
    rmap_h,
    order_h,
    cos_h,
    out_h,
    land,
    covv,
    out_ref,
    rmap_ref,
    order_ref,
    cos_ref,
    x_ref,
    mixv,
    latc,
    latb,
    lonc,
    lonb,
    inv_ref,
    kin_ref,
    nr_ref,
    join_ref,
    y_ref,
    ext,
    lw,
    pack,
    land_p,
    raw_rows,
    rows_a,
    far_a,
    rows_w,
    rows_c,
    delta,
    ids,
    beside,
    lat_c,
    lon_c,
    bext,
    hot,
    cht,
    amat,
    send_ref,
    sizer,
    local_sem,
    send_sem,
    recv_sem,
    all_sem,
):
    steps, levels, rows, lanes = latc.shape
    count = nlon * nlat
    my_lon, my_lat = lax.axis_index("lon"), lax.axis_index("lat")
    me = my_lon * nlat + my_lat
    blk = covv.shape[0]

    def place(device):
        return (device // nlat, lax.rem(device, nlat))

    barrier = pltpu.get_barrier_semaphore()

    def fetch(src, dst, slot):
        pltpu.make_async_copy(src, dst, local_sem.at[slot]).start()

    def drain(sem, count_rows):
        part = sizer.at[pl.ds(0, count_rows)]
        pltpu.make_async_copy(part, part, sem).wait()

    def got(slot, count_rows):
        drain(local_sem.at[slot], count_rows)

    far_first = jnp.where(my_lon >= nlon // 2, 1, 0)

    def greet(k, carry):
        device = far_first * k + (1 - far_first) * (count - 1 - k)

        @pl.when(device != me)
        def _():
            pl.semaphore_signal(barrier, inc=1, device_id=place(device), device_id_type=MESH)

        return carry

    lax.fori_loop(0, count // 4, greet, 0)
    fetch(mix_h.at[1], mixv.at[1], 0)
    fetch(adj_h, x_ref, 1)
    fetch(latc_h.at[1], latc.at[1], 2)
    fetch(latb_h.at[1], latb.at[1], 2)
    fetch(lonc_h.at[1], lonc.at[1], 3)
    fetch(lonb_h.at[1], lonb.at[1], 3)
    fetch(latc_h.at[0], latc.at[0], 4)
    fetch(latb_h.at[0], latb.at[0], 4)
    fetch(lonc_h.at[0], lonc.at[0], 4)
    fetch(lonb_h.at[0], lonb.at[0], 4)
    fetch(rmap_h, rmap_ref, 5)
    fetch(order_h, order_ref, 5)
    fetch(cos_h, cos_ref, 5)
    fetch(mix_h.at[0], mixv.at[0], 6)
    fetch(cov_h.at[(my_lat * width) // blk], covv, 7)
    lax.fori_loop(count // 4, count, greet, 0)

    lane = lax.broadcasted_iota(jnp.int32, (rows, lanes), 1)
    pair = lane // 2
    even = lax.rem(lane, 2) == 0
    zero = jnp.zeros((rows, lanes), jnp.float32)

    def roll(value, shift):
        return pltpu.roll(value, shift, 1)

    def remote(src, dst, send_slot, recv_slot, device):
        pltpu.make_async_remote_copy(
            src_ref=src,
            dst_ref=dst,
            send_sem=send_sem.at[send_slot],
            recv_sem=recv_sem.at[recv_slot],
            device_id=device,
            device_id_type=MESH,
        ).start()

    north = (my_lon, lax.rem(my_lat + 1, nlat))
    south = (my_lon, lax.rem(my_lat + nlat - 1, nlat))
    east = (lax.rem(my_lon + 1, nlon), my_lat)
    west = (lax.rem(my_lon + nlon - 1, nlon), my_lat)

    meet = levels // 2

    def coefficients(s):
        def sweep(order, before, after):
            ahead = None
            for level in order:
                inner, outer = before(level), after(level)
                if ahead is None:
                    inv = 1.0 / (1.0 + outer)
                    kin_ref[s, level] = zero
                else:
                    inv = 1.0 / ((1.0 + outer) + inner * (1.0 - ahead))
                    kin_ref[s, level] = inner * inv
                inv_ref[s, level] = inv
                ahead = outer * inv
                nr_ref[s, level] = ahead
            return ahead

        def below(level):
            return mixv[s, level - 1] if level > 0 else None

        def above(level):
            return mixv[s, level] if level < levels - 1 else None

        up = sweep(range(meet), below, above)
        down = sweep(range(levels - 1, meet - 1, -1), above, below)
        join_ref[s] = 1.0 / (1.0 - up * down)

    def tail_head(value, level, tail, head):
        turned = roll(value, 2 * level + 2)
        return jnp.where(pair == level, turned, tail), jnp.where(pair == level + 1, turned, head)

    def solve(s):
        def carry(level, carried):
            value = x_ref[level] * inv_ref[s, level]
            return value if carried is None else value + kin_ref[s, level] * carried

        up = down = None
        for i in range(levels - meet):
            if i < meet:
                up = carry(i, up)
                y_ref[i] = up
            level = levels - 1 - i
            down = carry(level, down)
            y_ref[level] = down
        tail = head = zero
        up_value = down_value = None
        for i in range(levels - meet):
            level = meet + i
            if i == 0:
                down_value = (down + nr_ref[s, level] * up) * join_ref[s]
            else:
                down_value = y_ref[level] + nr_ref[s, level] * down_value
            found = [(level, down_value)]
            if i < meet:
                level = meet - 1 - i
                if i == 0:
                    up_value = up + nr_ref[s, level] * down_value
                else:
                    up_value = y_ref[level] + nr_ref[s, level] * up_value
                found.append((level, up_value))
            for level, value in found:
                y_ref[level] = value
                raw_rows[0, pl.ds(2 * level, 2), :] = value[rows - 2 :]
                raw_rows[1, pl.ds(2 * level, 2), :] = value[:2]
                tail, head = tail_head(value, level, tail, head)
        head = roll(head, lanes - 2)
        for member, value in enumerate((tail, head)):
            pack[s, member, 0, OWN : OWN + rows] = value
            at = 2 * member
            rows_a[0, s, at : at + 2] = value[rows - 2 :]
            rows_a[1, s, at : at + 2] = value[:2]

    def pack_weights(s):
        def body(level, carry):
            ct, ch, bt, bh = carry
            ct, ch = tail_head(latc[s, level], level, ct, ch)
            both = (latc[s, level], latb[s, level].astype(jnp.float32))
            bt, bh = tail_head(both[1], level, bt, bh)
            for member in range(2):
                rows_w[0, s, member, pl.ds(2 * level, 2), :] = both[member][rows - 2 :]
                rows_w[1, s, member, pl.ds(2 * level, 2), :] = both[member][:2]
            return ct, ch, bt, bh

        ct, ch, bt, bh = lax.fori_loop(0, levels, body, (zero,) * 4, unroll=True)
        found = ((ct, bt), (roll(ch, lanes - 2), roll(bh, lanes - 2)))
        for end in range(2):
            for member in range(2):
                pack[s, end, 1 + member, OWN : OWN + rows] = found[end][member]
        for member in range(2):
            at = 4 + 2 * member
            rows_a[0, s, at : at + 2] = found[1][member][rows - 2 :]
            rows_a[1, s, at : at + 2] = found[1][member][:2]

    def row_weights(s):
        lane = lax.broadcasted_iota(jnp.int32, (2 * levels, lanes), 1)
        for side in range(2):
            m2, m1, m0, p1 = face_weights(rows_w[side, s, 0], rows_w[side, s, 1])
            ahead1 = jnp.where(lane <= lanes - 2, roll(m1, lanes - 1), 0.0)
            ahead2 = jnp.where(lane <= lanes - 3, roll(m2, lanes - 2), 0.0)
            here = jnp.where(lane >= 1, m0, 0.0)
            behind = jnp.where(lane >= 2, roll(p1, 1), 0.0)
            found = (1.0 - ahead1 + here, ahead1 - ahead2, ahead2, behind - here, -behind)
            for k, value in enumerate(found):
                rows_c[side, k] = value

    def lat_rows(s):
        for side in range(2):
            a = raw_rows[side]
            value = rows_c[side, 0] * a
            for k, turn in ((1, lanes - 1), (2, lanes - 2), (3, 1), (4, 2)):
                value = value + rows_c[side, k] * roll(a, turn)
            rows_a[side, s, 8:] = value

    def lat_pass(a, courant, branch):
        at = lax.broadcasted_iota(jnp.int32, a.shape, 1)
        m2, m1, m0, p1 = face_weights(courant, branch)
        jump = jnp.where(at >= 1, a - roll(a, 1), 0.0)
        out = a + m0 * jump + roll(m1 * jump, lanes - 1)
        out = out + roll(jnp.where(at >= 2, m2 * jump, 0.0), lanes - 2)
        return out + roll(jnp.where(at <= lanes - 2, p1 * jump, 0.0), 1)

    def lat_inner(s):
        def body(level, carry):
            out = lat_pass(y_ref[level], latc[s, level], latb[s, level])
            ext[s, level, OWN : OWN + rows] = out
            return carry

        lax.fori_loop(0, levels, body, 0, unroll=True)

    def edge_terms(s, at):
        count_rows = at.stop - at.start
        lane = lax.broadcasted_iota(jnp.int32, (count_rows, lanes), 1)
        even = lax.rem(lane, 2) == 0
        tail, head = pack[s, 0, 0, at], pack[s, 1, 0, at]
        before, after = land_p[s, 0, 0, at], land_p[s, 1, 0, at]
        m2_after, m1_after, _, _ = face_weights(land_p[s, 1, 1, at], land_p[s, 1, 2, at])
        _, _, m0_head, p1_head = face_weights(pack[s, 1, 1, at], pack[s, 1, 2, at])
        _, _, _, p1_before = face_weights(land_p[s, 0, 1, at], land_p[s, 0, 2, at])
        jump = after - jnp.where(even, roll(tail, lanes - 1), roll(after, 1))
        top_here = jnp.where(has_north, m2_after * jump, 0.0)
        top_next = jnp.where(jnp.logical_and(even, has_north), m1_after * jump, 0.0)
        jump = jnp.where(even, head - roll(before, lanes - 1), before - roll(before, 1))
        flux = jnp.where(has_south, jnp.where(even, p1_head, p1_before) * jump, 0.0)
        low_here = jnp.where(has_south, m0_head * jump, 0.0)
        edge = jnp.logical_or(lane < 2, lane >= lanes - 2)

        def turned_back(by):
            def turn(value, shift):
                shift = (shift - by) % lanes
                return roll(value, shift) if shift else value

            first = lax.rem(lane + by, 4) < 2
            evens = lax.rem(lane + by, 2) == 0
            top = turn(top_here, 0) + turn(top_next, 1)
            low = jnp.where(evens, turn(low_here, 2) + turn(flux, 1), turn(flux, 3))
            return jnp.where(first, top, low), jnp.where(first, low, top)

        return turned_back, edge

    def own_edges(s):
        turned_back, edge = edge_terms(s, slice(OWN, OWN + rows))
        both = turned_back(0)
        for level in range(levels):
            turned = roll(both[level % 2], lanes - 2 - 2 * level)
            ext[s, level, OWN : OWN + rows] += jnp.where(edge, turned, 0.0)

    def far_edges(s):
        end = OWN + rows
        for side, where in enumerate((slice(OWN - 2, OWN), slice(end, end + 2))):
            for member in range(2):
                pack[s, member, 0, where] = far_a[side, s, 2 * member : 2 * member + 2]
                far = 4 + 2 * member
                pack[s, 1, 1 + member, where] = far_a[side, s, far : far + 2]
        down = lax.broadcasted_iota(jnp.int32, (8, lanes), 0)
        for side, (at, row) in enumerate(((slice(0, OWN), OWN - 2), (slice(end, end + OWN), 0))):
            turned_back, edge = edge_terms(s, at)
            both = turned_back(0), turned_back(1)
            rows2 = [
                jnp.where(
                    lax.rem(down // 2 + levels - 1, 2) == 0,
                    jnp.broadcast_to(both[odd][0][row + odd : row + odd + 1], (8, lanes)),
                    jnp.broadcast_to(both[odd][1][row + odd : row + odd + 1], (8, lanes)),
                )
                for odd in range(2)
            ]
            tile = jnp.where(lax.rem(down, 2) == 0, rows2[0], rows2[1])
            for v in range((2 * levels + 7) // 8):
                turn = (8 * v - 2 * levels) % lanes
                late = turn > lanes - 8
                source = roll(tile, lanes // 2) if late else tile
                turn = turn - lanes // 2 if late else turn
                turned = pltpu.roll(source, turn, 1, stride=1, stride_axis=0)
                delta[side, 8 * v : 8 * v + 8] = jnp.where(edge, turned, 0.0)

    def edges_and_lon(s, target, part):
        end = OWN + rows
        for level in range(*part):
            far, two = slice(8 + 2 * level, 10 + 2 * level), slice(2 * (levels - 1 - level), 2 * (levels - level))
            ext[s, level, OWN - 2 : OWN] = far_a[0, s, far] + delta[0, two]
            ext[s, level, end : end + 2] = far_a[1, s, far] + delta[1, two]
        for level in range(*part):
            target[level] = lon_level(s, level)

    def lon_own_weights(s):
        def body(level, carry):
            found = face_weights(
                lonc[s, level], lonb[s, level]
            )
            for member in range(4):
                lw[s, member, level, OWN : OWN + rows] = found[member]
            return carry

        lax.fori_loop(0, levels, body, 0, unroll=True)

    def lon_level(s, level):
        a = [ext[s, level, OWN + k : OWN + k + rows] for k in range(-2, 3)]
        w = [
            lw[s, member, level, OWN + 2 - member : OWN + 2 - member + rows]
            for member in range(4)
        ]
        out = a[2] + w[0] * (a[4] - a[3]) + w[1] * (a[3] - a[2])
        return out + w[2] * (a[2] - a[1]) + w[3] * (a[1] - a[0])

    def send_lon(s, part, slot):
        end = OWN + rows
        for member, src, dst, size, device in (
            (0, OWN, end, 2, west),
            (1, OWN, end, 1, west),
            (3, end - 1, OWN - 1, 1, east),
        ):
            at = pl.ds(part[0], part[1] - part[0])
            remote(
                lw.at[s, member, at, pl.ds(src, size), :],
                lw.at[s, member, at, pl.ds(dst, size), :],
                0,
                slot,
                device,
            )

    def find_slots():
        order = order_ref[...]
        table = jnp.concatenate([order // blk, lax.rem(order, blk)], axis=0)
        table = table.astype(jnp.float32).astype(jnp.bfloat16)
        high = order.shape[0]
        down = lax.broadcasted_iota(jnp.int32, (lanes, lanes), 0)
        row_of = lax.broadcasted_iota(jnp.int32, (high, lanes), 0)
        for i in range(rows):
            region = rmap_ref[i : i + 1, :]
            hit = jnp.where(down == lax.rem(region, 128), 1.0, 0.0).astype(jnp.bfloat16)
            found = jnp.dot(table, hit, preferred_element_type=jnp.float32)
            both = found[:high] * float(blk) + found[high:]
            both = jnp.where(row_of == region // 128, both, 0.0)
            ids[2, OWN + i : OWN + i + 1] = jnp.sum(both, axis=0, keepdims=True)

    def spread(i, slot):
        groups = hot.shape[0] // 2
        slot = slot.astype(jnp.int32)
        high = lax.broadcasted_iota(jnp.int32, (2 * groups, lanes), 0) // 2
        low = lax.broadcasted_iota(jnp.int32, (blk, lanes), 0)
        at = slice(i * lanes, (i + 1) * lanes)
        hot[:, at] = jnp.where(high == slot // blk, 1.0, 0.0).astype(jnp.bfloat16)
        cht[:, at] = jnp.where(low == lax.rem(slot, blk), 1.0, 0.0).astype(jnp.bfloat16)

    def regions(pushed, side, later):
        tile, many = 16, hot.shape[0]
        step0 = lax.rem(lax.broadcasted_iota(jnp.int32, (tile, lanes), 0), 2) == 0
        for i in range(rows + 5):
            here = slice(i * lanes, (i + 1) * lanes)
            first = pushed[i : i + 1] if i < rows + 4 else side
            second = later[i - 2 : i - 1] if 2 <= i < rows + 2 else jnp.zeros_like(first)
            value = jnp.where(
                step0, jnp.broadcast_to(first, (tile, lanes)), jnp.broadcast_to(second, (tile, lanes))
            )
            coarse = value.astype(jnp.bfloat16)
            fine = (value - coarse.astype(jnp.float32)).astype(jnp.bfloat16)
            for part, piece in enumerate((coarse, fine)):
                for at in range(0, many, tile):
                    amat[part * many + at : part * many + at + tile, here] = (
                        hot[at : at + tile, here] * piece
                    )
        sums = lax.dot_general(
            amat[...], cht[...], (((1,), (1,)), ((), ())), preferred_element_type=jnp.float32
        )
        sums = sums[:many] + sums[many:]
        for group in range(many // 2):
            send_ref[group] = sums[2 * group : 2 * group + 2]

    tall_rows = rows + 2 * OWN
    few = slice(OWN - 2, OWN + rows + 6)
    has_north, has_south = my_lat < nlat - 1, my_lat > 0

    def push_lat():
        courant = jnp.where(jnp.logical_and(lane == 0, my_lat == 0), 0.0, latc[0, 0])
        m2, m1, m0, p1 = face_weights(courant, latb[0, 0])
        north_c = jnp.where(has_north, beside[1, 3, OWN : OWN + rows], 0.0)
        n2, n1, n0, np1 = face_weights(north_c, beside[1, 4, OWN : OWN + rows])
        ahead1 = jnp.where(lane == lanes - 1, roll(n1, lanes - 1), roll(m1, lanes - 1))
        round2 = roll(m2, lanes - 2)
        ahead2 = jnp.where(lane >= lanes - 2, roll(n2, lanes - 2), round2)
        behind = roll(p1, 1)
        lat_c[0, 0] = 1.0 - ahead1 + m0
        lat_c[0, 1] = jnp.where(lane <= lanes - 2, ahead1 - ahead2, 0.0)
        lat_c[0, 2] = jnp.where(lane <= lanes - 3, ahead2, 0.0)
        lat_c[0, 3] = jnp.where(lane >= 1, behind - m0, 0.0)
        lat_c[0, 4] = jnp.where(lane >= 2, -behind, 0.0)
        last, first = jnp.logical_and(lane == lanes - 1, has_south), jnp.logical_and(lane == 0, has_north)
        lat_c[1, 1] = jnp.where(last, roll(m1, lanes - 1) - round2, 0.0)
        lat_c[1, 2] = jnp.where(jnp.logical_and(lane >= lanes - 2, has_south), round2, 0.0)
        lat_c[1, 3] = jnp.where(first, behind - n0, 0.0)
        second = jnp.logical_and(lane == 1, has_north)
        lat_c[1, 4] = jnp.where(first, -behind, jnp.where(second, -roll(np1, 1), 0.0))

    def push_lon(side):
        down = lax.broadcasted_iota(jnp.int32, (tall_rows, lanes), 0)
        across = lax.broadcasted_iota(jnp.int32, (tall_rows, lanes), 1)
        faces = jnp.logical_and(down >= OWN, down <= OWN + rows)
        here, south_of = cos_ref[my_lat], cos_ref[lax.rem(my_lat + nlat - 1, nlat)]
        north_of = cos_ref[lax.rem(my_lat + 1, nlat)]
        across1 = lax.broadcasted_iota(jnp.int32, (1, lanes), 1)
        at_north = jnp.logical_and(across < 2, has_north)
        at_south = jnp.logical_and(across >= lanes - 2, has_south)
        if side == 0:
            courant, branch, cosine = ids[0], ids[1], here
        else:
            courant, branch = (
                jnp.where(at_north, beside[1, m], jnp.where(at_south, beside[0, m], 0.0))
                for m in range(2)
            )
            cosine = jnp.where(across1 < 2, north_of, south_of)
        m2, m1, m0, p1 = face_weights(jnp.where(faces, courant, 0.0), branch)
        ahead1 = pltpu.roll(m1, tall_rows - 1, 0)
        ahead2 = pltpu.roll(m2, tall_rows - 2, 0)
        behind = pltpu.roll(p1, 1, 0)
        found = (1.0 - ahead1 + m0, ahead1 - ahead2, ahead2, behind - m0, -behind)
        for k, value in enumerate(found):
            lon_c[side, k] = value[few] * cosine

    def squeeze(value):
        return jnp.sum(pltpu.roll(value, 0, 1, stride=4, stride_axis=0), axis=0, keepdims=True)

    def side_slots():
        shape = (rows + 8, lanes)
        down = lax.broadcasted_iota(jnp.int32, shape, 0)
        across = lax.broadcasted_iota(jnp.int32, shape, 1)
        at_north = jnp.logical_and(across < 2, has_north)
        at_south = jnp.logical_and(across >= lanes - 2, has_south)
        side = jnp.where(at_north, beside[1, 2, few], jnp.where(at_south, beside[0, 2, few], 0.0))
        side = squeeze(jnp.where(down < rows + 4, side, 0.0))
        spread(rows + 4, side)

    def push_totals():
        a = y_ref[0]
        turned = (a, roll(a, lanes - 1), roll(a, lanes - 2), roll(a, 1), roll(a, 2))
        for side in range(2):
            value = lat_c[side, 1] * turned[1]
            for k in range(2, 5):
                value = value + lat_c[side, k] * turned[k]
            if side == 0:
                value = value + lat_c[0, 0] * a
            bext[side, OWN : OWN + rows] = value
        found = []
        for side in range(2):
            value = jnp.zeros((rows + 8, lanes), jnp.float32)
            for k, step in enumerate((0, 1, 2, -1, -2)):
                at = OWN - 2 + step
                value = value + lon_c[side, k] * bext[side, at : at + rows + 8]
            found.append(value)
        regions(found[0], squeeze(found[1]), x_ref[0] * cos_ref[my_lat])

    got(0, (levels - 1) * rows)
    coefficients(1)
    got(1, levels * rows)
    solve(1)
    got(2, 2 * levels * rows)
    pack_weights(1)
    row_weights(1)
    lat_rows(1)
    got(3, 2 * levels * rows)
    lon_own_weights(1)
    got(4, 4 * levels * rows)
    got(5, rows + order_ref.shape[0] + nlat)
    ids[0, OWN : OWN + rows] = lonc[0, 0]
    ids[1, OWN : OWN + rows] = lonb[0, 0].astype(jnp.float32)
    ids[3, OWN : OWN + rows] = latc[0, 0]
    ids[4, OWN : OWN + rows] = latb[0, 0].astype(jnp.float32)
    find_slots()
    bext[...] = jnp.zeros_like(bext)
    pl.semaphore_wait(barrier, count - 1)

    turn = {1: lax.rem(my_lon + 1, nlon), -1: lax.rem(my_lon + nlon - 1, nlon)}
    own_rows, first, last_two = pl.ds(OWN, rows), pl.ds(OWN, 2), pl.ds(OWN + rows - 2, 2)
    low, high = pl.ds(OWN - 2, 2), pl.ds(OWN + rows, 2)

    toward = (north[1], south[1])
    send_if, recv_if = (has_north, has_south), (has_south, has_north)
    column_rows = rows + 4

    def send_columns(source, target, recv_base, diagonal):
        for end in range(2):

            @pl.when(send_if[end])
            def _():
                for lon, src, dst in (
                    ((turn[1], last_two, low), (turn[-1], first, high))
                    if diagonal
                    else ((my_lon, own_rows, own_rows),)
                ):
                    remote(
                        source(end, src),
                        target(end, dst),
                        1,
                        recv_base + (1 if diagonal else 0),
                        (lon, toward[end]),
                    )

    beside_count = jnp.where(has_north, 1, 0) + jnp.where(has_south, 1, 0)

    def drain_beside(sem, count_rows):
        for ends in (1, 2):

            @pl.when(beside_count == ends)
            def _():
                drain(sem, ends * count_rows)

    half = levels // 2
    parts = ((0, half), (half, levels))
    spans = (pl.ds(0, 8 + 2 * half), pl.ds(8 + 2 * half, 2 * (levels - half)))
    border = (2 * (8 + 2 * half), 4 * (levels - half))

    def send_border(s, part, slot):
        at = spans[part]
        remote(rows_a.at[0, s, at, :], far_a.at[0, s, at, :], 0, slot, east)
        remote(rows_a.at[1, s, at, :], far_a.at[1, s, at, :], 0, slot, west)

    border_rows = sum(border)
    lon_rows = 4 * levels

    def group_of(device):
        return (device * width) // blk

    def scatter(k, carry):
        device = lax.rem(me + k, count)
        pltpu.make_async_remote_copy(
            src_ref=send_ref.at[group_of(device)],
            dst_ref=land.at[me],
            send_sem=all_sem.at[0],
            recv_sem=all_sem.at[1],
            device_id=place(device),
            device_id_type=MESH,
        ).start()
        return carry

    three = pl.ds(0, 3)

    def send_packs(diagonal):
        send_columns(
            lambda end, at: pack.at[1, end, :, at, :],
            lambda end, at: land_p.at[1, end, :, at, :],
            5,
            diagonal,
        )
        if diagonal:
            send_columns(
                lambda end, at: ids.at[three, at, :],
                lambda end, at: beside.at[end, three, at, :],
                7,
                True,
            )
        else:
            send_columns(
                lambda end, at: ids.at[:, at, :], lambda end, at: beside.at[end, :, at, :], 7, False
            )

    send_packs(True)
    remote(ids.at[three, last_two, :], ids.at[three, low, :], 0, 4, east)
    remote(ids.at[three, first, :], ids.at[three, high, :], 0, 4, west)
    for part, slot in ((0, 1), (1, 3)):
        send_border(1, part, slot)
        if part == 0:
            send_packs(False)
        send_lon(1, parts[part], slot)
    lat_inner(1)
    got(6, (levels - 1) * rows)
    coefficients(0)
    lon_own_weights(0)
    send_lon(0, (0, levels), 0)
    pack_weights(0)
    row_weights(0)
    for diagonal in (True, False):
        send_columns(
            lambda end, at: pack.at[0, end, 1:3, at, :],
            lambda end, at: land_p.at[0, end, 1:3, at, :],
            9,
            diagonal,
        )
    for i in range(rows):
        spread(2 + i, ids[2, OWN + i : OWN + i + 1])
    drain_beside(recv_sem.at[5], 3 * rows)
    own_edges(1)
    drain_beside(recv_sem.at[7], 5 * rows)
    push_lat()
    drain(recv_sem.at[4], 12)
    push_lon(0)
    for i in (0, 1, rows + 2, rows + 3):
        spread(i, ids[2, OWN - 2 + i : OWN - 1 + i])
    drain_beside(recv_sem.at[8], 12)
    push_lon(1)
    side_slots()
    drain_beside(recv_sem.at[6], 12)
    for part, slot in ((0, 1), (1, 3)):
        drain(recv_sem.at[slot], border[part] + 4 * (parts[part][1] - parts[part][0]))
        if part == 0:
            far_edges(1)
        edges_and_lon(1, x_ref, parts[part])
    solve(0)
    lat_rows(0)
    for diagonal in (True, False):
        send_columns(
            lambda end, at: pack.at[0, end, 0, at, :],
            lambda end, at: land_p.at[0, end, 0, at, :],
            9,
            diagonal,
        )
    send_border(0, 0, 2)
    send_border(0, 1, 11)
    push_totals()
    lax.fori_loop(1, count, scatter, 0)
    fetch(send_ref.at[group_of(me)], land.at[me], 8)
    lat_inner(0)
    got(7, blk * blk // lanes)
    drain(recv_sem.at[0], lon_rows)
    drain_beside(recv_sem.at[9], 3 * rows)
    own_edges(0)
    drain_beside(recv_sem.at[10], 12)
    for part, slot in ((0, 2), (1, 11)):
        drain(recv_sem.at[slot], border[part])
        if part == 0:
            far_edges(0)
        edges_and_lon(0, out_ref, parts[part])
    fetch(out_ref, out_h, 8)
    got(8, levels * rows + 2 * blk // lanes)
    drain(send_sem.at[0], 2 * (border_rows + lon_rows) + 12)
    drain_beside(send_sem.at[1], 9 * column_rows + 2 * rows)
    every = land.at[pl.ds(0, count - 1)]
    pltpu.make_async_copy(every, every, all_sem.at[0]).wait()
    pltpu.make_async_copy(every, every, all_sem.at[1]).wait()


def finish(adjoint_v, land, cov, adjoint_h, flux_h, flux, sem):
    whole = pltpu.make_async_copy(adjoint_v, adjoint_h, sem.at[0])
    whole.start()
    totals = jnp.sum(land[...], axis=0)
    coarse = totals.astype(jnp.bfloat16).astype(jnp.float32)
    rest = jnp.zeros((12, totals.shape[1]), jnp.float32)
    both = jnp.concatenate([coarse, totals - coarse, rest], axis=0).astype(jnp.bfloat16)
    cov_high = cov[...].astype(jnp.bfloat16)
    cov_low = (cov[...] - cov_high.astype(jnp.float32)).astype(jnp.bfloat16)
    found = jnp.dot(both, cov_high, preferred_element_type=jnp.float32)
    found = found + jnp.dot(both, cov_low, preferred_element_type=jnp.float32)
    flux[...] = found[:2] + found[2:4]
    part = pltpu.make_async_copy(flux, flux_h, sem.at[1])
    part.start()
    part.wait()
    whole.wait()


def per_device(
    nlon,
    nlat,
    adjoint_final,
    lon_courant,
    lon_branch,
    lat_courant,
    lat_branch,
    mixing,
    region_map,
    region_order,
    prior_cov,
):
    steps, levels, rows, lanes = lon_courant.shape
    regions = region_order.shape[0]
    blk = prior_cov.shape[1]
    width = regions // (nlon * nlat)
    lat_total = lanes * nlat
    lat_index = np.arange(lat_total, dtype=np.float32)
    angle = (lat_index + np.float32(0.5)) * np.float32(math.pi / lat_total)
    cosines = np.cos((angle - np.float32(0.5 * math.pi)).astype(np.float32))
    cosines = jnp.asarray(cosines.astype(np.float32).reshape(nlat, 1, lanes))
    f32, i32, b16 = jnp.float32, jnp.int32, jnp.bfloat16
    field = (levels, rows, lanes)
    tall = (levels, rows + 2 * OWN, lanes)
    vm = pltpu.VMEM
    scratch = [
        vm(field, f32),
        vm((rows, lanes), i32),
        vm((regions // 128, 128), i32),
        vm((nlat, 1, lanes), f32),
        vm(field, f32),
        vm((steps, levels - 1, rows, lanes), f32),
        vm((steps,) + field, f32),
        vm((steps,) + field, i32),
        vm((steps,) + field, f32),
        vm((steps,) + field, i32),
        vm((steps,) + field, f32),
        vm((steps,) + field, f32),
        vm((steps,) + field, f32),
        vm((steps, rows, lanes), f32),
        vm(field, f32),
        vm((steps,) + tall, f32),
        vm((steps, 4) + tall, f32),
        vm((steps, 2, 3, rows + 2 * OWN, lanes), f32),
        vm((steps, 2, 3, rows + 2 * OWN, lanes), f32),
        vm((2, 2 * levels, lanes), f32),
        vm((2, steps, 2 * levels + 8, lanes), f32),
        vm((2, steps, 2 * levels + 8, lanes), f32),
        vm((2, steps, 2, 2 * levels, lanes), f32),
        vm((2, 5, 2 * levels, lanes), f32),
        vm((2, 2 * levels + 8, lanes), f32),
        vm((5, rows + 2 * OWN, lanes), f32),
        vm((2, 5, rows + 2 * OWN, lanes), f32),
        vm((2, 5, rows, lanes), f32),
        vm((2, 5, rows + 8, lanes), f32),
        vm((2, rows + 2 * OWN, lanes), f32),
        vm((2 * (regions // blk), (rows + 5) * lanes), b16),
        vm((blk, (rows + 5) * lanes), b16),
        vm((4 * (regions // blk), (rows + 5) * lanes), b16),
        vm((regions // blk, 2, blk), f32),
        vm((4 * levels * rows, lanes), f32),
        pltpu.SemaphoreType.DMA((9,)),
        pltpu.SemaphoreType.DMA((2,)),
        pltpu.SemaphoreType.DMA((12,)),
        pltpu.SemaphoreType.DMA((2,)),
    ]
    adjoint, landed, cov = pl.pallas_call(
        functools.partial(kernel, nlon, nlat, width),
        out_shape=(
            pltpu.VMEM(field, f32),
            pltpu.VMEM((nlon * nlat, steps, blk), f32),
            pltpu.VMEM((blk, blk), f32),
        ),
        in_specs=[pl.BlockSpec(memory_space=pltpu.HBM)] * 10,
        out_specs=(pl.BlockSpec(memory_space=pl.ANY),) * 3,
        scratch_shapes=scratch,
        compiler_params=pltpu.CompilerParams(
            collective_id=0, has_side_effects=True, vmem_limit_bytes=61 * 1024 * 1024
        ),
    )(
        adjoint_final,
        lon_courant,
        lon_branch,
        lat_courant,
        lat_branch,
        mixing,
        prior_cov,
        region_map,
        region_order.reshape(regions // 128, 128),
        cosines,
    )
    adjoint, flux = pl.pallas_call(
        finish,
        out_shape=(
            jax.ShapeDtypeStruct(field, f32),
            jax.ShapeDtypeStruct((steps, blk), f32),
        ),
        in_specs=[
            pl.BlockSpec(memory_space=pl.ANY),
            pl.BlockSpec(memory_space=pltpu.VMEM),
            pl.BlockSpec(memory_space=pltpu.VMEM),
        ],
        out_specs=(pl.BlockSpec(memory_space=pl.ANY),) * 2,
        scratch_shapes=[vm((steps, blk), f32), pltpu.SemaphoreType.DMA((2,))],
    )(*(pltpu.with_memory_space_constraint(x, pltpu.VMEM) for x in (adjoint, landed, cov)))
    if width < blk:
        start = lax.rem(lax.axis_index("lat") * width, blk)
        flux = lax.dynamic_slice_in_dim(flux, start, width, 1)
    return adjoint, flux


def solution(mesh):
    four = P(None, None, "lon", "lat")
    placed = (
        P(None, "lon", "lat"),
        four,
        four,
        four,
        four,
        four,
        P("lon", "lat"),
        P(),
        P("lon", None, None),
    )
    return jax.shard_map(
        functools.partial(per_device, mesh.shape["lon"], mesh.shape["lat"]),
        mesh=mesh,
        in_specs=placed,
        out_specs=(P(None, "lon", "lat"), P(None, ("lon", "lat"))),
        check_vma=False,
    )
```

```python
import functools
import math

import jax
import jax.numpy as jnp
import numpy as np
from jax import lax
from jax.experimental import pallas as pl
from jax.experimental.pallas import tpu as pltpu
from jax.sharding import PartitionSpec as P

MESH = pl.DeviceIdType.MESH
OWN = 8


def face_weights(courant, branch):
    lean_part = courant * (0.5 * (1.0 - jnp.abs(courant)))
    one_part = jnp.where(branch == 1, lean_part, 0.0)
    two_part = jnp.where(branch == 2, lean_part, 0.0)
    donor = courant - one_part + two_part
    left = courant > 0.0
    return (
        jnp.where(left, -two_part, 0.0),
        jnp.where(left, donor, one_part),
        jnp.where(left, one_part, donor),
        jnp.where(left, 0.0, -two_part),
    )


def kernel(
    nlon,
    nlat,
    width,
    adj_h,
    lonc_h,
    lonb_h,
    latc_h,
    latb_h,
    mix_h,
    cov_h,
    rmap_h,
    order_h,
    cos_h,
    out_h,
    land,
    covv,
    out_ref,
    rmap_ref,
    order_ref,
    cos_ref,
    x_ref,
    mixv,
    latc,
    latb,
    lonc,
    lonb,
    inv_ref,
    kin_ref,
    nr_ref,
    join_ref,
    y_ref,
    ext,
    lw,
    pack,
    land_p,
    raw_rows,
    rows_a,
    far_a,
    rows_w,
    rows_c,
    delta,
    ids,
    beside,
    lat_c,
    lon_c,
    bext,
    hot,
    cht,
    amat,
    send_ref,
    sizer,
    local_sem,
    send_sem,
    recv_sem,
    all_sem,
):
    steps, levels, rows, lanes = latc.shape
    count = nlon * nlat
    my_lon, my_lat = lax.axis_index("lon"), lax.axis_index("lat")
    me = my_lon * nlat + my_lat
    blk = covv.shape[0]

    def place(device):
        return (device // nlat, lax.rem(device, nlat))

    barrier = pltpu.get_barrier_semaphore()

    def fetch(src, dst, slot):
        pltpu.make_async_copy(src, dst, local_sem.at[slot]).start()

    def drain(sem, count_rows):
        part = sizer.at[pl.ds(0, count_rows)]
        pltpu.make_async_copy(part, part, sem).wait()

    def got(slot, count_rows):
        drain(local_sem.at[slot], count_rows)

    far_first = jnp.where(my_lon >= nlon // 2, 1, 0)

    def greet(k, carry):
        device = far_first * k + (1 - far_first) * (count - 1 - k)

        @pl.when(device != me)
        def _():
            pl.semaphore_signal(barrier, inc=1, device_id=place(device), device_id_type=MESH)

        return carry

    lax.fori_loop(0, count // 4, greet, 0)
    fetch(mix_h.at[1], mixv.at[1], 0)
    fetch(adj_h, x_ref, 1)
    fetch(latc_h.at[1], latc.at[1], 2)
    fetch(latb_h.at[1], latb.at[1], 2)
    fetch(lonc_h.at[1], lonc.at[1], 2)
    fetch(lonb_h.at[1], lonb.at[1], 2)
    fetch(latc_h.at[0], latc.at[0], 3)
    fetch(latb_h.at[0], latb.at[0], 3)
    fetch(lonc_h.at[0], lonc.at[0], 3)
    fetch(lonb_h.at[0], lonb.at[0], 3)
    fetch(rmap_h, rmap_ref, 3)
    fetch(order_h, order_ref, 3)
    fetch(cos_h, cos_ref, 3)
    fetch(mix_h.at[0], mixv.at[0], 4)
    fetch(cov_h.at[(my_lat * width) // blk], covv, 4)
    lax.fori_loop(count // 4, count, greet, 0)

    lane = lax.broadcasted_iota(jnp.int32, (rows, lanes), 1)
    pair = lane // 2
    even = lax.rem(lane, 2) == 0
    zero = jnp.zeros((rows, lanes), jnp.float32)

    def roll(value, shift):
        return pltpu.roll(value, shift, 1)

    def remote(src, dst, send_slot, recv_slot, device):
        pltpu.make_async_remote_copy(
            src_ref=src,
            dst_ref=dst,
            send_sem=send_sem.at[send_slot],
            recv_sem=recv_sem.at[recv_slot],
            device_id=device,
            device_id_type=MESH,
        ).start()

    north = (my_lon, lax.rem(my_lat + 1, nlat))
    south = (my_lon, lax.rem(my_lat + nlat - 1, nlat))
    east = (lax.rem(my_lon + 1, nlon), my_lat)
    west = (lax.rem(my_lon + nlon - 1, nlon), my_lat)

    meet = levels // 2

    def coefficients(s):
        def sweep(order, before, after):
            ahead = None
            for level in order:
                inner, outer = before(level), after(level)
                if ahead is None:
                    inv = 1.0 / (1.0 + outer)
                    kin_ref[s, level] = zero
                else:
                    inv = 1.0 / ((1.0 + outer) + inner * (1.0 - ahead))
                    kin_ref[s, level] = inner * inv
                inv_ref[s, level] = inv
                ahead = outer * inv
                nr_ref[s, level] = ahead
            return ahead

        def below(level):
            return mixv[s, level - 1] if level > 0 else None

        def above(level):
            return mixv[s, level] if level < levels - 1 else None

        up = sweep(range(meet), below, above)
        down = sweep(range(levels - 1, meet - 1, -1), above, below)
        join_ref[s] = 1.0 / (1.0 - up * down)

    def tail_head(value, level, tail, head):
        turned = roll(value, 2 * level + 2)
        return jnp.where(pair == level, turned, tail), jnp.where(pair == level + 1, turned, head)

    def solve(s):
        def carry(level, carried):
            value = x_ref[level] * inv_ref[s, level]
            return value if carried is None else value + kin_ref[s, level] * carried

        up = down = None
        for i in range(levels - meet):
            if i < meet:
                up = carry(i, up)
                y_ref[i] = up
            level = levels - 1 - i
            down = carry(level, down)
            y_ref[level] = down
        tail = head = zero
        up_value = down_value = None
        for i in range(levels - meet):
            level = meet + i
            if i == 0:
                down_value = (down + nr_ref[s, level] * up) * join_ref[s]
            else:
                down_value = y_ref[level] + nr_ref[s, level] * down_value
            found = [(level, down_value)]
            if i < meet:
                level = meet - 1 - i
                if i == 0:
                    up_value = up + nr_ref[s, level] * down_value
                else:
                    up_value = y_ref[level] + nr_ref[s, level] * up_value
                found.append((level, up_value))
            for level, value in found:
                y_ref[level] = value
                raw_rows[0, pl.ds(2 * level, 2), :] = value[rows - 2 :]
                raw_rows[1, pl.ds(2 * level, 2), :] = value[:2]
                tail, head = tail_head(value, level, tail, head)
        head = roll(head, lanes - 2)
        for member, value in enumerate((tail, head)):
            pack[s, member, 0, OWN : OWN + rows] = value
            at = 2 * member
            rows_a[0, s, at : at + 2] = value[rows - 2 :]
            rows_a[1, s, at : at + 2] = value[:2]

    def pack_weights(s):
        def body(level, carry):
            ct, ch, bt, bh = carry
            ct, ch = tail_head(latc[s, level], level, ct, ch)
            both = (latc[s, level], latb[s, level].astype(jnp.float32))
            bt, bh = tail_head(both[1], level, bt, bh)
            for member in range(2):
                rows_w[0, s, member, pl.ds(2 * level, 2), :] = both[member][rows - 2 :]
                rows_w[1, s, member, pl.ds(2 * level, 2), :] = both[member][:2]
            return ct, ch, bt, bh

        ct, ch, bt, bh = lax.fori_loop(0, levels, body, (zero,) * 4, unroll=True)
        found = ((ct, bt), (roll(ch, lanes - 2), roll(bh, lanes - 2)))
        for end in range(2):
            for member in range(2):
                pack[s, end, 1 + member, OWN : OWN + rows] = found[end][member]
        for member in range(2):
            at = 4 + 2 * member
            rows_a[0, s, at : at + 2] = found[1][member][rows - 2 :]
            rows_a[1, s, at : at + 2] = found[1][member][:2]

    def row_weights(s):
        lane = lax.broadcasted_iota(jnp.int32, (2 * levels, lanes), 1)
        for side in range(2):
            m2, m1, m0, p1 = face_weights(rows_w[side, s, 0], rows_w[side, s, 1])
            ahead1 = jnp.where(lane <= lanes - 2, roll(m1, lanes - 1), 0.0)
            ahead2 = jnp.where(lane <= lanes - 3, roll(m2, lanes - 2), 0.0)
            here = jnp.where(lane >= 1, m0, 0.0)
            behind = jnp.where(lane >= 2, roll(p1, 1), 0.0)
            found = (1.0 - ahead1 + here, ahead1 - ahead2, ahead2, behind - here, -behind)
            for k, value in enumerate(found):
                rows_c[side, k] = value

    def lat_rows(s):
        for side in range(2):
            a = raw_rows[side]
            value = rows_c[side, 0] * a
            for k, turn in ((1, lanes - 1), (2, lanes - 2), (3, 1), (4, 2)):
                value = value + rows_c[side, k] * roll(a, turn)
            rows_a[side, s, 8:] = value

    def lat_pass(a, courant, branch):
        at = lax.broadcasted_iota(jnp.int32, a.shape, 1)
        m2, m1, m0, p1 = face_weights(courant, branch)
        jump = jnp.where(at >= 1, a - roll(a, 1), 0.0)
        out = a + m0 * jump + roll(m1 * jump, lanes - 1)
        out = out + roll(jnp.where(at >= 2, m2 * jump, 0.0), lanes - 2)
        return out + roll(jnp.where(at <= lanes - 2, p1 * jump, 0.0), 1)

    def lat_inner(s):
        def body(level, carry):
            out = lat_pass(y_ref[level], latc[s, level], latb[s, level])
            ext[s, level, OWN : OWN + rows] = out
            return carry

        lax.fori_loop(0, levels, body, 0, unroll=True)

    def edge_terms(s, at):
        count_rows = at.stop - at.start
        lane = lax.broadcasted_iota(jnp.int32, (count_rows, lanes), 1)
        even = lax.rem(lane, 2) == 0
        tail, head = pack[s, 0, 0, at], pack[s, 1, 0, at]
        before, after = land_p[s, 0, 0, at], land_p[s, 1, 0, at]
        m2_after, m1_after, _, _ = face_weights(land_p[s, 1, 1, at], land_p[s, 1, 2, at])
        _, _, m0_head, p1_head = face_weights(pack[s, 1, 1, at], pack[s, 1, 2, at])
        _, _, _, p1_before = face_weights(land_p[s, 0, 1, at], land_p[s, 0, 2, at])
        jump = after - jnp.where(even, roll(tail, lanes - 1), roll(after, 1))
        top_here = jnp.where(has_north, m2_after * jump, 0.0)
        top_next = jnp.where(jnp.logical_and(even, has_north), m1_after * jump, 0.0)
        jump = jnp.where(even, head - roll(before, lanes - 1), before - roll(before, 1))
        flux = jnp.where(has_south, jnp.where(even, p1_head, p1_before) * jump, 0.0)
        low_here = jnp.where(has_south, m0_head * jump, 0.0)
        edge = jnp.logical_or(lane < 2, lane >= lanes - 2)

        def turned_back(by):
            def turn(value, shift):
                shift = (shift - by) % lanes
                return roll(value, shift) if shift else value

            first = lax.rem(lane + by, 4) < 2
            evens = lax.rem(lane + by, 2) == 0
            top = turn(top_here, 0) + turn(top_next, 1)
            low = jnp.where(evens, turn(low_here, 2) + turn(flux, 1), turn(flux, 3))
            return jnp.where(first, top, low), jnp.where(first, low, top)

        return turned_back, edge

    def own_edges(s):
        turned_back, edge = edge_terms(s, slice(OWN, OWN + rows))
        both = turned_back(0)
        for level in range(levels):
            turned = roll(both[level % 2], lanes - 2 - 2 * level)
            ext[s, level, OWN : OWN + rows] += jnp.where(edge, turned, 0.0)

    def far_edges(s):
        end = OWN + rows
        for side, where in enumerate((slice(OWN - 2, OWN), slice(end, end + 2))):
            for member in range(2):
                pack[s, member, 0, where] = far_a[side, s, 2 * member : 2 * member + 2]
                far = 4 + 2 * member
                pack[s, 1, 1 + member, where] = far_a[side, s, far : far + 2]
        down = lax.broadcasted_iota(jnp.int32, (8, lanes), 0)
        for side, (at, row) in enumerate(((slice(0, OWN), OWN - 2), (slice(end, end + OWN), 0))):
            turned_back, edge = edge_terms(s, at)
            both = turned_back(0), turned_back(1)
            rows2 = [
                jnp.where(
                    lax.rem(down // 2 + levels - 1, 2) == 0,
                    jnp.broadcast_to(both[odd][0][row + odd : row + odd + 1], (8, lanes)),
                    jnp.broadcast_to(both[odd][1][row + odd : row + odd + 1], (8, lanes)),
                )
                for odd in range(2)
            ]
            tile = jnp.where(lax.rem(down, 2) == 0, rows2[0], rows2[1])
            for v in range((2 * levels + 7) // 8):
                turn = (8 * v - 2 * levels) % lanes
                late = turn > lanes - 8
                source = roll(tile, lanes // 2) if late else tile
                turn = turn - lanes // 2 if late else turn
                turned = pltpu.roll(source, turn, 1, stride=1, stride_axis=0)
                delta[side, 8 * v : 8 * v + 8] = jnp.where(edge, turned, 0.0)

    def edges_and_lon(s, target, part):
        end = OWN + rows
        for level in range(*part):
            far, two = slice(8 + 2 * level, 10 + 2 * level), slice(2 * (levels - 1 - level), 2 * (levels - level))
            ext[s, level, OWN - 2 : OWN] = far_a[0, s, far] + delta[0, two]
            ext[s, level, end : end + 2] = far_a[1, s, far] + delta[1, two]
        for level in range(*part):
            target[level] = lon_level(s, level)

    def lon_own_weights(s):
        def body(level, carry):
            found = face_weights(
                lonc[s, level], lonb[s, level]
            )
            for member in range(4):
                lw[s, member, level, OWN : OWN + rows] = found[member]
            return carry

        lax.fori_loop(0, levels, body, 0, unroll=True)

    def lon_level(s, level):
        a = [ext[s, level, OWN + k : OWN + k + rows] for k in range(-2, 3)]
        w = [
            lw[s, member, level, OWN + 2 - member : OWN + 2 - member + rows]
            for member in range(4)
        ]
        out = a[2] + w[0] * (a[4] - a[3]) + w[1] * (a[3] - a[2])
        return out + w[2] * (a[2] - a[1]) + w[3] * (a[1] - a[0])

    def send_lon(s, part, slot):
        end = OWN + rows
        for member, src, dst, size, device in (
            (0, OWN, end, 2, west),
            (1, OWN, end, 1, west),
            (3, end - 1, OWN - 1, 1, east),
        ):
            at = pl.ds(part[0], part[1] - part[0])
            remote(
                lw.at[s, member, at, pl.ds(src, size), :],
                lw.at[s, member, at, pl.ds(dst, size), :],
                0,
                slot,
                device,
            )

    def find_slots():
        order = order_ref[...]
        table = jnp.concatenate([order // blk, lax.rem(order, blk)], axis=0)
        table = table.astype(jnp.float32).astype(jnp.bfloat16)
        high = order.shape[0]
        down = lax.broadcasted_iota(jnp.int32, (lanes, lanes), 0)
        row_of = lax.broadcasted_iota(jnp.int32, (high, lanes), 0)
        for i in range(rows):
            region = rmap_ref[i : i + 1, :]
            hit = jnp.where(down == lax.rem(region, 128), 1.0, 0.0).astype(jnp.bfloat16)
            found = jnp.dot(table, hit, preferred_element_type=jnp.float32)
            both = found[:high] * float(blk) + found[high:]
            both = jnp.where(row_of == region // 128, both, 0.0)
            ids[2, OWN + i : OWN + i + 1] = jnp.sum(both, axis=0, keepdims=True)

    def spread(i, slot):
        groups = hot.shape[0] // 2
        slot = slot.astype(jnp.int32)
        high = lax.broadcasted_iota(jnp.int32, (2 * groups, lanes), 0) // 2
        low = lax.broadcasted_iota(jnp.int32, (blk, lanes), 0)
        at = slice(i * lanes, (i + 1) * lanes)
        hot[:, at] = jnp.where(high == slot // blk, 1.0, 0.0).astype(jnp.bfloat16)
        cht[:, at] = jnp.where(low == lax.rem(slot, blk), 1.0, 0.0).astype(jnp.bfloat16)

    def regions(pushed, side, later):
        tile, many = 16, hot.shape[0]
        step0 = lax.rem(lax.broadcasted_iota(jnp.int32, (tile, lanes), 0), 2) == 0
        for i in range(rows + 5):
            here = slice(i * lanes, (i + 1) * lanes)
            first = pushed[i : i + 1] if i < rows + 4 else side
            second = later[i - 2 : i - 1] if 2 <= i < rows + 2 else jnp.zeros_like(first)
            value = jnp.where(
                step0, jnp.broadcast_to(first, (tile, lanes)), jnp.broadcast_to(second, (tile, lanes))
            )
            coarse = value.astype(jnp.bfloat16)
            fine = (value - coarse.astype(jnp.float32)).astype(jnp.bfloat16)
            for part, piece in enumerate((coarse, fine)):
                for at in range(0, many, tile):
                    amat[part * many + at : part * many + at + tile, here] = (
                        hot[at : at + tile, here] * piece
                    )
        sums = lax.dot_general(
            amat[...], cht[...], (((1,), (1,)), ((), ())), preferred_element_type=jnp.float32
        )
        sums = sums[:many] + sums[many:]
        for group in range(many // 2):
            send_ref[group] = sums[2 * group : 2 * group + 2]

    tall_rows = rows + 2 * OWN
    few = slice(OWN - 2, OWN + rows + 6)
    has_north, has_south = my_lat < nlat - 1, my_lat > 0

    def push_lat():
        courant = jnp.where(jnp.logical_and(lane == 0, my_lat == 0), 0.0, latc[0, 0])
        m2, m1, m0, p1 = face_weights(courant, latb[0, 0])
        north_c = jnp.where(has_north, beside[1, 3, OWN : OWN + rows], 0.0)
        n2, n1, n0, np1 = face_weights(north_c, beside[1, 4, OWN : OWN + rows])
        ahead1 = jnp.where(lane == lanes - 1, roll(n1, lanes - 1), roll(m1, lanes - 1))
        round2 = roll(m2, lanes - 2)
        ahead2 = jnp.where(lane >= lanes - 2, roll(n2, lanes - 2), round2)
        behind = roll(p1, 1)
        lat_c[0, 0] = 1.0 - ahead1 + m0
        lat_c[0, 1] = jnp.where(lane <= lanes - 2, ahead1 - ahead2, 0.0)
        lat_c[0, 2] = jnp.where(lane <= lanes - 3, ahead2, 0.0)
        lat_c[0, 3] = jnp.where(lane >= 1, behind - m0, 0.0)
        lat_c[0, 4] = jnp.where(lane >= 2, -behind, 0.0)
        last, first = jnp.logical_and(lane == lanes - 1, has_south), jnp.logical_and(lane == 0, has_north)
        lat_c[1, 1] = jnp.where(last, roll(m1, lanes - 1) - round2, 0.0)
        lat_c[1, 2] = jnp.where(jnp.logical_and(lane >= lanes - 2, has_south), round2, 0.0)
        lat_c[1, 3] = jnp.where(first, behind - n0, 0.0)
        second = jnp.logical_and(lane == 1, has_north)
        lat_c[1, 4] = jnp.where(first, -behind, jnp.where(second, -roll(np1, 1), 0.0))

    def push_lon(side):
        down = lax.broadcasted_iota(jnp.int32, (tall_rows, lanes), 0)
        across = lax.broadcasted_iota(jnp.int32, (tall_rows, lanes), 1)
        faces = jnp.logical_and(down >= OWN, down <= OWN + rows)
        here, south_of = cos_ref[my_lat], cos_ref[lax.rem(my_lat + nlat - 1, nlat)]
        north_of = cos_ref[lax.rem(my_lat + 1, nlat)]
        across1 = lax.broadcasted_iota(jnp.int32, (1, lanes), 1)
        at_north = jnp.logical_and(across < 2, has_north)
        at_south = jnp.logical_and(across >= lanes - 2, has_south)
        if side == 0:
            courant, branch, cosine = ids[0], ids[1], here
        else:
            courant, branch = (
                jnp.where(at_north, beside[1, m], jnp.where(at_south, beside[0, m], 0.0))
                for m in range(2)
            )
            cosine = jnp.where(across1 < 2, north_of, south_of)
        m2, m1, m0, p1 = face_weights(jnp.where(faces, courant, 0.0), branch)
        ahead1 = pltpu.roll(m1, tall_rows - 1, 0)
        ahead2 = pltpu.roll(m2, tall_rows - 2, 0)
        behind = pltpu.roll(p1, 1, 0)
        found = (1.0 - ahead1 + m0, ahead1 - ahead2, ahead2, behind - m0, -behind)
        for k, value in enumerate(found):
            lon_c[side, k] = value[few] * cosine

    def squeeze(value):
        return jnp.sum(pltpu.roll(value, 0, 1, stride=4, stride_axis=0), axis=0, keepdims=True)

    def side_slots():
        shape = (rows + 8, lanes)
        down = lax.broadcasted_iota(jnp.int32, shape, 0)
        across = lax.broadcasted_iota(jnp.int32, shape, 1)
        at_north = jnp.logical_and(across < 2, has_north)
        at_south = jnp.logical_and(across >= lanes - 2, has_south)
        side = jnp.where(at_north, beside[1, 2, few], jnp.where(at_south, beside[0, 2, few], 0.0))
        side = squeeze(jnp.where(down < rows + 4, side, 0.0))
        spread(rows + 4, side)

    def push_totals():
        a = y_ref[0]
        turned = (a, roll(a, lanes - 1), roll(a, lanes - 2), roll(a, 1), roll(a, 2))
        for side in range(2):
            value = lat_c[side, 1] * turned[1]
            for k in range(2, 5):
                value = value + lat_c[side, k] * turned[k]
            if side == 0:
                value = value + lat_c[0, 0] * a
            bext[side, OWN : OWN + rows] = value
        found = []
        for side in range(2):
            value = jnp.zeros((rows + 8, lanes), jnp.float32)
            for k, step in enumerate((0, 1, 2, -1, -2)):
                at = OWN - 2 + step
                value = value + lon_c[side, k] * bext[side, at : at + rows + 8]
            found.append(value)
        regions(found[0], squeeze(found[1]), x_ref[0] * cos_ref[my_lat])

    got(0, (levels - 1) * rows)
    coefficients(1)
    got(1, levels * rows)
    solve(1)
    got(2, 4 * levels * rows)
    pack_weights(1)
    row_weights(1)
    lat_rows(1)
    lon_own_weights(1)
    got(3, 4 * levels * rows + rows + order_ref.shape[0] + nlat)
    ids[0, OWN : OWN + rows] = lonc[0, 0]
    ids[1, OWN : OWN + rows] = lonb[0, 0].astype(jnp.float32)
    ids[3, OWN : OWN + rows] = latc[0, 0]
    ids[4, OWN : OWN + rows] = latb[0, 0].astype(jnp.float32)
    find_slots()
    bext[...] = jnp.zeros_like(bext)
    pl.semaphore_wait(barrier, count - 1)

    turn = {1: lax.rem(my_lon + 1, nlon), -1: lax.rem(my_lon + nlon - 1, nlon)}
    own_rows, first, last_two = pl.ds(OWN, rows), pl.ds(OWN, 2), pl.ds(OWN + rows - 2, 2)
    low, high = pl.ds(OWN - 2, 2), pl.ds(OWN + rows, 2)

    toward = (north[1], south[1])
    send_if, recv_if = (has_north, has_south), (has_south, has_north)
    column_rows = rows + 4

    def send_columns(source, target, recv_base, diagonal):
        for end in range(2):

            @pl.when(send_if[end])
            def _():
                for lon, src, dst in (
                    ((turn[1], last_two, low), (turn[-1], first, high))
                    if diagonal
                    else ((my_lon, own_rows, own_rows),)
                ):
                    remote(
                        source(end, src),
                        target(end, dst),
                        1,
                        recv_base + (1 if diagonal else 0),
                        (lon, toward[end]),
                    )

    beside_count = jnp.where(has_north, 1, 0) + jnp.where(has_south, 1, 0)

    def drain_beside(sem, count_rows):
        for ends in (1, 2):

            @pl.when(beside_count == ends)
            def _():
                drain(sem, ends * count_rows)

    half = levels // 2
    parts = ((0, half), (half, levels))
    spans = (pl.ds(0, 8 + 2 * half), pl.ds(8 + 2 * half, 2 * (levels - half)))
    border = (2 * (8 + 2 * half), 4 * (levels - half))

    def send_border(s, part, slot):
        at = spans[part]
        remote(rows_a.at[0, s, at, :], far_a.at[0, s, at, :], 0, slot, east)
        remote(rows_a.at[1, s, at, :], far_a.at[1, s, at, :], 0, slot, west)

    border_rows = sum(border)
    lon_rows = 4 * levels

    def group_of(device):
        return (device * width) // blk

    def scatter(k, carry):
        device = lax.rem(me + k, count)
        pltpu.make_async_remote_copy(
            src_ref=send_ref.at[group_of(device)],
            dst_ref=land.at[me],
            send_sem=all_sem.at[0],
            recv_sem=all_sem.at[1],
            device_id=place(device),
            device_id_type=MESH,
        ).start()
        return carry

    three = pl.ds(0, 3)

    def send_packs(diagonal):
        send_columns(
            lambda end, at: pack.at[1, end, :, at, :],
            lambda end, at: land_p.at[1, end, :, at, :],
            5,
            diagonal,
        )
        if diagonal:
            send_columns(
                lambda end, at: ids.at[three, at, :],
                lambda end, at: beside.at[end, three, at, :],
                5,
                True,
            )
        else:
            send_columns(
                lambda end, at: ids.at[:, at, :], lambda end, at: beside.at[end, :, at, :], 5, False
            )

    send_packs(True)
    remote(ids.at[three, last_two, :], ids.at[three, low, :], 0, 4, east)
    remote(ids.at[three, first, :], ids.at[three, high, :], 0, 4, west)
    send_packs(False)
    for part, slot in ((0, 1), (1, 3)):
        send_border(1, part, slot)
        send_lon(1, parts[part], slot)
    lat_inner(1)
    got(4, (levels - 1) * rows + blk * blk // lanes)
    coefficients(0)
    lon_own_weights(0)
    send_lon(0, (0, levels), 0)
    pack_weights(0)
    row_weights(0)
    for diagonal in (True, False):
        send_columns(
            lambda end, at: pack.at[0, end, 1:3, at, :],
            lambda end, at: land_p.at[0, end, 1:3, at, :],
            8,
            diagonal,
        )
    for i in range(rows):
        spread(2 + i, ids[2, OWN + i : OWN + i + 1])
    drain_beside(recv_sem.at[5], 8 * rows)
    own_edges(1)
    push_lat()
    drain(recv_sem.at[4], 12)
    push_lon(0)
    for i in (0, 1, rows + 2, rows + 3):
        spread(i, ids[2, OWN - 2 + i : OWN - 1 + i])
    drain_beside(recv_sem.at[6], 24)
    for part, slot in ((0, 1), (1, 3)):
        drain(recv_sem.at[slot], border[part] + 4 * (parts[part][1] - parts[part][0]))
        if part == 0:
            far_edges(1)
        else:
            push_lon(1)
            side_slots()
        edges_and_lon(1, x_ref, parts[part])
    solve(0)
    lat_rows(0)
    for diagonal in (True, False):
        send_columns(
            lambda end, at: pack.at[0, end, 0, at, :],
            lambda end, at: land_p.at[0, end, 0, at, :],
            8,
            diagonal,
        )
    send_border(0, 0, 2)
    send_border(0, 1, 7)
    push_totals()
    lax.fori_loop(1, count, scatter, 0)
    fetch(send_ref.at[group_of(me)], land.at[me], 5)
    lat_inner(0)
    drain(recv_sem.at[0], lon_rows)
    drain_beside(recv_sem.at[8], 3 * rows)
    own_edges(0)
    drain_beside(recv_sem.at[9], 12)
    for part, slot in ((0, 2), (1, 7)):
        drain(recv_sem.at[slot], border[part])
        if part == 0:
            far_edges(0)
        edges_and_lon(0, out_ref, parts[part])
    fetch(out_ref, out_h, 5)
    got(5, levels * rows + 2 * blk // lanes)
    drain(send_sem.at[0], 2 * (border_rows + lon_rows) + 12)
    drain_beside(send_sem.at[1], 9 * column_rows + 2 * rows)
    every = land.at[pl.ds(0, count - 1)]
    pltpu.make_async_copy(every, every, all_sem.at[0]).wait()
    pltpu.make_async_copy(every, every, all_sem.at[1]).wait()


def finish(adjoint_v, land, cov, adjoint_h, flux_h, flux, sem):
    whole = pltpu.make_async_copy(adjoint_v, adjoint_h, sem.at[0])
    whole.start()
    totals = jnp.sum(land[...], axis=0)
    coarse = totals.astype(jnp.bfloat16).astype(jnp.float32)
    rest = jnp.zeros((12, totals.shape[1]), jnp.float32)
    both = jnp.concatenate([coarse, totals - coarse, rest], axis=0).astype(jnp.bfloat16)
    cov_high = cov[...].astype(jnp.bfloat16)
    cov_low = (cov[...] - cov_high.astype(jnp.float32)).astype(jnp.bfloat16)
    found = jnp.dot(both, cov_high, preferred_element_type=jnp.float32)
    found = found + jnp.dot(both, cov_low, preferred_element_type=jnp.float32)
    flux[...] = found[:2] + found[2:4]
    part = pltpu.make_async_copy(flux, flux_h, sem.at[1])
    part.start()
    part.wait()
    whole.wait()


def per_device(
    nlon,
    nlat,
    adjoint_final,
    lon_courant,
    lon_branch,
    lat_courant,
    lat_branch,
    mixing,
    region_map,
    region_order,
    prior_cov,
):
    steps, levels, rows, lanes = lon_courant.shape
    regions = region_order.shape[0]
    blk = prior_cov.shape[1]
    width = regions // (nlon * nlat)
    lat_total = lanes * nlat
    lat_index = np.arange(lat_total, dtype=np.float32)
    angle = (lat_index + np.float32(0.5)) * np.float32(math.pi / lat_total)
    cosines = np.cos((angle - np.float32(0.5 * math.pi)).astype(np.float32))
    cosines = jnp.asarray(cosines.astype(np.float32).reshape(nlat, 1, lanes))
    f32, i32, b16 = jnp.float32, jnp.int32, jnp.bfloat16
    field = (levels, rows, lanes)
    tall = (levels, rows + 2 * OWN, lanes)
    vm = pltpu.VMEM
    scratch = [
        vm(field, f32),
        vm((rows, lanes), i32),
        vm((regions // 128, 128), i32),
        vm((nlat, 1, lanes), f32),
        vm(field, f32),
        vm((steps, levels - 1, rows, lanes), f32),
        vm((steps,) + field, f32),
        vm((steps,) + field, i32),
        vm((steps,) + field, f32),
        vm((steps,) + field, i32),
        vm((steps,) + field, f32),
        vm((steps,) + field, f32),
        vm((steps,) + field, f32),
        vm((steps, rows, lanes), f32),
        vm(field, f32),
        vm((steps,) + tall, f32),
        vm((steps, 4) + tall, f32),
        vm((steps, 2, 3, rows + 2 * OWN, lanes), f32),
        vm((steps, 2, 3, rows + 2 * OWN, lanes), f32),
        vm((2, 2 * levels, lanes), f32),
        vm((2, steps, 2 * levels + 8, lanes), f32),
        vm((2, steps, 2 * levels + 8, lanes), f32),
        vm((2, steps, 2, 2 * levels, lanes), f32),
        vm((2, 5, 2 * levels, lanes), f32),
        vm((2, 2 * levels + 8, lanes), f32),
        vm((5, rows + 2 * OWN, lanes), f32),
        vm((2, 5, rows + 2 * OWN, lanes), f32),
        vm((2, 5, rows, lanes), f32),
        vm((2, 5, rows + 8, lanes), f32),
        vm((2, rows + 2 * OWN, lanes), f32),
        vm((2 * (regions // blk), (rows + 5) * lanes), b16),
        vm((blk, (rows + 5) * lanes), b16),
        vm((4 * (regions // blk), (rows + 5) * lanes), b16),
        vm((regions // blk, 2, blk), f32),
        vm((5 * levels * rows, lanes), f32),
        pltpu.SemaphoreType.DMA((6,)),
        pltpu.SemaphoreType.DMA((2,)),
        pltpu.SemaphoreType.DMA((10,)),
        pltpu.SemaphoreType.DMA((2,)),
    ]
    adjoint, landed, cov = pl.pallas_call(
        functools.partial(kernel, nlon, nlat, width),
        out_shape=(
            pltpu.VMEM(field, f32),
            pltpu.VMEM((nlon * nlat, steps, blk), f32),
            pltpu.VMEM((blk, blk), f32),
        ),
        in_specs=[pl.BlockSpec(memory_space=pltpu.HBM)] * 10,
        out_specs=(pl.BlockSpec(memory_space=pl.ANY),) * 3,
        scratch_shapes=scratch,
        compiler_params=pltpu.CompilerParams(
            collective_id=0, has_side_effects=True, vmem_limit_bytes=61 * 1024 * 1024
        ),
    )(
        adjoint_final,
        lon_courant,
        lon_branch,
        lat_courant,
        lat_branch,
        mixing,
        prior_cov,
        region_map,
        region_order.reshape(regions // 128, 128),
        cosines,
    )
    adjoint, flux = pl.pallas_call(
        finish,
        out_shape=(
            jax.ShapeDtypeStruct(field, f32),
            jax.ShapeDtypeStruct((steps, blk), f32),
        ),
        in_specs=[
            pl.BlockSpec(memory_space=pl.ANY),
            pl.BlockSpec(memory_space=pltpu.VMEM),
            pl.BlockSpec(memory_space=pltpu.VMEM),
        ],
        out_specs=(pl.BlockSpec(memory_space=pl.ANY),) * 2,
        scratch_shapes=[vm((steps, blk), f32), pltpu.SemaphoreType.DMA((2,))],
    )(*(pltpu.with_memory_space_constraint(x, pltpu.VMEM) for x in (adjoint, landed, cov)))
    if width < blk:
        start = lax.rem(lax.axis_index("lat") * width, blk)
        flux = lax.dynamic_slice_in_dim(flux, start, width, 1)
    return adjoint, flux


def solution(mesh):
    four = P(None, None, "lon", "lat")
    placed = (
        P(None, "lon", "lat"),
        four,
        four,
        four,
        four,
        four,
        P("lon", "lat"),
        P(),
        P("lon", None, None),
    )
    return jax.shard_map(
        functools.partial(per_device, mesh.shape["lon"], mesh.shape["lat"]),
        mesh=mesh,
        in_specs=placed,
        out_specs=(P(None, "lon", "lat"), P(None, ("lon", "lat"))),
        check_vma=False,
    )
```

```python
import functools
import math

import jax
import jax.numpy as jnp
import numpy as np
from jax import lax
from jax.experimental import pallas as pl
from jax.experimental.pallas import tpu as pltpu
from jax.sharding import PartitionSpec as P

MESH = pl.DeviceIdType.MESH
OWN = 8


def face_weights(courant, branch):
    lean_part = courant * (0.5 * (1.0 - jnp.abs(courant)))
    one_part = jnp.where(branch == 1, lean_part, 0.0)
    two_part = jnp.where(branch == 2, lean_part, 0.0)
    donor = courant - one_part + two_part
    left = courant > 0.0
    return (
        jnp.where(left, -two_part, 0.0),
        jnp.where(left, donor, one_part),
        jnp.where(left, one_part, donor),
        jnp.where(left, 0.0, -two_part),
    )


def kernel(
    nlon,
    nlat,
    width,
    adj_h,
    lonc_h,
    lonb_h,
    latc_h,
    latb_h,
    mix_h,
    cov_h,
    rmap_h,
    order_h,
    cos_h,
    out_h,
    land,
    covv,
    out_ref,
    rmap_ref,
    order_ref,
    cos_ref,
    x_ref,
    mixv,
    latc,
    latb,
    lonc,
    lonb,
    inv_ref,
    kin_ref,
    nr_ref,
    join_ref,
    y_ref,
    ext,
    lw,
    pack,
    land_p,
    raw_rows,
    rows_a,
    far_a,
    rows_w,
    rows_c,
    delta,
    ids,
    beside,
    lat_c,
    lon_c,
    bext,
    hot,
    cht,
    amat,
    send_ref,
    sizer,
    local_sem,
    send_sem,
    recv_sem,
    all_sem,
):
    steps, levels, rows, lanes = latc.shape
    count = nlon * nlat
    my_lon, my_lat = lax.axis_index("lon"), lax.axis_index("lat")
    me = my_lon * nlat + my_lat
    blk = covv.shape[0]

    def place(device):
        return (device // nlat, lax.rem(device, nlat))

    barrier = pltpu.get_barrier_semaphore()

    def fetch(src, dst, slot):
        pltpu.make_async_copy(src, dst, local_sem.at[slot]).start()

    def drain(sem, count_rows):
        part = sizer.at[pl.ds(0, count_rows)]
        pltpu.make_async_copy(part, part, sem).wait()

    def got(slot, count_rows):
        drain(local_sem.at[slot], count_rows)

    far_first = jnp.where(my_lon >= nlon // 2, 1, 0)

    def greet(k, carry):
        device = far_first * k + (1 - far_first) * (count - 1 - k)

        @pl.when(device != me)
        def _():
            pl.semaphore_signal(barrier, inc=1, device_id=place(device), device_id_type=MESH)

        return carry

    lax.fori_loop(0, count // 4, greet, 0)
    fetch(mix_h.at[1], mixv.at[1], 0)
    fetch(adj_h, x_ref, 1)
    fetch(latc_h.at[1], latc.at[1], 2)
    fetch(latb_h.at[1], latb.at[1], 2)
    fetch(lonc_h.at[1], lonc.at[1], 2)
    fetch(lonb_h.at[1], lonb.at[1], 2)
    fetch(latc_h.at[0], latc.at[0], 3)
    fetch(latb_h.at[0], latb.at[0], 3)
    fetch(lonc_h.at[0], lonc.at[0], 3)
    fetch(lonb_h.at[0], lonb.at[0], 3)
    fetch(rmap_h, rmap_ref, 3)
    fetch(order_h, order_ref, 3)
    fetch(cos_h, cos_ref, 3)
    fetch(mix_h.at[0], mixv.at[0], 4)
    fetch(cov_h.at[(my_lat * width) // blk], covv, 4)
    lax.fori_loop(count // 4, count, greet, 0)

    lane = lax.broadcasted_iota(jnp.int32, (rows, lanes), 1)
    pair = lane // 2
    even = lax.rem(lane, 2) == 0
    zero = jnp.zeros((rows, lanes), jnp.float32)

    def roll(value, shift):
        return pltpu.roll(value, shift, 1)

    def remote(src, dst, send_slot, recv_slot, device):
        pltpu.make_async_remote_copy(
            src_ref=src,
            dst_ref=dst,
            send_sem=send_sem.at[send_slot],
            recv_sem=recv_sem.at[recv_slot],
            device_id=device,
            device_id_type=MESH,
        ).start()

    north = (my_lon, lax.rem(my_lat + 1, nlat))
    south = (my_lon, lax.rem(my_lat + nlat - 1, nlat))
    east = (lax.rem(my_lon + 1, nlon), my_lat)
    west = (lax.rem(my_lon + nlon - 1, nlon), my_lat)

    meet = levels // 2

    def coefficients(s):
        def sweep(order, before, after):
            ahead = None
            for level in order:
                inner, outer = before(level), after(level)
                if ahead is None:
                    inv = 1.0 / (1.0 + outer)
                    kin_ref[s, level] = zero
                else:
                    inv = 1.0 / ((1.0 + outer) + inner * (1.0 - ahead))
                    kin_ref[s, level] = inner * inv
                inv_ref[s, level] = inv
                ahead = outer * inv
                nr_ref[s, level] = ahead
            return ahead

        def below(level):
            return mixv[s, level - 1] if level > 0 else None

        def above(level):
            return mixv[s, level] if level < levels - 1 else None

        up = sweep(range(meet), below, above)
        down = sweep(range(levels - 1, meet - 1, -1), above, below)
        join_ref[s] = 1.0 / (1.0 - up * down)

    def tail_head(value, level, tail, head):
        turned = roll(value, 2 * level + 2)
        return jnp.where(pair == level, turned, tail), jnp.where(pair == level + 1, turned, head)

    def solve(s):
        def carry(level, carried):
            value = x_ref[level] * inv_ref[s, level]
            return value if carried is None else value + kin_ref[s, level] * carried

        up = down = None
        for i in range(levels - meet):
            if i < meet:
                up = carry(i, up)
                y_ref[i] = up
            level = levels - 1 - i
            down = carry(level, down)
            y_ref[level] = down
        tail = head = zero
        up_value = down_value = None
        for i in range(levels - meet):
            level = meet + i
            if i == 0:
                down_value = (down + nr_ref[s, level] * up) * join_ref[s]
            else:
                down_value = y_ref[level] + nr_ref[s, level] * down_value
            found = [(level, down_value)]
            if i < meet:
                level = meet - 1 - i
                if i == 0:
                    up_value = up + nr_ref[s, level] * down_value
                else:
                    up_value = y_ref[level] + nr_ref[s, level] * up_value
                found.append((level, up_value))
            for level, value in found:
                y_ref[level] = value
                raw_rows[0, pl.ds(2 * level, 2), :] = value[rows - 2 :]
                raw_rows[1, pl.ds(2 * level, 2), :] = value[:2]
                tail, head = tail_head(value, level, tail, head)
        head = roll(head, lanes - 2)
        for member, value in enumerate((tail, head)):
            pack[s, member, 0, OWN : OWN + rows] = value
            at = 2 * member
            rows_a[0, s, at : at + 2] = value[rows - 2 :]
            rows_a[1, s, at : at + 2] = value[:2]

    def pack_weights(s):
        def body(level, carry):
            ct, ch, bt, bh = carry
            ct, ch = tail_head(latc[s, level], level, ct, ch)
            both = (latc[s, level], latb[s, level].astype(jnp.float32))
            bt, bh = tail_head(both[1], level, bt, bh)
            for member in range(2):
                rows_w[0, s, member, pl.ds(2 * level, 2), :] = both[member][rows - 2 :]
                rows_w[1, s, member, pl.ds(2 * level, 2), :] = both[member][:2]
            return ct, ch, bt, bh

        ct, ch, bt, bh = lax.fori_loop(0, levels, body, (zero,) * 4, unroll=True)
        found = ((ct, bt), (roll(ch, lanes - 2), roll(bh, lanes - 2)))
        for end in range(2):
            for member in range(2):
                pack[s, end, 1 + member, OWN : OWN + rows] = found[end][member]
        for member in range(2):
            at = 4 + 2 * member
            rows_a[0, s, at : at + 2] = found[1][member][rows - 2 :]
            rows_a[1, s, at : at + 2] = found[1][member][:2]

    def row_weights(s):
        lane = lax.broadcasted_iota(jnp.int32, (2 * levels, lanes), 1)
        for side in range(2):
            m2, m1, m0, p1 = face_weights(rows_w[side, s, 0], rows_w[side, s, 1])
            ahead1 = jnp.where(lane <= lanes - 2, roll(m1, lanes - 1), 0.0)
            ahead2 = jnp.where(lane <= lanes - 3, roll(m2, lanes - 2), 0.0)
            here = jnp.where(lane >= 1, m0, 0.0)
            behind = jnp.where(lane >= 2, roll(p1, 1), 0.0)
            found = (1.0 - ahead1 + here, ahead1 - ahead2, ahead2, behind - here, -behind)
            for k, value in enumerate(found):
                rows_c[side, k] = value

    def lat_rows(s):
        for side in range(2):
            a = raw_rows[side]
            value = rows_c[side, 0] * a
            for k, turn in ((1, lanes - 1), (2, lanes - 2), (3, 1), (4, 2)):
                value = value + rows_c[side, k] * roll(a, turn)
            rows_a[side, s, 8:] = value

    def lat_pass(a, courant, branch):
        at = lax.broadcasted_iota(jnp.int32, a.shape, 1)
        m2, m1, m0, p1 = face_weights(courant, branch)
        jump = jnp.where(at >= 1, a - roll(a, 1), 0.0)
        out = a + m0 * jump + roll(m1 * jump, lanes - 1)
        out = out + roll(jnp.where(at >= 2, m2 * jump, 0.0), lanes - 2)
        return out + roll(jnp.where(at <= lanes - 2, p1 * jump, 0.0), 1)

    def lat_inner(s):
        def body(level, carry):
            out = lat_pass(y_ref[level], latc[s, level], latb[s, level])
            ext[s, level, OWN : OWN + rows] = out
            return carry

        lax.fori_loop(0, levels, body, 0, unroll=True)

    def edge_terms(s, at):
        count_rows = at.stop - at.start
        lane = lax.broadcasted_iota(jnp.int32, (count_rows, lanes), 1)
        even = lax.rem(lane, 2) == 0
        tail, head = pack[s, 0, 0, at], pack[s, 1, 0, at]
        before, after = land_p[s, 0, 0, at], land_p[s, 1, 0, at]
        m2_after, m1_after, _, _ = face_weights(land_p[s, 1, 1, at], land_p[s, 1, 2, at])
        _, _, m0_head, p1_head = face_weights(pack[s, 1, 1, at], pack[s, 1, 2, at])
        _, _, _, p1_before = face_weights(land_p[s, 0, 1, at], land_p[s, 0, 2, at])
        jump = after - jnp.where(even, roll(tail, lanes - 1), roll(after, 1))
        top_here = jnp.where(has_north, m2_after * jump, 0.0)
        top_next = jnp.where(jnp.logical_and(even, has_north), m1_after * jump, 0.0)
        jump = jnp.where(even, head - roll(before, lanes - 1), before - roll(before, 1))
        flux = jnp.where(has_south, jnp.where(even, p1_head, p1_before) * jump, 0.0)
        low_here = jnp.where(has_south, m0_head * jump, 0.0)
        edge = jnp.logical_or(lane < 2, lane >= lanes - 2)

        def turned_back(by):
            def turn(value, shift):
                shift = (shift - by) % lanes
                return roll(value, shift) if shift else value

            first = lax.rem(lane + by, 4) < 2
            evens = lax.rem(lane + by, 2) == 0
            top = turn(top_here, 0) + turn(top_next, 1)
            low = jnp.where(evens, turn(low_here, 2) + turn(flux, 1), turn(flux, 3))
            return jnp.where(first, top, low), jnp.where(first, low, top)

        return turned_back, edge

    def own_edges(s):
        turned_back, edge = edge_terms(s, slice(OWN, OWN + rows))
        both = turned_back(0)
        for level in range(levels):
            turned = roll(both[level % 2], lanes - 2 - 2 * level)
            ext[s, level, OWN : OWN + rows] += jnp.where(edge, turned, 0.0)

    def far_edges(s):
        end = OWN + rows
        for side, where in enumerate((slice(OWN - 2, OWN), slice(end, end + 2))):
            for member in range(2):
                pack[s, member, 0, where] = far_a[side, s, 2 * member : 2 * member + 2]
                far = 4 + 2 * member
                pack[s, 1, 1 + member, where] = far_a[side, s, far : far + 2]
        down = lax.broadcasted_iota(jnp.int32, (8, lanes), 0)
        for side, (at, row) in enumerate(((slice(0, OWN), OWN - 2), (slice(end, end + OWN), 0))):
            turned_back, edge = edge_terms(s, at)
            both = turned_back(0), turned_back(1)
            rows2 = [
                jnp.where(
                    lax.rem(down // 2 + levels - 1, 2) == 0,
                    jnp.broadcast_to(both[odd][0][row + odd : row + odd + 1], (8, lanes)),
                    jnp.broadcast_to(both[odd][1][row + odd : row + odd + 1], (8, lanes)),
                )
                for odd in range(2)
            ]
            tile = jnp.where(lax.rem(down, 2) == 0, rows2[0], rows2[1])
            for v in range((2 * levels + 7) // 8):
                turn = (8 * v - 2 * levels) % lanes
                late = turn > lanes - 8
                source = roll(tile, lanes // 2) if late else tile
                turn = turn - lanes // 2 if late else turn
                turned = pltpu.roll(source, turn, 1, stride=1, stride_axis=0)
                delta[side, 8 * v : 8 * v + 8] = jnp.where(edge, turned, 0.0)

    def edges_and_lon(s, target, part):
        end = OWN + rows
        for level in range(*part):
            far, two = slice(8 + 2 * level, 10 + 2 * level), slice(2 * (levels - 1 - level), 2 * (levels - level))
            ext[s, level, OWN - 2 : OWN] = far_a[0, s, far] + delta[0, two]
            ext[s, level, end : end + 2] = far_a[1, s, far] + delta[1, two]
        for level in range(*part):
            target[level] = lon_level(s, level)

    def lon_own_weights(s):
        def body(level, carry):
            found = face_weights(
                lonc[s, level], lonb[s, level]
            )
            for member in range(4):
                lw[s, member, level, OWN : OWN + rows] = found[member]
            return carry

        lax.fori_loop(0, levels, body, 0, unroll=True)

    def lon_level(s, level):
        a = [ext[s, level, OWN + k : OWN + k + rows] for k in range(-2, 3)]
        w = [
            lw[s, member, level, OWN + 2 - member : OWN + 2 - member + rows]
            for member in range(4)
        ]
        out = a[2] + w[0] * (a[4] - a[3]) + w[1] * (a[3] - a[2])
        return out + w[2] * (a[2] - a[1]) + w[3] * (a[1] - a[0])

    def send_lon(s, part, slot):
        end = OWN + rows
        for member, src, dst, size, device in (
            (0, OWN, end, 2, west),
            (1, OWN, end, 1, west),
            (3, end - 1, OWN - 1, 1, east),
        ):
            at = pl.ds(part[0], part[1] - part[0])
            remote(
                lw.at[s, member, at, pl.ds(src, size), :],
                lw.at[s, member, at, pl.ds(dst, size), :],
                0,
                slot,
                device,
            )

    def find_slots():
        order = order_ref[...]
        table = jnp.concatenate([order // blk, lax.rem(order, blk)], axis=0)
        table = table.astype(jnp.float32).astype(jnp.bfloat16)
        high = order.shape[0]
        down = lax.broadcasted_iota(jnp.int32, (lanes, lanes), 0)
        row_of = lax.broadcasted_iota(jnp.int32, (high, lanes), 0)
        for i in range(rows):
            region = rmap_ref[i : i + 1, :]
            hit = jnp.where(down == lax.rem(region, 128), 1.0, 0.0).astype(jnp.bfloat16)
            found = jnp.dot(table, hit, preferred_element_type=jnp.float32)
            both = found[:high] * float(blk) + found[high:]
            both = jnp.where(row_of == region // 128, both, 0.0)
            ids[2, OWN + i : OWN + i + 1] = jnp.sum(both, axis=0, keepdims=True)

    def spread(i, slot):
        groups = hot.shape[0] // 2
        slot = slot.astype(jnp.int32)
        high = lax.broadcasted_iota(jnp.int32, (2 * groups, lanes), 0) // 2
        low = lax.broadcasted_iota(jnp.int32, (blk, lanes), 0)
        at = slice(i * lanes, (i + 1) * lanes)
        hot[:, at] = jnp.where(high == slot // blk, 1.0, 0.0).astype(jnp.bfloat16)
        cht[:, at] = jnp.where(low == lax.rem(slot, blk), 1.0, 0.0).astype(jnp.bfloat16)

    def regions(pushed, side, later):
        tile, many = 16, hot.shape[0]
        step0 = lax.rem(lax.broadcasted_iota(jnp.int32, (tile, lanes), 0), 2) == 0
        for i in range(rows + 5):
            here = slice(i * lanes, (i + 1) * lanes)
            first = pushed[i : i + 1] if i < rows + 4 else side
            second = later[i - 2 : i - 1] if 2 <= i < rows + 2 else jnp.zeros_like(first)
            value = jnp.where(
                step0, jnp.broadcast_to(first, (tile, lanes)), jnp.broadcast_to(second, (tile, lanes))
            )
            coarse = value.astype(jnp.bfloat16)
            fine = (value - coarse.astype(jnp.float32)).astype(jnp.bfloat16)
            for part, piece in enumerate((coarse, fine)):
                for at in range(0, many, tile):
                    amat[part * many + at : part * many + at + tile, here] = (
                        hot[at : at + tile, here] * piece
                    )
        sums = lax.dot_general(
            amat[...], cht[...], (((1,), (1,)), ((), ())), preferred_element_type=jnp.float32
        )
        sums = sums[:many] + sums[many:]
        for group in range(many // 2):
            send_ref[group] = sums[2 * group : 2 * group + 2]

    tall_rows = rows + 2 * OWN
    few = slice(OWN - 2, OWN + rows + 6)
    has_north, has_south = my_lat < nlat - 1, my_lat > 0

    def push_lat():
        courant = jnp.where(jnp.logical_and(lane == 0, my_lat == 0), 0.0, latc[0, 0])
        m2, m1, m0, p1 = face_weights(courant, latb[0, 0])
        north_c = jnp.where(has_north, beside[1, 3, OWN : OWN + rows], 0.0)
        n2, n1, n0, np1 = face_weights(north_c, beside[1, 4, OWN : OWN + rows])
        ahead1 = jnp.where(lane == lanes - 1, roll(n1, lanes - 1), roll(m1, lanes - 1))
        round2 = roll(m2, lanes - 2)
        ahead2 = jnp.where(lane >= lanes - 2, roll(n2, lanes - 2), round2)
        behind = roll(p1, 1)
        lat_c[0, 0] = 1.0 - ahead1 + m0
        lat_c[0, 1] = jnp.where(lane <= lanes - 2, ahead1 - ahead2, 0.0)
        lat_c[0, 2] = jnp.where(lane <= lanes - 3, ahead2, 0.0)
        lat_c[0, 3] = jnp.where(lane >= 1, behind - m0, 0.0)
        lat_c[0, 4] = jnp.where(lane >= 2, -behind, 0.0)
        last, first = jnp.logical_and(lane == lanes - 1, has_south), jnp.logical_and(lane == 0, has_north)
        lat_c[1, 1] = jnp.where(last, roll(m1, lanes - 1) - round2, 0.0)
        lat_c[1, 2] = jnp.where(jnp.logical_and(lane >= lanes - 2, has_south), round2, 0.0)
        lat_c[1, 3] = jnp.where(first, behind - n0, 0.0)
        second = jnp.logical_and(lane == 1, has_north)
        lat_c[1, 4] = jnp.where(first, -behind, jnp.where(second, -roll(np1, 1), 0.0))

    def push_lon(side):
        down = lax.broadcasted_iota(jnp.int32, (tall_rows, lanes), 0)
        across = lax.broadcasted_iota(jnp.int32, (tall_rows, lanes), 1)
        faces = jnp.logical_and(down >= OWN, down <= OWN + rows)
        here, south_of = cos_ref[my_lat], cos_ref[lax.rem(my_lat + nlat - 1, nlat)]
        north_of = cos_ref[lax.rem(my_lat + 1, nlat)]
        across1 = lax.broadcasted_iota(jnp.int32, (1, lanes), 1)
        at_north = jnp.logical_and(across < 2, has_north)
        at_south = jnp.logical_and(across >= lanes - 2, has_south)
        if side == 0:
            courant, branch, cosine = ids[0], ids[1], here
        else:
            courant, branch = (
                jnp.where(at_north, beside[1, m], jnp.where(at_south, beside[0, m], 0.0))
                for m in range(2)
            )
            cosine = jnp.where(across1 < 2, north_of, south_of)
        m2, m1, m0, p1 = face_weights(jnp.where(faces, courant, 0.0), branch)
        ahead1 = pltpu.roll(m1, tall_rows - 1, 0)
        ahead2 = pltpu.roll(m2, tall_rows - 2, 0)
        behind = pltpu.roll(p1, 1, 0)
        found = (1.0 - ahead1 + m0, ahead1 - ahead2, ahead2, behind - m0, -behind)
        for k, value in enumerate(found):
            lon_c[side, k] = value[few] * cosine

    def squeeze(value):
        return jnp.sum(pltpu.roll(value, 0, 1, stride=4, stride_axis=0), axis=0, keepdims=True)

    def side_slots():
        shape = (rows + 8, lanes)
        down = lax.broadcasted_iota(jnp.int32, shape, 0)
        across = lax.broadcasted_iota(jnp.int32, shape, 1)
        at_north = jnp.logical_and(across < 2, has_north)
        at_south = jnp.logical_and(across >= lanes - 2, has_south)
        side = jnp.where(at_north, beside[1, 2, few], jnp.where(at_south, beside[0, 2, few], 0.0))
        side = squeeze(jnp.where(down < rows + 4, side, 0.0))
        spread(rows + 4, side)

    def push_totals():
        a = y_ref[0]
        turned = (a, roll(a, lanes - 1), roll(a, lanes - 2), roll(a, 1), roll(a, 2))
        for side in range(2):
            value = lat_c[side, 1] * turned[1]
            for k in range(2, 5):
                value = value + lat_c[side, k] * turned[k]
            if side == 0:
                value = value + lat_c[0, 0] * a
            bext[side, OWN : OWN + rows] = value
        found = []
        for side in range(2):
            value = jnp.zeros((rows + 8, lanes), jnp.float32)
            for k, step in enumerate((0, 1, 2, -1, -2)):
                at = OWN - 2 + step
                value = value + lon_c[side, k] * bext[side, at : at + rows + 8]
            found.append(value)
        regions(found[0], squeeze(found[1]), x_ref[0] * cos_ref[my_lat])

    got(0, (levels - 1) * rows)
    coefficients(1)
    got(1, levels * rows)
    solve(1)
    got(2, 4 * levels * rows)
    pack_weights(1)
    row_weights(1)
    lat_rows(1)
    lon_own_weights(1)
    got(3, 4 * levels * rows + rows + order_ref.shape[0] + nlat)
    ids[0, OWN : OWN + rows] = lonc[0, 0]
    ids[1, OWN : OWN + rows] = lonb[0, 0].astype(jnp.float32)
    ids[3, OWN : OWN + rows] = latc[0, 0]
    ids[4, OWN : OWN + rows] = latb[0, 0].astype(jnp.float32)
    find_slots()
    bext[...] = jnp.zeros_like(bext)
    pl.semaphore_wait(barrier, count - 1)

    turn = {1: lax.rem(my_lon + 1, nlon), -1: lax.rem(my_lon + nlon - 1, nlon)}
    own_rows, first, last_two = pl.ds(OWN, rows), pl.ds(OWN, 2), pl.ds(OWN + rows - 2, 2)
    low, high = pl.ds(OWN - 2, 2), pl.ds(OWN + rows, 2)

    toward = (north[1], south[1])
    send_if, recv_if = (has_north, has_south), (has_south, has_north)
    column_rows = rows + 4

    def send_end(source, target, recv_base, diagonal, end, lat):
        for lon, src, dst in (
            ((turn[1], last_two, low), (turn[-1], first, high))
            if diagonal
            else ((my_lon, own_rows, own_rows),)
        ):
            remote(
                source(end, src),
                target(end, dst),
                1,
                recv_base + (1 if diagonal else 0),
                (lon, lat),
            )

    def send_columns(source, target, recv_base, diagonal):
        if nlat == 2:
            send_end(source, target, recv_base, diagonal, my_lat, 1 - my_lat)
            return
        for end in range(2):

            @pl.when(send_if[end])
            def _():
                send_end(source, target, recv_base, diagonal, end, toward[end])

    beside_count = jnp.where(has_north, 1, 0) + jnp.where(has_south, 1, 0)

    def drain_beside(sem, count_rows):
        if nlat == 2:
            drain(sem, count_rows)
            return
        for ends in (1, 2):

            @pl.when(beside_count == ends)
            def _():
                drain(sem, ends * count_rows)

    half = 2 * levels // 3
    parts = ((0, half), (half, levels))
    spans = (pl.ds(0, 8 + 2 * half), pl.ds(8 + 2 * half, 2 * (levels - half)))
    border = (2 * (8 + 2 * half), 4 * (levels - half))

    def send_border(s, part, slot):
        at = spans[part]
        remote(rows_a.at[0, s, at, :], far_a.at[0, s, at, :], 0, slot, east)
        remote(rows_a.at[1, s, at, :], far_a.at[1, s, at, :], 0, slot, west)

    border_rows = sum(border)
    lon_rows = 4 * levels

    def group_of(device):
        return (device * width) // blk

    def scatter(k, carry):
        device = lax.rem(me + k, count)
        pltpu.make_async_remote_copy(
            src_ref=send_ref.at[group_of(device)],
            dst_ref=land.at[me],
            send_sem=all_sem.at[0],
            recv_sem=all_sem.at[1],
            device_id=place(device),
            device_id_type=MESH,
        ).start()
        return carry

    three = pl.ds(0, 3)

    def send_packs(diagonal):
        send_columns(
            lambda end, at: pack.at[1, end, :, at, :],
            lambda end, at: land_p.at[1, end, :, at, :],
            5,
            diagonal,
        )
        if diagonal:
            send_columns(
                lambda end, at: ids.at[three, at, :],
                lambda end, at: beside.at[end, three, at, :],
                5,
                True,
            )
        else:
            send_columns(
                lambda end, at: ids.at[:, at, :], lambda end, at: beside.at[end, :, at, :], 5, False
            )

    send_packs(True)
    remote(ids.at[three, last_two, :], ids.at[three, low, :], 0, 4, east)
    remote(ids.at[three, first, :], ids.at[three, high, :], 0, 4, west)
    send_packs(False)
    for part, slot in ((0, 1), (1, 3)):
        send_border(1, part, slot)
        send_lon(1, parts[part], slot)
    lat_inner(1)
    got(4, (levels - 1) * rows + blk * blk // lanes)
    coefficients(0)
    lon_own_weights(0)
    send_lon(0, (0, levels), 0)
    pack_weights(0)
    row_weights(0)
    for diagonal in (True, False):
        send_columns(
            lambda end, at: pack.at[0, end, 1:3, at, :],
            lambda end, at: land_p.at[0, end, 1:3, at, :],
            8,
            diagonal,
        )
    for i in range(rows):
        spread(2 + i, ids[2, OWN + i : OWN + i + 1])
    drain_beside(recv_sem.at[5], 8 * rows)
    own_edges(1)
    push_lat()
    drain(recv_sem.at[4], 12)
    push_lon(0)
    for i in (0, 1, rows + 2, rows + 3):
        spread(i, ids[2, OWN - 2 + i : OWN - 1 + i])
    drain_beside(recv_sem.at[6], 24)
    for part, slot in ((0, 1), (1, 3)):
        drain(recv_sem.at[slot], border[part] + 4 * (parts[part][1] - parts[part][0]))
        if part == 0:
            far_edges(1)
        else:
            push_lon(1)
            side_slots()
        edges_and_lon(1, x_ref, parts[part])
    solve(0)
    lat_rows(0)
    for diagonal in (True, False):
        send_columns(
            lambda end, at: pack.at[0, end, 0, at, :],
            lambda end, at: land_p.at[0, end, 0, at, :],
            8,
            diagonal,
        )
    send_border(0, 0, 2)
    send_border(0, 1, 7)
    push_totals()
    lax.fori_loop(1, count, scatter, 0)
    fetch(send_ref.at[group_of(me)], land.at[me], 5)
    lat_inner(0)
    drain(recv_sem.at[0], lon_rows)
    drain_beside(recv_sem.at[8], 3 * rows)
    own_edges(0)
    drain_beside(recv_sem.at[9], 12)
    for part, slot in ((0, 2), (1, 7)):
        drain(recv_sem.at[slot], border[part])
        if part == 0:
            far_edges(0)
        edges_and_lon(0, out_ref, parts[part])
    fetch(out_ref, out_h, 5)
    got(5, levels * rows + 2 * blk // lanes)
    drain(send_sem.at[0], 2 * (border_rows + lon_rows) + 12)
    drain_beside(send_sem.at[1], 9 * column_rows + 2 * rows)
    every = land.at[pl.ds(0, count - 1)]
    pltpu.make_async_copy(every, every, all_sem.at[0]).wait()
    pltpu.make_async_copy(every, every, all_sem.at[1]).wait()


def finish(adjoint_v, land, cov, adjoint_h, flux_h, flux, sem):
    whole = pltpu.make_async_copy(adjoint_v, adjoint_h, sem.at[0])
    whole.start()
    totals = jnp.sum(land[...], axis=0)
    coarse = totals.astype(jnp.bfloat16).astype(jnp.float32)
    rest = jnp.zeros((12, totals.shape[1]), jnp.float32)
    both = jnp.concatenate([coarse, totals - coarse, rest], axis=0).astype(jnp.bfloat16)
    cov_high = cov[...].astype(jnp.bfloat16)
    cov_low = (cov[...] - cov_high.astype(jnp.float32)).astype(jnp.bfloat16)
    found = jnp.dot(both, cov_high, preferred_element_type=jnp.float32)
    found = found + jnp.dot(both, cov_low, preferred_element_type=jnp.float32)
    flux[...] = found[:2] + found[2:4]
    part = pltpu.make_async_copy(flux, flux_h, sem.at[1])
    part.start()
    part.wait()
    whole.wait()


def per_device(
    nlon,
    nlat,
    adjoint_final,
    lon_courant,
    lon_branch,
    lat_courant,
    lat_branch,
    mixing,
    region_map,
    region_order,
    prior_cov,
):
    steps, levels, rows, lanes = lon_courant.shape
    regions = region_order.shape[0]
    blk = prior_cov.shape[1]
    width = regions // (nlon * nlat)
    lat_total = lanes * nlat
    lat_index = np.arange(lat_total, dtype=np.float32)
    angle = (lat_index + np.float32(0.5)) * np.float32(math.pi / lat_total)
    cosines = np.cos((angle - np.float32(0.5 * math.pi)).astype(np.float32))
    cosines = jnp.asarray(cosines.astype(np.float32).reshape(nlat, 1, lanes))
    f32, i32, b16 = jnp.float32, jnp.int32, jnp.bfloat16
    field = (levels, rows, lanes)
    tall = (levels, rows + 2 * OWN, lanes)
    vm = pltpu.VMEM
    scratch = [
        vm(field, f32),
        vm((rows, lanes), i32),
        vm((regions // 128, 128), i32),
        vm((nlat, 1, lanes), f32),
        vm(field, f32),
        vm((steps, levels - 1, rows, lanes), f32),
        vm((steps,) + field, f32),
        vm((steps,) + field, i32),
        vm((steps,) + field, f32),
        vm((steps,) + field, i32),
        vm((steps,) + field, f32),
        vm((steps,) + field, f32),
        vm((steps,) + field, f32),
        vm((steps, rows, lanes), f32),
        vm(field, f32),
        vm((steps,) + tall, f32),
        vm((steps, 4) + tall, f32),
        vm((steps, 2, 3, rows + 2 * OWN, lanes), f32),
        vm((steps, 2, 3, rows + 2 * OWN, lanes), f32),
        vm((2, 2 * levels, lanes), f32),
        vm((2, steps, 2 * levels + 8, lanes), f32),
        vm((2, steps, 2 * levels + 8, lanes), f32),
        vm((2, steps, 2, 2 * levels, lanes), f32),
        vm((2, 5, 2 * levels, lanes), f32),
        vm((2, 2 * levels + 8, lanes), f32),
        vm((5, rows + 2 * OWN, lanes), f32),
        vm((2, 5, rows + 2 * OWN, lanes), f32),
        vm((2, 5, rows, lanes), f32),
        vm((2, 5, rows + 8, lanes), f32),
        vm((2, rows + 2 * OWN, lanes), f32),
        vm((2 * (regions // blk), (rows + 5) * lanes), b16),
        vm((blk, (rows + 5) * lanes), b16),
        vm((4 * (regions // blk), (rows + 5) * lanes), b16),
        vm((regions // blk, 2, blk), f32),
        vm((5 * levels * rows, lanes), f32),
        pltpu.SemaphoreType.DMA((6,)),
        pltpu.SemaphoreType.DMA((2,)),
        pltpu.SemaphoreType.DMA((10,)),
        pltpu.SemaphoreType.DMA((2,)),
    ]
    adjoint, landed, cov = pl.pallas_call(
        functools.partial(kernel, nlon, nlat, width),
        out_shape=(
            pltpu.VMEM(field, f32),
            pltpu.VMEM((nlon * nlat, steps, blk), f32),
            pltpu.VMEM((blk, blk), f32),
        ),
        in_specs=[pl.BlockSpec(memory_space=pltpu.HBM)] * 10,
        out_specs=(pl.BlockSpec(memory_space=pl.ANY),) * 3,
        scratch_shapes=scratch,
        compiler_params=pltpu.CompilerParams(
            collective_id=0, has_side_effects=True, vmem_limit_bytes=61 * 1024 * 1024
        ),
    )(
        adjoint_final,
        lon_courant,
        lon_branch,
        lat_courant,
        lat_branch,
        mixing,
        prior_cov,
        region_map,
        region_order.reshape(regions // 128, 128),
        cosines,
    )
    adjoint, flux = pl.pallas_call(
        finish,
        out_shape=(
            jax.ShapeDtypeStruct(field, f32),
            jax.ShapeDtypeStruct((steps, blk), f32),
        ),
        in_specs=[
            pl.BlockSpec(memory_space=pl.ANY),
            pl.BlockSpec(memory_space=pltpu.VMEM),
            pl.BlockSpec(memory_space=pltpu.VMEM),
        ],
        out_specs=(pl.BlockSpec(memory_space=pl.ANY),) * 2,
        scratch_shapes=[vm((steps, blk), f32), pltpu.SemaphoreType.DMA((2,))],
    )(*(pltpu.with_memory_space_constraint(x, pltpu.VMEM) for x in (adjoint, landed, cov)))
    if width < blk:
        start = lax.rem(lax.axis_index("lat") * width, blk)
        flux = lax.dynamic_slice_in_dim(flux, start, width, 1)
    return adjoint, flux


def solution(mesh):
    four = P(None, None, "lon", "lat")
    placed = (
        P(None, "lon", "lat"),
        four,
        four,
        four,
        four,
        four,
        P("lon", "lat"),
        P(),
        P("lon", None, None),
    )
    return jax.shard_map(
        functools.partial(per_device, mesh.shape["lon"], mesh.shape["lat"]),
        mesh=mesh,
        in_specs=placed,
        out_specs=(P(None, "lon", "lat"), P(None, ("lon", "lat"))),
        check_vma=False,
    )
```

```python
import functools
import math

import jax
import jax.numpy as jnp
import numpy as np
from jax import lax
from jax.experimental import pallas as pl
from jax.experimental.pallas import tpu as pltpu
from jax.sharding import PartitionSpec as P

MESH = pl.DeviceIdType.MESH
OWN = 8


def face_weights(courant, branch):
    lean_part = courant * (0.5 * (1.0 - jnp.abs(courant)))
    one_part = jnp.where(branch == 1, lean_part, 0.0)
    two_part = jnp.where(branch == 2, lean_part, 0.0)
    donor = courant - one_part + two_part
    left = courant > 0.0
    return (
        jnp.where(left, -two_part, 0.0),
        jnp.where(left, donor, one_part),
        jnp.where(left, one_part, donor),
        jnp.where(left, 0.0, -two_part),
    )


def kernel(
    nlon,
    nlat,
    width,
    adj_h,
    lonc_h,
    lonb_h,
    latc_h,
    latb_h,
    mix_h,
    cov_h,
    rmap_h,
    order_h,
    cos_h,
    out_h,
    land,
    covv,
    out_ref,
    rmap_ref,
    order_ref,
    cos_ref,
    x_ref,
    mixv,
    latc,
    latb,
    lonc,
    lonb,
    inv_ref,
    kin_ref,
    nr_ref,
    join_ref,
    y_ref,
    ext,
    lw,
    pack,
    land_p,
    raw_rows,
    rows_a,
    far_a,
    rows_w,
    rows_c,
    delta,
    ids,
    beside,
    lat_c,
    lon_c,
    bext,
    hot,
    cht,
    amat,
    send_ref,
    sizer,
    local_sem,
    send_sem,
    recv_sem,
    all_sem,
):
    steps, levels, rows, lanes = latc.shape
    count = nlon * nlat
    my_lon, my_lat = lax.axis_index("lon"), lax.axis_index("lat")
    me = my_lon * nlat + my_lat
    blk = covv.shape[0]

    def place(device):
        return (device // nlat, lax.rem(device, nlat))

    barrier = pltpu.get_barrier_semaphore()

    def fetch(src, dst, slot):
        pltpu.make_async_copy(src, dst, local_sem.at[slot]).start()

    def drain(sem, count_rows):
        part = sizer.at[pl.ds(0, count_rows)]
        pltpu.make_async_copy(part, part, sem).wait()

    def got(slot, count_rows):
        drain(local_sem.at[slot], count_rows)

    far_first = jnp.where(my_lon >= nlon // 2, 1, 0)

    def greet(k, carry):
        device = far_first * k + (1 - far_first) * (count - 1 - k)

        @pl.when(device != me)
        def _():
            pl.semaphore_signal(barrier, inc=1, device_id=place(device), device_id_type=MESH)

        return carry

    lax.fori_loop(0, count // 4, greet, 0)
    fetch(mix_h.at[1], mixv.at[1], 0)
    fetch(adj_h, x_ref, 1)
    fetch(latc_h.at[1], latc.at[1], 2)
    fetch(latb_h.at[1], latb.at[1], 2)
    fetch(lonc_h.at[1], lonc.at[1], 2)
    fetch(lonb_h.at[1], lonb.at[1], 2)
    fetch(latc_h.at[0], latc.at[0], 3)
    fetch(latb_h.at[0], latb.at[0], 3)
    fetch(lonc_h.at[0], lonc.at[0], 3)
    fetch(lonb_h.at[0], lonb.at[0], 3)
    fetch(rmap_h, rmap_ref, 3)
    fetch(order_h, order_ref, 3)
    fetch(cos_h, cos_ref, 3)
    fetch(mix_h.at[0], mixv.at[0], 4)
    fetch(cov_h.at[(my_lat * width) // blk], covv, 4)
    lax.fori_loop(count // 4, count, greet, 0)

    lane = lax.broadcasted_iota(jnp.int32, (rows, lanes), 1)
    pair = lane // 2
    even = lax.rem(lane, 2) == 0
    zero = jnp.zeros((rows, lanes), jnp.float32)

    def roll(value, shift):
        return pltpu.roll(value, shift, 1)

    def remote(src, dst, send_slot, recv_slot, device):
        pltpu.make_async_remote_copy(
            src_ref=src,
            dst_ref=dst,
            send_sem=send_sem.at[send_slot],
            recv_sem=recv_sem.at[recv_slot],
            device_id=device,
            device_id_type=MESH,
        ).start()

    north = (my_lon, lax.rem(my_lat + 1, nlat))
    south = (my_lon, lax.rem(my_lat + nlat - 1, nlat))
    east = (lax.rem(my_lon + 1, nlon), my_lat)
    west = (lax.rem(my_lon + nlon - 1, nlon), my_lat)

    meet = levels // 2

    def coefficients(s):
        def sweep(order, before, after):
            ahead = None
            for level in order:
                inner, outer = before(level), after(level)
                if ahead is None:
                    inv = 1.0 / (1.0 + outer)
                    kin_ref[s, level] = zero
                else:
                    inv = 1.0 / ((1.0 + outer) + inner * (1.0 - ahead))
                    kin_ref[s, level] = inner * inv
                inv_ref[s, level] = inv
                ahead = outer * inv
                nr_ref[s, level] = ahead
            return ahead

        def below(level):
            return mixv[s, level - 1] if level > 0 else None

        def above(level):
            return mixv[s, level] if level < levels - 1 else None

        up = sweep(range(meet), below, above)
        down = sweep(range(levels - 1, meet - 1, -1), above, below)
        join_ref[s] = 1.0 / (1.0 - up * down)

    def tail_head(value, level, tail, head):
        turned = roll(value, 2 * level + 2)
        return jnp.where(pair == level, turned, tail), jnp.where(pair == level + 1, turned, head)

    def solve(s):
        def carry(level, carried):
            value = x_ref[level] * inv_ref[s, level]
            return value if carried is None else value + kin_ref[s, level] * carried

        up = down = None
        for i in range(levels - meet):
            if i < meet:
                up = carry(i, up)
                y_ref[i] = up
            level = levels - 1 - i
            down = carry(level, down)
            y_ref[level] = down
        tail = head = zero
        up_value = down_value = None
        for i in range(levels - meet):
            level = meet + i
            if i == 0:
                down_value = (down + nr_ref[s, level] * up) * join_ref[s]
            else:
                down_value = y_ref[level] + nr_ref[s, level] * down_value
            found = [(level, down_value)]
            if i < meet:
                level = meet - 1 - i
                if i == 0:
                    up_value = up + nr_ref[s, level] * down_value
                else:
                    up_value = y_ref[level] + nr_ref[s, level] * up_value
                found.append((level, up_value))
            for level, value in found:
                y_ref[level] = value
                raw_rows[0, pl.ds(2 * level, 2), :] = value[rows - 2 :]
                raw_rows[1, pl.ds(2 * level, 2), :] = value[:2]
                tail, head = tail_head(value, level, tail, head)
        head = roll(head, lanes - 2)
        for member, value in enumerate((tail, head)):
            pack[s, member, 0, OWN : OWN + rows] = value
            at = 2 * member
            rows_a[0, s, at : at + 2] = value[rows - 2 :]
            rows_a[1, s, at : at + 2] = value[:2]

    def pack_weights(s):
        def body(level, carry):
            ct, ch, bt, bh = carry
            ct, ch = tail_head(latc[s, level], level, ct, ch)
            both = (latc[s, level], latb[s, level].astype(jnp.float32))
            bt, bh = tail_head(both[1], level, bt, bh)
            for member in range(2):
                rows_w[0, s, member, pl.ds(2 * level, 2), :] = both[member][rows - 2 :]
                rows_w[1, s, member, pl.ds(2 * level, 2), :] = both[member][:2]
            return ct, ch, bt, bh

        ct, ch, bt, bh = lax.fori_loop(0, levels, body, (zero,) * 4, unroll=True)
        found = ((ct, bt), (roll(ch, lanes - 2), roll(bh, lanes - 2)))
        for end in range(2):
            for member in range(2):
                pack[s, end, 1 + member, OWN : OWN + rows] = found[end][member]
        for member in range(2):
            at = 4 + 2 * member
            rows_a[0, s, at : at + 2] = found[1][member][rows - 2 :]
            rows_a[1, s, at : at + 2] = found[1][member][:2]

    def row_weights(s):
        lane = lax.broadcasted_iota(jnp.int32, (2 * levels, lanes), 1)
        for side in range(2):
            m2, m1, m0, p1 = face_weights(rows_w[side, s, 0], rows_w[side, s, 1])
            ahead1 = jnp.where(lane <= lanes - 2, roll(m1, lanes - 1), 0.0)
            ahead2 = jnp.where(lane <= lanes - 3, roll(m2, lanes - 2), 0.0)
            here = jnp.where(lane >= 1, m0, 0.0)
            behind = jnp.where(lane >= 2, roll(p1, 1), 0.0)
            found = (1.0 - ahead1 + here, ahead1 - ahead2, ahead2, behind - here, -behind)
            for k, value in enumerate(found):
                rows_c[side, k] = value

    def lat_rows(s):
        for side in range(2):
            a = raw_rows[side]
            value = rows_c[side, 0] * a
            for k, turn in ((1, lanes - 1), (2, lanes - 2), (3, 1), (4, 2)):
                value = value + rows_c[side, k] * roll(a, turn)
            rows_a[side, s, 8:] = value

    def lat_pass(a, courant, branch):
        at = lax.broadcasted_iota(jnp.int32, a.shape, 1)
        m2, m1, m0, p1 = face_weights(courant, branch)
        jump = jnp.where(at >= 1, a - roll(a, 1), 0.0)
        out = a + m0 * jump + roll(m1 * jump, lanes - 1)
        out = out + roll(jnp.where(at >= 2, m2 * jump, 0.0), lanes - 2)
        return out + roll(jnp.where(at <= lanes - 2, p1 * jump, 0.0), 1)

    def lat_inner(s):
        def body(level, carry):
            out = lat_pass(y_ref[level], latc[s, level], latb[s, level])
            ext[s, level, OWN : OWN + rows] = out
            return carry

        lax.fori_loop(0, levels, body, 0, unroll=True)

    def edge_terms(s, at):
        count_rows = at.stop - at.start
        lane = lax.broadcasted_iota(jnp.int32, (count_rows, lanes), 1)
        even = lax.rem(lane, 2) == 0
        tail, head = pack[s, 0, 0, at], pack[s, 1, 0, at]
        before, after = land_p[s, 0, 0, at], land_p[s, 1, 0, at]
        m2_after, m1_after, _, _ = face_weights(land_p[s, 1, 1, at], land_p[s, 1, 2, at])
        _, _, m0_head, p1_head = face_weights(pack[s, 1, 1, at], pack[s, 1, 2, at])
        _, _, _, p1_before = face_weights(land_p[s, 0, 1, at], land_p[s, 0, 2, at])
        jump = after - jnp.where(even, roll(tail, lanes - 1), roll(after, 1))
        top_here = jnp.where(has_north, m2_after * jump, 0.0)
        top_next = jnp.where(jnp.logical_and(even, has_north), m1_after * jump, 0.0)
        jump = jnp.where(even, head - roll(before, lanes - 1), before - roll(before, 1))
        flux = jnp.where(has_south, jnp.where(even, p1_head, p1_before) * jump, 0.0)
        low_here = jnp.where(has_south, m0_head * jump, 0.0)
        edge = jnp.logical_or(lane < 2, lane >= lanes - 2)

        def turned_back(by):
            def turn(value, shift):
                shift = (shift - by) % lanes
                return roll(value, shift) if shift else value

            first = lax.rem(lane + by, 4) < 2
            evens = lax.rem(lane + by, 2) == 0
            top = turn(top_here, 0) + turn(top_next, 1)
            low = jnp.where(evens, turn(low_here, 2) + turn(flux, 1), turn(flux, 3))
            return jnp.where(first, top, low), jnp.where(first, low, top)

        return turned_back, edge

    def own_edges(s):
        turned_back, edge = edge_terms(s, slice(OWN, OWN + rows))
        both = turned_back(0)
        for level in range(levels):
            turned = roll(both[level % 2], lanes - 2 - 2 * level)
            ext[s, level, OWN : OWN + rows] += jnp.where(edge, turned, 0.0)

    def far_edges(s):
        end = OWN + rows
        for side, where in enumerate((slice(OWN - 2, OWN), slice(end, end + 2))):
            for member in range(2):
                pack[s, member, 0, where] = far_a[side, s, 2 * member : 2 * member + 2]
                far = 4 + 2 * member
                pack[s, 1, 1 + member, where] = far_a[side, s, far : far + 2]
        down = lax.broadcasted_iota(jnp.int32, (8, lanes), 0)
        for side, (at, row) in enumerate(((slice(0, OWN), OWN - 2), (slice(end, end + OWN), 0))):
            turned_back, edge = edge_terms(s, at)
            both = turned_back(0), turned_back(1)
            rows2 = [
                jnp.where(
                    lax.rem(down // 2 + levels - 1, 2) == 0,
                    jnp.broadcast_to(both[odd][0][row + odd : row + odd + 1], (8, lanes)),
                    jnp.broadcast_to(both[odd][1][row + odd : row + odd + 1], (8, lanes)),
                )
                for odd in range(2)
            ]
            tile = jnp.where(lax.rem(down, 2) == 0, rows2[0], rows2[1])
            for v in range((2 * levels + 7) // 8):
                turn = (8 * v - 2 * levels) % lanes
                late = turn > lanes - 8
                source = roll(tile, lanes // 2) if late else tile
                turn = turn - lanes // 2 if late else turn
                turned = pltpu.roll(source, turn, 1, stride=1, stride_axis=0)
                delta[side, 8 * v : 8 * v + 8] = jnp.where(edge, turned, 0.0)

    def edges_and_lon(s, target, part):
        end = OWN + rows
        for level in range(*part):
            far, two = slice(8 + 2 * level, 10 + 2 * level), slice(2 * (levels - 1 - level), 2 * (levels - level))
            ext[s, level, OWN - 2 : OWN] = far_a[0, s, far] + delta[0, two]
            ext[s, level, end : end + 2] = far_a[1, s, far] + delta[1, two]
        for level in range(*part):
            target[level] = lon_level(s, level)

    def lon_own_weights(s):
        def body(level, carry):
            found = face_weights(
                lonc[s, level], lonb[s, level]
            )
            for member in range(4):
                lw[s, member, level, OWN : OWN + rows] = found[member]
            return carry

        lax.fori_loop(0, levels, body, 0, unroll=True)

    def lon_level(s, level):
        a = [ext[s, level, OWN + k : OWN + k + rows] for k in range(-2, 3)]
        w = [
            lw[s, member, level, OWN + 2 - member : OWN + 2 - member + rows]
            for member in range(4)
        ]
        out = a[2] + w[0] * (a[4] - a[3]) + w[1] * (a[3] - a[2])
        return out + w[2] * (a[2] - a[1]) + w[3] * (a[1] - a[0])

    def send_lon(s, part, slot):
        end = OWN + rows
        for member, src, dst, size, device in (
            (0, OWN, end, 2, west),
            (1, OWN, end, 1, west),
            (3, end - 1, OWN - 1, 1, east),
        ):
            at = pl.ds(part[0], part[1] - part[0])
            remote(
                lw.at[s, member, at, pl.ds(src, size), :],
                lw.at[s, member, at, pl.ds(dst, size), :],
                0,
                slot,
                device,
            )

    def find_slots():
        order = order_ref[...]
        table = jnp.concatenate([order // blk, lax.rem(order, blk)], axis=0)
        table = table.astype(jnp.float32).astype(jnp.bfloat16)
        high = order.shape[0]
        down = lax.broadcasted_iota(jnp.int32, (lanes, lanes), 0)
        row_of = lax.broadcasted_iota(jnp.int32, (high, lanes), 0)
        for i in range(rows):
            region = rmap_ref[i : i + 1, :]
            hit = jnp.where(down == lax.rem(region, 128), 1.0, 0.0).astype(jnp.bfloat16)
            found = jnp.dot(table, hit, preferred_element_type=jnp.float32)
            both = found[:high] * float(blk) + found[high:]
            both = jnp.where(row_of == region // 128, both, 0.0)
            ids[2, OWN + i : OWN + i + 1] = jnp.sum(both, axis=0, keepdims=True)

    def spread(i, slot):
        groups = hot.shape[0] // 2
        slot = slot.astype(jnp.int32)
        high = lax.broadcasted_iota(jnp.int32, (2 * groups, lanes), 0) // 2
        low = lax.broadcasted_iota(jnp.int32, (blk, lanes), 0)
        at = slice(i * lanes, (i + 1) * lanes)
        hot[:, at] = jnp.where(high == slot // blk, 1.0, 0.0).astype(jnp.bfloat16)
        cht[:, at] = jnp.where(low == lax.rem(slot, blk), 1.0, 0.0).astype(jnp.bfloat16)

    def regions(pushed, side, later):
        tile, many = 16, hot.shape[0]
        step0 = lax.rem(lax.broadcasted_iota(jnp.int32, (tile, lanes), 0), 2) == 0
        for i in range(rows + 5):
            here = slice(i * lanes, (i + 1) * lanes)
            first = pushed[i : i + 1] if i < rows + 4 else side
            second = later[i - 2 : i - 1] if 2 <= i < rows + 2 else jnp.zeros_like(first)
            value = jnp.where(
                step0, jnp.broadcast_to(first, (tile, lanes)), jnp.broadcast_to(second, (tile, lanes))
            )
            coarse = value.astype(jnp.bfloat16)
            fine = (value - coarse.astype(jnp.float32)).astype(jnp.bfloat16)
            for part, piece in enumerate((coarse, fine)):
                for at in range(0, many, tile):
                    amat[part * many + at : part * many + at + tile, here] = (
                        hot[at : at + tile, here] * piece
                    )
        sums = lax.dot_general(
            amat[...], cht[...], (((1,), (1,)), ((), ())), preferred_element_type=jnp.float32
        )
        sums = sums[:many] + sums[many:]
        send_ref[...] = sums

    tall_rows = rows + 2 * OWN
    few = slice(OWN - 2, OWN + rows + 6)
    has_north, has_south = my_lat < nlat - 1, my_lat > 0

    def push_lat():
        courant = jnp.where(jnp.logical_and(lane == 0, my_lat == 0), 0.0, latc[0, 0])
        m2, m1, m0, p1 = face_weights(courant, latb[0, 0])
        north_c = jnp.where(has_north, beside[1, 3, OWN : OWN + rows], 0.0)
        n2, n1, n0, np1 = face_weights(north_c, beside[1, 4, OWN : OWN + rows])
        ahead1 = jnp.where(lane == lanes - 1, roll(n1, lanes - 1), roll(m1, lanes - 1))
        round2 = roll(m2, lanes - 2)
        ahead2 = jnp.where(lane >= lanes - 2, roll(n2, lanes - 2), round2)
        behind = roll(p1, 1)
        lat_c[0, 0] = 1.0 - ahead1 + m0
        lat_c[0, 1] = jnp.where(lane <= lanes - 2, ahead1 - ahead2, 0.0)
        lat_c[0, 2] = jnp.where(lane <= lanes - 3, ahead2, 0.0)
        lat_c[0, 3] = jnp.where(lane >= 1, behind - m0, 0.0)
        lat_c[0, 4] = jnp.where(lane >= 2, -behind, 0.0)
        last, first = jnp.logical_and(lane == lanes - 1, has_south), jnp.logical_and(lane == 0, has_north)
        lat_c[1, 1] = jnp.where(last, roll(m1, lanes - 1) - round2, 0.0)
        lat_c[1, 2] = jnp.where(jnp.logical_and(lane >= lanes - 2, has_south), round2, 0.0)
        lat_c[1, 3] = jnp.where(first, behind - n0, 0.0)
        second = jnp.logical_and(lane == 1, has_north)
        lat_c[1, 4] = jnp.where(first, -behind, jnp.where(second, -roll(np1, 1), 0.0))

    def push_lon(side):
        down = lax.broadcasted_iota(jnp.int32, (tall_rows, lanes), 0)
        across = lax.broadcasted_iota(jnp.int32, (tall_rows, lanes), 1)
        faces = jnp.logical_and(down >= OWN, down <= OWN + rows)
        here, south_of = cos_ref[my_lat], cos_ref[lax.rem(my_lat + nlat - 1, nlat)]
        north_of = cos_ref[lax.rem(my_lat + 1, nlat)]
        across1 = lax.broadcasted_iota(jnp.int32, (1, lanes), 1)
        at_north = jnp.logical_and(across < 2, has_north)
        at_south = jnp.logical_and(across >= lanes - 2, has_south)
        if side == 0:
            courant, branch, cosine = ids[0], ids[1], here
        else:
            courant, branch = (
                jnp.where(at_north, beside[1, m], jnp.where(at_south, beside[0, m], 0.0))
                for m in range(2)
            )
            cosine = jnp.where(across1 < 2, north_of, south_of)
        m2, m1, m0, p1 = face_weights(jnp.where(faces, courant, 0.0), branch)
        ahead1 = pltpu.roll(m1, tall_rows - 1, 0)
        ahead2 = pltpu.roll(m2, tall_rows - 2, 0)
        behind = pltpu.roll(p1, 1, 0)
        found = (1.0 - ahead1 + m0, ahead1 - ahead2, ahead2, behind - m0, -behind)
        for k, value in enumerate(found):
            lon_c[side, k] = value[few] * cosine

    def squeeze(value):
        return jnp.sum(pltpu.roll(value, 0, 1, stride=4, stride_axis=0), axis=0, keepdims=True)

    def side_slots():
        shape = (rows + 8, lanes)
        down = lax.broadcasted_iota(jnp.int32, shape, 0)
        across = lax.broadcasted_iota(jnp.int32, shape, 1)
        at_north = jnp.logical_and(across < 2, has_north)
        at_south = jnp.logical_and(across >= lanes - 2, has_south)
        side = jnp.where(at_north, beside[1, 2, few], jnp.where(at_south, beside[0, 2, few], 0.0))
        side = squeeze(jnp.where(down < rows + 4, side, 0.0))
        spread(rows + 4, side)

    def push_totals():
        a = y_ref[0]
        turned = (a, roll(a, lanes - 1), roll(a, lanes - 2), roll(a, 1), roll(a, 2))
        for side in range(2):
            value = lat_c[side, 1] * turned[1]
            for k in range(2, 5):
                value = value + lat_c[side, k] * turned[k]
            if side == 0:
                value = value + lat_c[0, 0] * a
            bext[side, OWN : OWN + rows] = value
        found = []
        for side in range(2):
            value = jnp.zeros((rows + 8, lanes), jnp.float32)
            for k, step in enumerate((0, 1, 2, -1, -2)):
                at = OWN - 2 + step
                value = value + lon_c[side, k] * bext[side, at : at + rows + 8]
            found.append(value)
        regions(found[0], squeeze(found[1]), x_ref[0] * cos_ref[my_lat])

    got(0, (levels - 1) * rows)
    coefficients(1)
    got(1, levels * rows)
    solve(1)
    got(2, 4 * levels * rows)
    pack_weights(1)
    row_weights(1)
    lat_rows(1)
    lon_own_weights(1)
    got(3, 4 * levels * rows + rows + order_ref.shape[0] + nlat)
    ids[0, OWN : OWN + rows] = lonc[0, 0]
    ids[1, OWN : OWN + rows] = lonb[0, 0].astype(jnp.float32)
    ids[3, OWN : OWN + rows] = latc[0, 0]
    ids[4, OWN : OWN + rows] = latb[0, 0].astype(jnp.float32)
    find_slots()
    bext[...] = jnp.zeros_like(bext)
    pl.semaphore_wait(barrier, count - 1)

    turn = {1: lax.rem(my_lon + 1, nlon), -1: lax.rem(my_lon + nlon - 1, nlon)}
    own_rows, first, last_two = pl.ds(OWN, rows), pl.ds(OWN, 2), pl.ds(OWN + rows - 2, 2)
    low, high = pl.ds(OWN - 2, 2), pl.ds(OWN + rows, 2)

    toward = (north[1], south[1])
    send_if, recv_if = (has_north, has_south), (has_south, has_north)
    column_rows = rows + 4

    def send_end(source, target, recv_base, diagonal, end, lat):
        for lon, src, dst in (
            ((turn[1], last_two, low), (turn[-1], first, high))
            if diagonal
            else ((my_lon, own_rows, own_rows),)
        ):
            remote(
                source(end, src),
                target(end, dst),
                1,
                recv_base + (1 if diagonal else 0),
                (lon, lat),
            )

    def send_columns(source, target, recv_base, diagonal):
        if nlat == 2:
            send_end(source, target, recv_base, diagonal, my_lat, 1 - my_lat)
            return
        for end in range(2):

            @pl.when(send_if[end])
            def _():
                send_end(source, target, recv_base, diagonal, end, toward[end])

    beside_count = jnp.where(has_north, 1, 0) + jnp.where(has_south, 1, 0)

    def drain_beside(sem, count_rows):
        if nlat == 2:
            drain(sem, count_rows)
            return
        for ends in (1, 2):

            @pl.when(beside_count == ends)
            def _():
                drain(sem, ends * count_rows)

    half = 2 * levels // 3
    parts = ((0, half), (half, levels))
    spans = (pl.ds(0, 8 + 2 * half), pl.ds(8 + 2 * half, 2 * (levels - half)))
    border = (2 * (8 + 2 * half), 4 * (levels - half))

    def send_border(s, part, slot):
        at = spans[part]
        remote(rows_a.at[0, s, at, :], far_a.at[0, s, at, :], 0, slot, east)
        remote(rows_a.at[1, s, at, :], far_a.at[1, s, at, :], 0, slot, west)

    border_rows = sum(border)
    lon_rows = 4 * levels

    def group_of(device):
        return (device * width) // blk

    def scatter(k, carry):
        device = lax.rem(me + k, count)
        pltpu.make_async_remote_copy(
            src_ref=send_ref.at[pl.ds(2 * group_of(device), 2), :],
            dst_ref=land.at[me],
            send_sem=all_sem.at[0],
            recv_sem=all_sem.at[1],
            device_id=place(device),
            device_id_type=MESH,
        ).start()
        return carry

    three = pl.ds(0, 3)

    def send_packs(diagonal):
        send_columns(
            lambda end, at: pack.at[1, end, :, at, :],
            lambda end, at: land_p.at[1, end, :, at, :],
            5,
            diagonal,
        )
        if diagonal:
            send_columns(
                lambda end, at: ids.at[three, at, :],
                lambda end, at: beside.at[end, three, at, :],
                5,
                True,
            )
        else:
            send_columns(
                lambda end, at: ids.at[:, at, :], lambda end, at: beside.at[end, :, at, :], 5, False
            )

    send_packs(True)
    remote(ids.at[three, last_two, :], ids.at[three, low, :], 0, 4, east)
    remote(ids.at[three, first, :], ids.at[three, high, :], 0, 4, west)
    send_packs(False)
    for part, slot in ((0, 1), (1, 3)):
        send_border(1, part, slot)
        send_lon(1, parts[part], slot)
    lat_inner(1)
    got(4, (levels - 1) * rows + blk * blk // lanes)
    coefficients(0)
    lon_own_weights(0)
    send_lon(0, (0, levels), 0)
    pack_weights(0)
    row_weights(0)
    for diagonal in (True, False):
        send_columns(
            lambda end, at: pack.at[0, end, 1:3, at, :],
            lambda end, at: land_p.at[0, end, 1:3, at, :],
            8,
            diagonal,
        )
    for i in range(rows):
        spread(2 + i, ids[2, OWN + i : OWN + i + 1])
    drain_beside(recv_sem.at[5], 8 * rows)
    own_edges(1)
    push_lat()
    drain(recv_sem.at[4], 12)
    push_lon(0)
    for i in (0, 1, rows + 2, rows + 3):
        spread(i, ids[2, OWN - 2 + i : OWN - 1 + i])
    drain_beside(recv_sem.at[6], 24)
    for part, slot in ((0, 1), (1, 3)):
        drain(recv_sem.at[slot], border[part] + 4 * (parts[part][1] - parts[part][0]))
        if part == 0:
            far_edges(1)
        else:
            push_lon(1)
            side_slots()
        edges_and_lon(1, x_ref, parts[part])
    solve(0)
    lat_rows(0)
    for diagonal in (True, False):
        send_columns(
            lambda end, at: pack.at[0, end, 0, at, :],
            lambda end, at: land_p.at[0, end, 0, at, :],
            8,
            diagonal,
        )
    send_border(0, 0, 2)
    send_border(0, 1, 7)
    push_totals()
    lax.fori_loop(1, count, scatter, 0)
    fetch(send_ref.at[pl.ds(2 * group_of(me), 2), :], land.at[me], 5)
    lat_inner(0)
    drain(recv_sem.at[0], lon_rows)
    drain_beside(recv_sem.at[8], 3 * rows)
    own_edges(0)
    drain_beside(recv_sem.at[9], 12)
    for part, slot in ((0, 2), (1, 7)):
        drain(recv_sem.at[slot], border[part])
        if part == 0:
            far_edges(0)
        edges_and_lon(0, out_ref, parts[part])
    fetch(out_ref, out_h, 5)
    got(5, levels * rows + 2 * blk // lanes)
    drain(send_sem.at[0], 2 * (border_rows + lon_rows) + 12)
    drain_beside(send_sem.at[1], 9 * column_rows + 2 * rows)
    every = land.at[pl.ds(0, count - 1)]
    pltpu.make_async_copy(every, every, all_sem.at[0]).wait()
    pltpu.make_async_copy(every, every, all_sem.at[1]).wait()


def finish(adjoint_v, land, cov, adjoint_h, flux_h, flux, sem):
    whole = pltpu.make_async_copy(adjoint_v, adjoint_h, sem.at[0])
    whole.start()
    totals = jnp.sum(land[...], axis=0)
    coarse = totals.astype(jnp.bfloat16).astype(jnp.float32)
    rest = jnp.zeros((12, totals.shape[1]), jnp.float32)
    both = jnp.concatenate([coarse, totals - coarse, rest], axis=0).astype(jnp.bfloat16)
    cov_high = cov[...].astype(jnp.bfloat16)
    cov_low = (cov[...] - cov_high.astype(jnp.float32)).astype(jnp.bfloat16)
    found = jnp.dot(both, cov_high, preferred_element_type=jnp.float32)
    found = found + jnp.dot(both, cov_low, preferred_element_type=jnp.float32)
    flux[...] = found[:2] + found[2:4]
    part = pltpu.make_async_copy(flux, flux_h, sem.at[1])
    part.start()
    part.wait()
    whole.wait()


def per_device(
    nlon,
    nlat,
    adjoint_final,
    lon_courant,
    lon_branch,
    lat_courant,
    lat_branch,
    mixing,
    region_map,
    region_order,
    prior_cov,
):
    steps, levels, rows, lanes = lon_courant.shape
    regions = region_order.shape[0]
    blk = prior_cov.shape[1]
    width = regions // (nlon * nlat)
    lat_total = lanes * nlat
    lat_index = np.arange(lat_total, dtype=np.float32)
    angle = (lat_index + np.float32(0.5)) * np.float32(math.pi / lat_total)
    cosines = np.cos((angle - np.float32(0.5 * math.pi)).astype(np.float32))
    cosines = jnp.asarray(cosines.astype(np.float32).reshape(nlat, 1, lanes))
    f32, i32, b16 = jnp.float32, jnp.int32, jnp.bfloat16
    field = (levels, rows, lanes)
    tall = (levels, rows + 2 * OWN, lanes)
    vm = pltpu.VMEM
    scratch = [
        vm(field, f32),
        vm((rows, lanes), i32),
        vm((regions // 128, 128), i32),
        vm((nlat, 1, lanes), f32),
        vm(field, f32),
        vm((steps, levels - 1, rows, lanes), f32),
        vm((steps,) + field, f32),
        vm((steps,) + field, i32),
        vm((steps,) + field, f32),
        vm((steps,) + field, i32),
        vm((steps,) + field, f32),
        vm((steps,) + field, f32),
        vm((steps,) + field, f32),
        vm((steps, rows, lanes), f32),
        vm(field, f32),
        vm((steps,) + tall, f32),
        vm((steps, 4) + tall, f32),
        vm((steps, 2, 3, rows + 2 * OWN, lanes), f32),
        vm((steps, 2, 3, rows + 2 * OWN, lanes), f32),
        vm((2, 2 * levels, lanes), f32),
        vm((2, steps, 2 * levels + 8, lanes), f32),
        vm((2, steps, 2 * levels + 8, lanes), f32),
        vm((2, steps, 2, 2 * levels, lanes), f32),
        vm((2, 5, 2 * levels, lanes), f32),
        vm((2, 2 * levels + 8, lanes), f32),
        vm((5, rows + 2 * OWN, lanes), f32),
        vm((2, 5, rows + 2 * OWN, lanes), f32),
        vm((2, 5, rows, lanes), f32),
        vm((2, 5, rows + 8, lanes), f32),
        vm((2, rows + 2 * OWN, lanes), f32),
        vm((2 * (regions // blk), (rows + 5) * lanes), b16),
        vm((blk, (rows + 5) * lanes), b16),
        vm((4 * (regions // blk), (rows + 5) * lanes), b16),
        vm((2 * (regions // blk), blk), f32),
        vm((5 * levels * rows, lanes), f32),
        pltpu.SemaphoreType.DMA((6,)),
        pltpu.SemaphoreType.DMA((2,)),
        pltpu.SemaphoreType.DMA((10,)),
        pltpu.SemaphoreType.DMA((2,)),
    ]
    adjoint, landed, cov = pl.pallas_call(
        functools.partial(kernel, nlon, nlat, width),
        out_shape=(
            pltpu.VMEM(field, f32),
            pltpu.VMEM((nlon * nlat, steps, blk), f32),
            pltpu.VMEM((blk, blk), f32),
        ),
        in_specs=[pl.BlockSpec(memory_space=pltpu.HBM)] * 10,
        out_specs=(pl.BlockSpec(memory_space=pl.ANY),) * 3,
        scratch_shapes=scratch,
        compiler_params=pltpu.CompilerParams(
            collective_id=0, has_side_effects=True, vmem_limit_bytes=61 * 1024 * 1024
        ),
    )(
        adjoint_final,
        lon_courant,
        lon_branch,
        lat_courant,
        lat_branch,
        mixing,
        prior_cov,
        region_map,
        region_order.reshape(regions // 128, 128),
        cosines,
    )
    adjoint, flux = pl.pallas_call(
        finish,
        out_shape=(
            jax.ShapeDtypeStruct(field, f32),
            jax.ShapeDtypeStruct((steps, blk), f32),
        ),
        in_specs=[
            pl.BlockSpec(memory_space=pl.ANY),
            pl.BlockSpec(memory_space=pltpu.VMEM),
            pl.BlockSpec(memory_space=pltpu.VMEM),
        ],
        out_specs=(pl.BlockSpec(memory_space=pl.ANY),) * 2,
        scratch_shapes=[vm((steps, blk), f32), pltpu.SemaphoreType.DMA((2,))],
    )(*(pltpu.with_memory_space_constraint(x, pltpu.VMEM) for x in (adjoint, landed, cov)))
    if width < blk:
        start = lax.rem(lax.axis_index("lat") * width, blk)
        flux = lax.dynamic_slice_in_dim(flux, start, width, 1)
    return adjoint, flux


def solution(mesh):
    four = P(None, None, "lon", "lat")
    placed = (
        P(None, "lon", "lat"),
        four,
        four,
        four,
        four,
        four,
        P("lon", "lat"),
        P(),
        P("lon", None, None),
    )
    return jax.shard_map(
        functools.partial(per_device, mesh.shape["lon"], mesh.shape["lat"]),
        mesh=mesh,
        in_specs=placed,
        out_specs=(P(None, "lon", "lat"), P(None, ("lon", "lat"))),
        check_vma=False,
    )
```
